256 devices in a mesh: brick: 64 (over z, x, core), spec: 4 (over y).
Axes of the slice: x: 4, y: 4, z: 8, core: 2. Of those that a mesh axis runs over, the one named last changes fastest.
Arguments:
- rhs: float32 [4, 128, 256, 256], P('spec', 'brick'), may hold values from -24 to 24
- density: float32 [128, 256, 256], P('brick', 'spec'), may hold values from 0.01 to 0.1
- kappa: float32 [4], P('spec'), may hold values from 0.5 to 4
- block_group: int32 [64, 16], replicated, may hold values from 0 to 255, as said below
Outputs:
- solution: float32 [4, 128, 256, 256], P('spec', 'brick')
- residual: float32 [4, 128, 256, 256], P('spec', 'brick')
The draws below stay inside these ranges and needn't reach their ends.
Inputs may be any that keep to these rules, and one draw needn't show every extreme that they name: `block_group`: every aggregate id 0 to 255 names at least one block; the blocks of one aggregate share one tile position and lie on consecutive bricks.
All inputs are finite; a program needn't handle non-finite values.
Results may differ from the reference program's by a relative error of at most 0.0003.
Values sent between devices are 32-bit elements; how exact they have to be, the bound alone decides.
No kernel may reach another device: no remote copies, remote signals or barrier semaphores. Data moves between devices by JAX's collectives and lax.ppermute only.
A program may use at most 64 MiB of HBM per device.

```python
import math
import jax
import jax.numpy as jnp
from jax import lax

CX = 2
NY = 256
NZ = 256
TILES = 4
CYCLES = 1
COARSE_SWEEPS = 3
SPECIES = 4
NX = 128
NBLK = 16
NAGG = 256
SEGS = 16


def draw_block_group(key, part):
    first_key, second_key = jax.random.split(key)
    bricks = NX // CX
    tile_keys = jax.random.split(first_key, NBLK)
    orders = jax.vmap(lambda single: jax.random.permutation(single, bricks - 1))(tile_keys)
    cuts = (orders < SEGS - 1).astype(jnp.int32)
    segment = jnp.concatenate([jnp.zeros((NBLK, 1), jnp.int32), jnp.cumsum(cuts, axis=1).astype(jnp.int32)], axis=1)
    labels = jnp.arange(NBLK, dtype=jnp.int32)[:, None] * SEGS + segment
    relabel = jax.random.permutation(second_key, NAGG).astype(jnp.int32)
    return jnp.take(relabel, labels.T, axis=0).astype(jnp.int32)


def steps_of(key, shape, shards, least, high):
    factor_of = 1.0
    for position, parts in shards:
        heights = jax.random.uniform(jax.random.fold_in(jax.random.fold_in(key, 6), position), (parts,), jnp.float32, least / len(shards), high / len(shards))
        factor_of = factor_of * jnp.repeat(jnp.exp(heights), shape[position] // parts).reshape((-1,) + (1,) * (len(shape) - 1 - position))
    return factor_of


def gaussian(rng, shape, spread, bound, shards=(), kind=jnp.bfloat16):
    entries = spread * jax.random.normal(rng, shape, jnp.float32)
    if shards:
        entries = entries * steps_of(rng, shape, shards, -0.22, 0.18)
    return jnp.clip(entries, -bound, bound).astype(kind)


def setup_inputs(seed: int = 0) -> dict:
    key_of = jax.random.split(jax.random.key(seed), 5)
    return {
        "rhs": gaussian(key_of[0], (SPECIES, NX, NY, NZ), 4.0, 24.0, ((0, 4), (1, 64)), jnp.float32),
        "density": jnp.clip(jnp.exp(math.log(0.1) - 2.3025851 * jax.random.uniform(key_of[1], (NX, NY, NZ), jnp.float32) ** steps_of(key_of[1], (NX, NY, NZ), ((0, 64), (1, 4)), -0.2, 0.2)), 0.01, 0.1),
        "kappa": jnp.clip(jnp.exp(math.log(4.0) - 2.0794415 * jax.random.uniform(key_of[2], (SPECIES,), jnp.float32) ** steps_of(key_of[2], (SPECIES,), ((0, 4),), -0.2, 0.2)), 0.5, 4.0),
        "block_group": draw_block_group(jax.random.fold_in(key_of[4], 71), 0),
    }


relax_fine = 0.85
relax_coarse = 0.6


def filter_along(field, axis):
    length = field.shape[axis]
    widths = [(0, 0)] * field.ndim
    widths[axis] = (1, 1)
    padded = jnp.pad(field, widths)
    lower = lax.slice_in_dim(padded, 0, length, axis=axis)
    upper = lax.slice_in_dim(padded, 2, length + 2, axis=axis)
    return field + 0.5 * (lower + upper)


def stencil_sum(field):
    return filter_along(filter_along(filter_along(field, 1), 2), 3)


def operate(field, center, scale):
    return center * field - 2.0 * scale * stencil_sum(field)


def relax(field, source, center, diagonal, scale):
    return field + relax_fine * (source - operate(field, center, scale)) / diagonal


def coarsen(field):
    leading = field.shape[:-3]
    first, second, third = field.shape[-3:]
    count = len(leading)
    blocks = field.reshape(leading + (first // 2, 2, second // 2, 2, third // 2, 2))
    return jnp.sum(blocks, axis=(count + 1, count + 3, count + 5)) * 0.125


def refine(field):
    leading = field.shape[:-3]
    first, second, third = field.shape[-3:]
    shaped = field.reshape(leading + (first, 1, second, 1, third, 1))
    grown = jnp.broadcast_to(shaped, leading + (first, 2, second, 2, third, 2))
    return grown.reshape(leading + (2 * first, 2 * second, 2 * third))


def cell_groups(rows, thickness, height, width):
    count = rows.shape[0]
    shaped = rows.reshape(count, 1, TILES, 1, TILES, 1)
    grown = jnp.broadcast_to(shaped, (count, thickness, TILES, height // TILES, TILES, width // TILES))
    return grown.reshape(count * thickness, height, width)


def same_weight(padded, extent):
    first, second, third = extent
    center = padded[1:1 + first, 1:1 + second, 1:1 + third]
    total = jnp.zeros(extent, jnp.float32)
    for first_step in (-1, 0, 1):
        for second_step in (-1, 0, 1):
            for third_step in (-1, 0, 1):
                weight = 0.5 ** (abs(first_step) + abs(second_step) + abs(third_step))
                shifted = lax.slice(padded, (1 + first_step, 1 + second_step, 1 + third_step),
                                    (1 + first_step + first, 1 + second_step + second, 1 + third_step + third))
                total = total + weight * (shifted == center).astype(jnp.float32)
    return total


def group_sums(field, groups):
    flat = groups.reshape(-1)
    return jax.vmap(lambda layer: jax.ops.segment_sum(layer.reshape(-1), flat, num_segments=NAGG))(field)


def reference(rhs, density, kappa, block_group):
    scale = kappa[:, None, None, None]
    center = density[None] + 16.0 * scale
    diagonal = density[None] + 14.0 * scale
    density_coarse = coarsen(density)
    scale_coarse = 0.25 * scale
    center_coarse = density_coarse[None] + 16.0 * scale_coarse
    diagonal_coarse = density_coarse[None] + 14.0 * scale_coarse
    groups = cell_groups(block_group, CX // 2, NY // 2, NZ // 2)
    padded = jnp.pad(groups, 1, constant_values=-1)
    same = same_weight(padded, groups.shape)
    totals = group_sums(jnp.stack([density_coarse, 16.0 - 2.0 * same]), groups)
    coarse_diag = totals[0][None] + (0.25 * kappa)[:, None] * totals[1][None]
    solution = jnp.zeros_like(rhs)
    for cycle in range(CYCLES):
        solution = relax(solution, rhs, center, diagonal, scale)
        solution = relax(solution, rhs, center, diagonal, scale)
        fine_res = rhs - operate(solution, center, scale)
        coarse_res = coarsen(fine_res)
        correction = relax(jnp.zeros_like(coarse_res), coarse_res, center_coarse, diagonal_coarse, scale_coarse)
        correction = relax(correction, coarse_res, center_coarse, diagonal_coarse, scale_coarse)
        remainder = coarse_res - operate(correction, center_coarse, scale_coarse)
        group_rhs = group_sums(remainder, groups)
        group_fix = relax_coarse * group_rhs / coarse_diag
        for sweep in range(COARSE_SWEEPS - 1):
            image = operate(jnp.take(group_fix, groups, axis=1), center_coarse, scale_coarse)
            group_fix = group_fix + relax_coarse * (group_rhs - group_sums(image, groups)) / coarse_diag
        correction = correction + jnp.take(group_fix, groups, axis=1)
        correction = relax(correction, coarse_res, center_coarse, diagonal_coarse, scale_coarse)
        correction = relax(correction, coarse_res, center_coarse, diagonal_coarse, scale_coarse)
        solution = solution + refine(correction)
        solution = relax(solution, rhs, center, diagonal, scale)
        solution = relax(solution, rhs, center, diagonal, scale)
    residual = rhs - operate(solution, center, scale)
    return solution, residual
```

```python
import functools

import jax
import jax.numpy as jnp
from jax import lax
from jax.experimental import pallas as pl
from jax.experimental.pallas import tpu as pltpu
from jax.sharding import PartitionSpec as P

WEIGHT = 0.85
COARSE_WEIGHT = 0.6
COARSE_SWEEPS = 3
TILES = 4
CHUNK = 64
f32 = jnp.float32
bf16 = jnp.bfloat16
VM = pl.BlockSpec(memory_space=pltpu.VMEM)
SM = pl.BlockSpec(memory_space=pltpu.SMEM)
PARAMS = pltpu.CompilerParams(vmem_limit_bytes=48 * 1024 * 1024)


def iota(shape, dim):
    return lax.broadcasted_iota(jnp.int32, shape, dim)


def split(x):
    high = x.astype(bf16)
    rest = x - high.astype(f32)
    middle = rest.astype(bf16)
    low = (rest - middle.astype(f32)).astype(bf16)
    return high, middle, low


def dot_exact(x, w):
    high, middle, low = split(x)
    dot = functools.partial(jnp.dot, preferred_element_type=f32)
    return dot(high, w) + (dot(middle, w) + dot(low, w))


def filter_z(y):
    width = y.shape[1]
    lane = iota(y.shape, 1)
    before = jnp.where(lane == 0, 0.0, pltpu.roll(y, 1, 1))
    after = jnp.where(lane == width - 1, 0.0, pltpu.roll(y, width - 1, 1))
    return y + 0.5 * (before + after)


def filter_yz(m):
    rows = m.shape[0]
    y = m + 0.5 * (pltpu.roll(m, 1, 0) + pltpu.roll(m, rows - 1, 0))
    return filter_z(y[8 : rows - 8])


def stencil(ref, i, row, rows):
    part = pl.ds(row, rows + 16)
    return filter_yz(ref[i, part, :] + 0.5 * (ref[i - 1, part, :] + ref[i + 1, part, :]))


def clear_edges(ref):
    layers, rows, width = ref.shape
    zero = jnp.zeros((layers, 8, width), f32)
    ref[:, 0:8, :] = zero
    ref[:, rows - 8 : rows, :] = zero


def chunks(rows, body):
    def step(c, carry):
        body(pl.multiple_of(c * CHUNK, CHUNK))
        return carry

    lax.fori_loop(0, rows // CHUNK, step, 0)


def coarsen_z(rows, width):
    return ((iota((width, width // 2), 0) >> 1) == iota((width, width // 2), 1)).astype(bf16)


def put_halves(ref, i, part, x):
    half = x.shape[1] // 2
    ref[i, 0, part, :] = x[:, :half]
    ref[i, 1, part, :] = x[:, half:]


def pair_rows(ref, i, half):
    even, odd = pl.ds(0, half, stride=2), pl.ds(1, half, stride=2)
    return jnp.concatenate([ref[i, k, even, :] + ref[i, k, odd, :] for k in range(2)], 1)


def gather_kernel(meta, rhs, shard, p1, p2, p3, own):
    count = 4
    rows = shard.shape[1]
    own[0:2] = rhs[0]
    for k, piece in enumerate((shard, p1, p2, p3)):
        owner = lax.rem(meta[2] - k + count, count)
        own[2:4, pl.ds(pl.multiple_of(owner * rows, rows), rows), :] = piece[...]


def first_kernel(
    meta, kappa, own, from_a, from_b,
    s2_out, wd_out, rhs_halo, send_a, send_b, payload,
    s1, s2, wd, rhs_w, work,
):
    core, brick, bricks = meta[0], meta[1], meta[3]
    scale = kappa[0]
    scale1 = 0.25 * scale
    height, width = own.shape[1:]
    half = height // 2
    clear_edges(s1)
    clear_edges(s2)

    base_b = 4 * core
    base_a = 4 * (1 - core)
    valid_lo = (brick > 0).astype(f32)
    valid_hi = (brick < bricks - 1).astype(f32)
    valid_b = jnp.where(core == 0, valid_lo, valid_hi)
    valid_a = jnp.where(core == 0, valid_hi, valid_lo)
    for ref, base, valid in ((from_b, base_b, valid_b), (from_a, base_a, valid_a), (own, 2, None)):
        top = WEIGHT if valid is None else WEIGHT * valid

        def begin(row, ref=ref, base=base, top=top):
            part = pl.ds(row, CHUNK)
            pair = jnp.zeros((CHUNK, width), f32)
            for layer in range(2):
                density = ref[2 + layer, part, :]
                source = ref[layer, part, :]
                factor = top / (density + 14.0 * scale)
                wd[base + layer, part, :] = factor
                rhs_w[base + layer, part, :] = source
                s1[base + layer, pl.ds(row + 8, CHUNK), :] = factor * source
                pair = pair + density
            put_halves(work, base >> 1, part, pair)

        chunks(height, begin)

    for j in range(1, 5):

        def smooth(row, j=j):
            part = pl.ds(row, CHUNK)
            v = s1[j, pl.ds(row + 8, CHUNK), :]
            f = stencil(s1, j, row, CHUNK)
            new = (1.0 - WEIGHT) * v + wd[j, part, :] * (rhs_w[j, part, :] + 2.0 * scale * (f - v))
            s2[j - 1, pl.ds(row + 8, CHUNK), :] = new
            s2_out[j - 1, part, :] = new
            wd_out[j - 1, part, :] = wd[j, part, :]

        chunks(height, smooth)
    rhs_halo[0] = rhs_w[1]
    rhs_halo[1] = rhs_w[4]

    def restrict(row):
        part = pl.ds(row, CHUNK)
        total = jnp.zeros((CHUNK, width), f32)
        for layer in range(2):
            v = s2[1 + layer, pl.ds(row + 8, CHUNK), :]
            f = stencil(s2, 1 + layer, row, CHUNK)
            center = own[2 + layer, part, :] + 16.0 * scale
            total = total + (own[layer, part, :] - center * v + 2.0 * scale * f)
        put_halves(work, 3, part, total)

    chunks(height, restrict)
    columns = coarsen_z(height, width)
    density1 = [0.125 * dot_exact(pair_rows(work, i, half), columns) for i in range(3)]
    coarse_res = 0.125 * dot_exact(pair_rows(work, 3, half), columns)

    send_a[0:half, :] = coarse_res
    send_a[half : 2 * half, :] = density1[1]
    mine = s2_out[1 + core]
    other = s2_out[2 - core]
    send_a[2 * half : 4 * half, :] = mine[:, :half]
    send_a[4 * half : 6 * half, :] = mine[:, half:]
    send_b[0] = other

    first = 0.85 * coarse_res / (density1[1] + 14.0 * scale1)
    pad = jnp.zeros((8, half), f32)
    spread = filter_yz(jnp.concatenate([pad, first, pad], 0))
    own_factor = WEIGHT / (density1[1] + 14.0 * scale1)
    shares = [
        (WEIGHT * valid_lo) * scale1 / (density1[0] + 14.0 * scale1) * spread,
        (1.0 - WEIGHT) * first + own_factor * (coarse_res + 2.0 * scale1 * (spread - first)),
        (WEIGHT * valid_hi) * scale1 / (density1[2] + 14.0 * scale1) * spread,
    ]
    block = half // TILES
    filtered = []
    plain = []
    for e, share in enumerate(shares):
        rest = -(density1[e] + 16.0 * scale1) * share
        if e == 1:
            rest = rest + coarse_res
        for t in range(TILES):
            at = t * block
            row = 2.0 * jnp.sum(share[at : at + block], axis=0, keepdims=True)
            row = row - 0.5 * (share[at : at + 1] + share[at + block - 1 : at + block])
            if t > 0:
                row = row + 0.5 * share[at - 1 : at]
            if t < TILES - 1:
                row = row + 0.5 * share[at + block : at + block + 1]
            filtered.append(row)
            plain.append(jnp.sum(rest[at : at + block], axis=0, keepdims=True))
    for t in range(TILES):
        plain.append(jnp.sum(density1[1][t * block : (t + 1) * block], axis=0, keepdims=True))
    filtered.append(jnp.zeros((4, half), f32))
    filtered = jnp.concatenate(filtered, 0)
    plain = jnp.concatenate(plain, 0)
    cell = iota((half, 128), 0)
    tile = iota((half, 128), 1) & 3
    start = tile * block
    inside = ((cell >= start) & (cell < start + block)).astype(f32)
    ends = ((cell == start) | (cell == start + block - 1)).astype(f32)
    beside = ((cell == start - 1) | (cell == start + block)).astype(f32)
    plain_w = inside.astype(bf16)
    filter_w = (2.0 * inside - 0.5 * ends + 0.5 * beside).astype(bf16)
    row = iota((16, 128), 0)
    lane = iota((16, 128), 1)
    fits = ((lane >> 2) & 3) == (row & 3)
    out = jnp.where(fits & ((lane >> 4) == (row >> 2)), dot_exact(filtered, filter_w), 0.0)
    out = jnp.where(row >= 12, 0.0, out)
    out = out + jnp.where(fits & ((lane >> 4) == (row >> 2) + 3), dot_exact(plain, plain_w), 0.0)
    payload[...] = jnp.broadcast_to(jnp.sum(out, axis=0, keepdims=True), payload.shape)


def lanes_sum(x):
    for step in (16, 32, 64):
        x = x + pltpu.roll(x, step, 1)
    return x


def row_before(x):
    return jnp.where(iota(x.shape, 0) == 0, 0.0, pltpu.roll(x, 1, 0))


def row_after(x):
    return jnp.where(iota(x.shape, 0) == x.shape[0] - 1, 0.0, pltpu.roll(x, x.shape[0] - 1, 0))


def solve_groups(gathered, ids, ids_packed, scale1, block):
    bricks = gathered.shape[0]
    lane = iota(gathered.shape, 1)
    slot = lane >> 4
    up = pltpu.roll(gathered, bricks - 1, 0)
    down = pltpu.roll(gathered, 1, 0)

    def pick(first):
        return lanes_sum(
            jnp.where(
                slot == first,
                up,
                jnp.where(slot == first + 1, gathered, jnp.where(slot == first + 2, down, 0.0)),
            )
        )

    filtered = pick(0)
    plain = pick(3)
    density_sum = lanes_sum(jnp.where(slot == 6, gathered, 0.0))
    remainder = plain + 2.0 * scale1 * filtered + scale1 * (row_before(filtered) + row_after(filtered))

    member = [(ids == ids_packed[j : j + 1]).astype(f32) for j in range(bricks // 8)]
    diagonal_lane = (iota(gathered.shape, 0) & 7) == slot

    def project(x):
        chosen = jnp.where(diagonal_lane, x, 0.0)
        total = jnp.zeros_like(x)
        for j in range(bricks // 8):
            total = total + member[j] * jnp.sum(chosen[8 * j : 8 * j + 8], axis=0, keepdims=True)
        return lanes_sum(total)

    place = iota(ids.shape, 0)
    ids_float = ids.astype(f32)
    as_before = jnp.where((place > 0) & (pltpu.roll(ids_float, 1, 0) == ids_float), 0.5, 0.0)
    as_after = jnp.where((place < bricks - 1) & (pltpu.roll(ids_float, bricks - 1, 0) == ids_float), 0.5, 0.0)
    inner = 2.0 * block - 1.0
    same = inner * inner * (1.0 + as_before + as_after)
    cells = float(block * block)
    diagonal = project(density_sum + scale1 * (16.0 * cells - 2.0 * same))
    group_rhs = project(remainder)
    column = lane & 3
    line = (lane >> 2) & 3
    center = density_sum + 16.0 * cells * scale1

    def image(g):
        z = inner * g + 0.5 * (
            jnp.where(column > 0, pltpu.roll(g, 1, 1), 0.0) + jnp.where(column < 3, pltpu.roll(g, 127, 1), 0.0)
        )
        y = inner * z + 0.5 * (
            jnp.where(line > 0, pltpu.roll(z, 4, 1), 0.0) + jnp.where(line < 3, pltpu.roll(z, 124, 1), 0.0)
        )
        return center * g - 2.0 * scale1 * (y + 0.5 * (row_before(y) + row_after(y)))

    factor = COARSE_WEIGHT / diagonal
    fix = factor * group_rhs
    for _ in range(COARSE_SWEEPS - 1):
        fix = fix + factor * (group_rhs - project(image(fix)))
    return fix


def second_kernel(
    meta, kappa, rhs, rhs_halo, s2, wd, send_a, sib, near_f, near, far, sib_near, sib_far, gathered, ids, ids_packed,
    sol_out, to_a, to_b,
    fixes, cres, cden, c1, c2, c3, grown, s3, s4,
):
    core, brick, bricks = meta[0], meta[1], meta[3]
    scale = kappa[0]
    scale1 = 0.25 * scale
    half = cres.shape[1]
    height, width = rhs.shape[2:]
    block = half // TILES
    for ref in (c1, c2, c3, s3, s4):
        clear_edges(ref)

    fixes[0:8, :] = jnp.zeros((8, 128), f32)
    count = gathered.shape[0]
    fixes[8 + count : 32 + count, :] = jnp.zeros((24, 128), f32)
    fixes[8 : 8 + count, :] = solve_groups(gathered[:, 0, :], ids[...], ids_packed[...], scale1, block)
    window = fixes[pl.ds(brick + 4, 16), :]
    lane = iota((128, TILES * half), 1)
    per = (lane >> (half.bit_length() - 1)) * 4 + ((lane & (half - 1)) >> (block.bit_length() - 1))
    spread = dot_exact(window, (iota((128, TILES * half), 0) == per).astype(bf16))

    sign = 2 * core - 1
    for ref, first, at in (
        (send_a, 0, 0), (sib, 0, -1),
        (near, 0, 1), (near, 2, 2), (far, 0, 3), (far, 2, 4),
        (sib_near, 0, -2), (sib_near, 2, -3), (sib_far, 0, -4),
    ):
        index = 4 + sign * at
        cres[index] = ref[first * half : (first + 1) * half, :]
        cden[index] = ref[(first + 1) * half : (first + 2) * half, :]

    body = pl.ds(8, half)
    factors = []
    for i in range(9):
        place = brick + (i - 4)
        valid = ((place >= 0) & (place < bricks)).astype(f32)
        factor = (WEIGHT * valid) / (cden[i] + 14.0 * scale1)
        cden[i] = factor
        c1[i, body, :] = factor * cres[i]

    def relax(ref, i, k):
        v = ref[i, body, :]
        f = stencil(ref, i, 0, half)
        return (1.0 - WEIGHT) * v + cden[k] * (cres[k] + 2.0 * scale1 * (f - v))

    for i in range(7):
        value = relax(c1, i + 1, i + 1)
        pieces = [
            jnp.broadcast_to(spread[i + 1 : i + 2, t * half : (t + 1) * half], (block, half)) for t in range(TILES)
        ]
        c2[i, body, :] = value + jnp.concatenate(pieces, 0)
    for i in range(5):
        c3[i, body, :] = relax(c2, i + 1, i + 2)
    columns = (iota((half, width), 0) == (iota((half, width), 1) >> 1)).astype(bf16)
    for i in range(3):
        fine = dot_exact(relax(c3, i + 1, i + 3), columns)
        put_halves(grown, i, pl.ds(0, half, stride=2), fine)
        put_halves(grown, i, pl.ds(1, half, stride=2), fine)

    inner = pl.ds(8, height)
    for k in range(2):
        side = slice(k * half, (k + 1) * half)
        for i in range(4):
            s3[i + 1, inner, side] = s2[i, :, side] + grown[(i + 1) >> 1, k]
        s3[5 * core, inner, side] = near_f[0, :, side] + grown[2 * core, k]
        s3[5 * (1 - core), inner, side] = sib[2 * (k + 1) * half : 2 * (k + 2) * half, :] + grown[2 * (1 - core), k]

    for j in range(4):

        def smooth(row, j=j):
            part = pl.ds(row, CHUNK)
            v = s3[j + 1, pl.ds(row + 8, CHUNK), :]
            f = stencil(s3, j + 1, row, CHUNK)
            source = rhs[0, j - 1, part, :] if j in (1, 2) else rhs_halo[j // 3, part, :]
            s4[j, pl.ds(row + 8, CHUNK), :] = (1.0 - WEIGHT) * v + wd[j, part, :] * (source + 2.0 * scale * (f - v))

        chunks(height, smooth)
    for j in range(2):

        def smooth_last(row, j=j):
            part = pl.ds(row, CHUNK)
            v = s4[j + 1, pl.ds(row + 8, CHUNK), :]
            f = stencil(s4, j + 1, row, CHUNK)
            new = (1.0 - WEIGHT) * v + wd[j + 1, part, :] * (rhs[0, j, part, :] + 2.0 * scale * (f - v))
            sol_out[0, j, part, :] = new

        chunks(height, smooth_last)
    to_a[...] = sol_out[0, pl.ds(1 - core, 1), :, :]
    to_b[...] = sol_out[0, pl.ds(core, 1), :, :]


def residual_kernel(meta, kappa, rhs, own, sol, halo_a, halo_b, out, s):
    core = meta[0]
    scale = kappa[0]
    height, width = rhs.shape[2:]
    clear_edges(s)
    inner = pl.ds(8, height)
    s[1, inner, :] = sol[0, 0]
    s[2, inner, :] = sol[0, 1]
    s[3 * core, inner, :] = halo_b[0]
    s[3 * (1 - core), inner, :] = halo_a[0]
    for j in range(2):

        def finish(row, j=j):
            part = pl.ds(row, CHUNK)
            v = s[j + 1, pl.ds(row + 8, CHUNK), :]
            f = stencil(s, j + 1, row, CHUNK)
            center = own[2 + j, part, :] + 16.0 * scale
            out[0, j, part, :] = rhs[0, j, part, :] - center * v + 2.0 * scale * f

        chunks(height, finish)


def shape(*dims):
    return jax.ShapeDtypeStruct(dims, f32)


def local(rhs, density, kappa, block_group):
    bricks = lax.axis_size("brick")
    species = lax.axis_size("spec")
    brick = lax.axis_index("brick")
    height, width = rhs.shape[2:]
    half = height // 2
    meta = jnp.stack([brick % 2, brick, lax.axis_index("spec"), jnp.int32(bricks)]).astype(jnp.int32)
    ids = jnp.tile(block_group, (1, 8))
    ids_packed = block_group.reshape(bricks // 8, 128)
    in_chip = [(i, i ^ 1) for i in range(bricks)]
    next_chip = [(i, ((i + 1) ^ 1) - 1) for i in range(1, bricks - 1)]
    second_chip = [(i, i - 3) for i in range(4, bricks, 2)] + [(i, i + 3) for i in range(1, bricks - 3, 2)]

    def swap_a(x):
        return lax.ppermute(x, "brick", in_chip)

    def swap_b(x):
        return lax.ppermute(x, "brick", next_chip)

    def swap_far(x):
        return lax.ppermute(x, "brick", second_chip)

    def around(x, k):
        return lax.ppermute(x, "spec", [(i, (i + k) % species) for i in range(species)])

    pieces = [around(density, k) for k in (1, 2, 3)]
    own = pl.pallas_call(
        gather_kernel,
        out_shape=shape(4, height, width),
        in_specs=[SM] + [VM] * 5,
        out_specs=VM,
        compiler_params=PARAMS,
        name="collect_density",
    )(meta, rhs, density, *pieces)

    from_b = swap_b(own)
    from_a = swap_a(own)
    s2, wd, rhs_halo, send_a, send_b, payload = pl.pallas_call(
        first_kernel,
        out_shape=(
            shape(4, height, width),
            shape(4, height, width),
            shape(2, height, width),
            shape(6 * half, half),
            shape(1, height, width),
            shape(bricks, 128),
        ),
        in_specs=[SM, SM] + [VM] * 3,
        out_specs=[VM] * 6,
        scratch_shapes=[
            pltpu.VMEM((6, height + 16, width), f32),
            pltpu.VMEM((4, height + 16, width), f32),
            pltpu.VMEM((6, height, width), f32),
            pltpu.VMEM((6, height, width), f32),
            pltpu.VMEM((4, 2, height, half), f32),
        ],
        compiler_params=PARAMS,
        name="smooth_and_restrict",
    )(meta, kappa, own, from_a, from_b)

    gathered = lax.all_to_all(payload.reshape(bricks, 1, 128), "brick", 0, 0, tiled=True)
    sib = swap_a(send_a)
    near_f = swap_b(send_b)
    both = jnp.concatenate([send_a[: 2 * half], sib[: 2 * half]], 0)
    near = swap_b(both)
    far = swap_far(both)
    sib_near = swap_a(near)
    sib_far = swap_a(far)

    solution, to_a, to_b = pl.pallas_call(
        second_kernel,
        out_shape=(shape(1, 2, height, width), shape(1, height, width), shape(1, height, width)),
        in_specs=[SM, SM] + [VM] * 14,
        out_specs=[VM] * 3,
        scratch_shapes=[
            pltpu.VMEM((bricks + 32, 128), f32),
            pltpu.VMEM((9, half, half), f32),
            pltpu.VMEM((9, half, half), f32),
            pltpu.VMEM((9, half + 16, half), f32),
            pltpu.VMEM((7, half + 16, half), f32),
            pltpu.VMEM((5, half + 16, half), f32),
            pltpu.VMEM((3, 2, height, half), f32),
            pltpu.VMEM((6, height + 16, width), f32),
            pltpu.VMEM((4, height + 16, width), f32),
        ],
        compiler_params=PARAMS,
        name="correct_and_smooth",
    )(
        meta, kappa, rhs, rhs_halo, s2, wd, send_a, sib, near_f, near, far, sib_near, sib_far, gathered, ids, ids_packed
    )

    halo_b = swap_b(to_b)
    halo_a = swap_a(to_a)
    residual = pl.pallas_call(
        residual_kernel,
        out_shape=shape(1, 2, height, width),
        in_specs=[SM, SM] + [VM] * 5,
        out_specs=VM,
        scratch_shapes=[pltpu.VMEM((4, height + 16, width), f32)],
        compiler_params=PARAMS,
        name="residual",
    )(meta, kappa, rhs, own, solution, halo_a, halo_b)
    return (solution, residual)


def solution(mesh):
    return jax.shard_map(
        local,
        mesh=mesh,
        in_specs=(P("spec", "brick", None, None), P("brick", "spec", None), P("spec"), P()),
        out_specs=(P("spec", "brick", None, None), P("spec", "brick", None, None)),
        check_vma=False,
    )
```

```python
import functools

import jax
import jax.numpy as jnp
from jax import lax
from jax.experimental import pallas as pl
from jax.experimental.pallas import tpu as pltpu
from jax.sharding import PartitionSpec as P

WEIGHT = 0.85
COARSE_WEIGHT = 0.6
COARSE_SWEEPS = 3
TILES = 4
CHUNK = 64
f32 = jnp.float32
bf16 = jnp.bfloat16
VM = pl.BlockSpec(memory_space=pltpu.VMEM)
ANY = pl.BlockSpec(memory_space=pl.ANY)
PARAMS = pltpu.CompilerParams(vmem_limit_bytes=16 * 1024 * 1024)


def iota(shape, dim):
    return lax.broadcasted_iota(jnp.int32, shape, dim)


def split(x):
    high = x.astype(bf16)
    rest = x - high.astype(f32)
    middle = rest.astype(bf16)
    low = (rest - middle.astype(f32)).astype(bf16)
    return high, middle, low


def dot_exact(x, w):
    high, middle, low = split(x)
    dot = functools.partial(jnp.dot, preferred_element_type=f32)
    return dot(high, w) + (dot(middle, w) + dot(low, w))


def filter_z(y):
    width = y.shape[1]
    lane = iota(y.shape, 1)
    before = jnp.where(lane == 0, 0.0, pltpu.roll(y, 1, 1))
    after = jnp.where(lane == width - 1, 0.0, pltpu.roll(y, width - 1, 1))
    return y + 0.5 * (before + after)


def filter_yz(m):
    rows = m.shape[0]
    y = m + 0.5 * (pltpu.roll(m, 1, 0) + pltpu.roll(m, rows - 1, 0))
    return filter_z(y[8 : rows - 8])


def stencil(ref, i, row, rows):
    part = pl.ds(row, rows + 16)
    return filter_yz(ref[i, part, :] + 0.5 * (ref[i - 1, part, :] + ref[i + 1, part, :]))


def clear_edges(ref):
    layers, rows, width = ref.shape
    zero = jnp.zeros((layers, 8, width), f32)
    ref[:, 0:8, :] = zero
    ref[:, rows - 8 : rows, :] = zero


def chunks(rows, body):
    def step(c, carry):
        body(pl.multiple_of(c * CHUNK, CHUNK))
        return carry

    lax.fori_loop(0, rows // CHUNK, step, 0)


def coarsen_z(rows, width):
    return ((iota((width, width // 2), 0) >> 1) == iota((width, width // 2), 1)).astype(bf16)


def put_halves(ref, i, part, x):
    half = x.shape[1] // 2
    ref[i, 0, part, :] = x[:, :half]
    ref[i, 1, part, :] = x[:, half:]


def pair_rows(ref, i, half):
    even, odd = pl.ds(0, half, stride=2), pl.ds(1, half, stride=2)
    return jnp.concatenate([ref[i, k, even, :] + ref[i, k, odd, :] for k in range(2)], 1)


def position():
    brick = lax.axis_index("brick")
    return brick & 1, brick, lax.axis_size("brick")


def start_all(copies):
    for copy in copies:
        copy.start()


def wait_all(copies):
    for copy in copies:
        copy.wait()


def join_kernel(mine, other, out, sems):
    rows = out.shape[0] // 2
    copies = [
        pltpu.make_async_copy(mine.at[pl.ds(0, rows)], out.at[pl.ds(0, rows)], sems.at[0]),
        pltpu.make_async_copy(other.at[pl.ds(0, rows)], out.at[pl.ds(rows, rows)], sems.at[1]),
    ]
    start_all(copies)
    wait_all(copies)


def gather_kernel(shard, p1, p2, p3, dens, sems):
    count = 4
    rows = shard.shape[1]
    copies = []
    for k, piece in enumerate((shard, p1, p2, p3)):
        owner = lax.rem(lax.axis_index("spec") - k + count, count)
        place = pl.ds(pl.multiple_of(owner * rows, rows), rows)
        copies.append(pltpu.make_async_copy(piece, dens.at[:, place, :], sems.at[k]))
    start_all(copies)
    wait_all(copies)


def first_kernel(
    kappa_in, rhs, dens, rhs_a, dens_a, rhs_b, dens_b,
    s2_out, halo_out, send_a, send_b, payload,
    s1, s2, wd, rhs_w, work, kappa, sems,
):
    core, brick, bricks = position()
    load = pltpu.make_async_copy(kappa_in, kappa, sems.at[0])
    load.start()
    height, width = dens.shape[1:]
    half = height // 2
    clear_edges(s1)
    clear_edges(s2)
    load.wait()
    scale = kappa[0]
    scale1 = 0.25 * scale

    base_b = 4 * core
    base_a = 4 * (1 - core)
    valid_lo = (brick > 0).astype(f32)
    valid_hi = (brick < bricks - 1).astype(f32)
    valid_b = jnp.where(core == 0, valid_lo, valid_hi)
    valid_a = jnp.where(core == 0, valid_hi, valid_lo)
    for ref, density_ref, base, valid in ((rhs_b, dens_b, base_b, valid_b), (rhs_a, dens_a, base_a, valid_a), (rhs, dens, 2, None)):
        top = WEIGHT if valid is None else WEIGHT * valid

        def begin(row, ref=ref, density_ref=density_ref, base=base, top=top):
            part = pl.ds(row, CHUNK)
            pair = jnp.zeros((CHUNK, width), f32)
            for layer in range(2):
                density = density_ref[layer, part, :]
                factor = top / (density + 14.0 * scale)
                wd[base + layer, part, :] = factor
                source = ref[0, layer, part, :]
                rhs_w[base + layer, part, :] = source
                s1[base + layer, pl.ds(row + 8, CHUNK), :] = factor * source
                pair = pair + density
            put_halves(work, base >> 1, part, pair)

        chunks(height, begin)

    for j in range(1, 5):

        def smooth(row, j=j):
            part = pl.ds(row, CHUNK)
            v = s1[j, pl.ds(row + 8, CHUNK), :]
            f = stencil(s1, j, row, CHUNK)
            new = (1.0 - WEIGHT) * v + wd[j, part, :] * (rhs_w[j, part, :] + 2.0 * scale * (f - v))
            s2[j - 1, pl.ds(row + 8, CHUNK), :] = new
            s2_out[j - 1, part, :] = new

        chunks(height, smooth)
    halo_out[0] = rhs_w[1]
    halo_out[1] = rhs_w[4]
    for ref, layer, edge in ((dens_b, 1 - core, core), (dens_a, core, 1 - core)):
        halo_out[2 + edge] = ref[layer]
    mine = 1 + core
    send_a[2 * half : 4 * half, :] = s2_out[mine, :, :half]
    send_a[4 * half : 6 * half, :] = s2_out[mine, :, half:]
    send_b[0] = s2_out[2 - core]

    def restrict(row):
        part = pl.ds(row, CHUNK)
        total = jnp.zeros((CHUNK, width), f32)
        for layer in range(2):
            v = s2[1 + layer, pl.ds(row + 8, CHUNK), :]
            f = stencil(s2, 1 + layer, row, CHUNK)
            center = dens[layer, part, :] + 16.0 * scale
            total = total + (rhs_w[2 + layer, part, :] - center * v + 2.0 * scale * f)
        put_halves(work, 3, part, total)

    chunks(height, restrict)
    columns = coarsen_z(height, width)
    density1 = [0.125 * dot_exact(pair_rows(work, i, half), columns) for i in range(3)]
    coarse_res = 0.125 * dot_exact(pair_rows(work, 3, half), columns)

    send_a[0:half, :] = coarse_res
    send_a[half : 2 * half, :] = density1[1]

    first = 0.85 * coarse_res / (density1[1] + 14.0 * scale1)
    pad = jnp.zeros((8, half), f32)
    spread = filter_yz(jnp.concatenate([pad, first, pad], 0))
    own_factor = WEIGHT / (density1[1] + 14.0 * scale1)
    shares = [
        (WEIGHT * valid_lo) * scale1 / (density1[0] + 14.0 * scale1) * spread,
        (1.0 - WEIGHT) * first + own_factor * (coarse_res + 2.0 * scale1 * (spread - first)),
        (WEIGHT * valid_hi) * scale1 / (density1[2] + 14.0 * scale1) * spread,
    ]
    block = half // TILES
    filtered = []
    plain = []
    for e, share in enumerate(shares):
        rest = -(density1[e] + 16.0 * scale1) * share
        if e == 1:
            rest = rest + coarse_res
        for t in range(TILES):
            at = t * block
            row = 2.0 * jnp.sum(share[at : at + block], axis=0, keepdims=True)
            row = row - 0.5 * (share[at : at + 1] + share[at + block - 1 : at + block])
            if t > 0:
                row = row + 0.5 * share[at - 1 : at]
            if t < TILES - 1:
                row = row + 0.5 * share[at + block : at + block + 1]
            filtered.append(row)
            plain.append(jnp.sum(rest[at : at + block], axis=0, keepdims=True))
    for t in range(TILES):
        plain.append(jnp.sum(density1[1][t * block : (t + 1) * block], axis=0, keepdims=True))
    filtered.append(jnp.zeros((4, half), f32))
    filtered = jnp.concatenate(filtered, 0)
    plain = jnp.concatenate(plain, 0)
    cell = iota((half, 128), 0)
    tile = iota((half, 128), 1) & 3
    start = tile * block
    inside = ((cell >= start) & (cell < start + block)).astype(f32)
    ends = ((cell == start) | (cell == start + block - 1)).astype(f32)
    beside = ((cell == start - 1) | (cell == start + block)).astype(f32)
    plain_w = inside.astype(bf16)
    filter_w = (2.0 * inside - 0.5 * ends + 0.5 * beside).astype(bf16)
    row = iota((16, 128), 0)
    lane = iota((16, 128), 1)
    fits = ((lane >> 2) & 3) == (row & 3)
    out = jnp.where(fits & ((lane >> 4) == (row >> 2)), dot_exact(filtered, filter_w), 0.0)
    out = jnp.where(row >= 12, 0.0, out)
    out = out + jnp.where(fits & ((lane >> 4) == (row >> 2) + 3), dot_exact(plain, plain_w), 0.0)
    payload[...] = jnp.broadcast_to(jnp.sum(out, axis=0, keepdims=True), payload.shape)


def lanes_sum(x):
    for step in (16, 32, 64):
        x = x + pltpu.roll(x, step, 1)
    return x


def row_before(x):
    return jnp.where(iota(x.shape, 0) == 0, 0.0, pltpu.roll(x, 1, 0))


def row_after(x):
    return jnp.where(iota(x.shape, 0) == x.shape[0] - 1, 0.0, pltpu.roll(x, x.shape[0] - 1, 0))


def solve_groups(gathered, groups, scale1, block):
    bricks = gathered.shape[0]
    lane = iota(gathered.shape, 1)
    slot = lane >> 4
    up = pltpu.roll(gathered, bricks - 1, 0)
    down = pltpu.roll(gathered, 1, 0)

    def pick(first):
        return lanes_sum(
            jnp.where(
                slot == first,
                up,
                jnp.where(slot == first + 1, gathered, jnp.where(slot == first + 2, down, 0.0)),
            )
        )

    filtered = pick(0)
    plain = pick(3)
    density_sum = lanes_sum(jnp.where(slot == 6, gathered, 0.0))
    remainder = plain + 2.0 * scale1 * filtered + scale1 * (row_before(filtered) + row_after(filtered))

    blocks = groups.shape[1]
    repeat = (iota((blocks, 128), 0) == (iota((blocks, 128), 1) & (blocks - 1))).astype(bf16)
    ids = jnp.dot(groups.astype(f32).astype(bf16), repeat, preferred_element_type=f32)
    diagonal_lane = (iota(gathered.shape, 0) & 7) == slot
    packed = jnp.where(diagonal_lane, ids, 0.0)
    member = [
        (ids == jnp.sum(packed[8 * j : 8 * j + 8], axis=0, keepdims=True)).astype(f32) for j in range(bricks // 8)
    ]

    def project(x):
        chosen = jnp.where(diagonal_lane, x, 0.0)
        total = jnp.zeros_like(x)
        for j in range(bricks // 8):
            total = total + member[j] * jnp.sum(chosen[8 * j : 8 * j + 8], axis=0, keepdims=True)
        return lanes_sum(total)

    place = iota(ids.shape, 0)
    as_before = jnp.where((place > 0) & (pltpu.roll(ids, 1, 0) == ids), 0.5, 0.0)
    as_after = jnp.where((place < bricks - 1) & (pltpu.roll(ids, bricks - 1, 0) == ids), 0.5, 0.0)
    inner = 2.0 * block - 1.0
    same = inner * inner * (1.0 + as_before + as_after)
    cells = float(block * block)
    diagonal = project(density_sum + scale1 * (16.0 * cells - 2.0 * same))
    group_rhs = project(remainder)
    column = lane & 3
    line = (lane >> 2) & 3
    center = density_sum + 16.0 * cells * scale1

    def image(g):
        z = inner * g + 0.5 * (
            jnp.where(column > 0, pltpu.roll(g, 1, 1), 0.0) + jnp.where(column < 3, pltpu.roll(g, 127, 1), 0.0)
        )
        y = inner * z + 0.5 * (
            jnp.where(line > 0, pltpu.roll(z, 4, 1), 0.0) + jnp.where(line < 3, pltpu.roll(z, 124, 1), 0.0)
        )
        return center * g - 2.0 * scale1 * (y + 0.5 * (row_before(y) + row_after(y)))

    factor = COARSE_WEIGHT / diagonal
    fix = factor * group_rhs
    for _ in range(COARSE_SWEEPS - 1):
        fix = fix + factor * (group_rhs - project(image(fix)))
    return fix


def second_kernel(
    kappa_in, rhs, dens, halo, s2, near_f, send_a, sib, near, far, sib_near, sib_far, gathered, groups,
    sol_out, to_a, to_b,
    fixes, cres, cden, c1, c2, c3, grown, s3, s4, wd, kappa, sems,
):
    core, brick, bricks = position()
    load = pltpu.make_async_copy(kappa_in, kappa, sems.at[0])
    load.start()
    half = cres.shape[1]
    height, width = rhs.shape[2:]
    block = half // TILES
    inner = pl.ds(8, height)
    for ref in (c1, c2, c3, s3, s4):
        clear_edges(ref)
    load.wait()
    scale = kappa[0]
    scale1 = 0.25 * scale

    fixes[0:8, :] = jnp.zeros((8, 128), f32)
    count = gathered.shape[0]
    fixes[8 + count : 32 + count, :] = jnp.zeros((24, 128), f32)
    fixes[8 : 8 + count, :] = solve_groups(gathered[:, 0, :], groups[...], scale1, block)
    window = fixes[pl.ds(brick + 4, 16), :]
    lane = iota((128, TILES * half), 1)
    per = (lane >> (half.bit_length() - 1)) * 4 + ((lane & (half - 1)) >> (block.bit_length() - 1))
    spread = dot_exact(window, (iota((128, TILES * half), 0) == per).astype(bf16))

    sign = 2 * core - 1
    for ref, first, at in (
        (send_a, 0, 0), (sib, 0, -1),
        (near, 0, 1), (near, 2, 2), (far, 0, 3), (far, 2, 4),
        (sib_near, 0, -2), (sib_near, 2, -3), (sib_far, 0, -4),
    ):
        index = 4 + sign * at
        cres[index] = ref[first * half : (first + 1) * half, :]
        cden[index] = ref[(first + 1) * half : (first + 2) * half, :]

    body = pl.ds(8, half)
    factors = []
    for i in range(9):
        place = brick + (i - 4)
        valid = ((place >= 0) & (place < bricks)).astype(f32)
        factor = (WEIGHT * valid) / (cden[i] + 14.0 * scale1)
        cden[i] = factor
        c1[i, body, :] = factor * cres[i]

    def relax(ref, i, k):
        v = ref[i, body, :]
        f = stencil(ref, i, 0, half)
        return (1.0 - WEIGHT) * v + cden[k] * (cres[k] + 2.0 * scale1 * (f - v))

    for i in range(7):
        value = relax(c1, i + 1, i + 1)
        pieces = [
            jnp.broadcast_to(spread[i + 1 : i + 2, t * half : (t + 1) * half], (block, half)) for t in range(TILES)
        ]
        c2[i, body, :] = value + jnp.concatenate(pieces, 0)
    for i in range(5):
        c3[i, body, :] = relax(c2, i + 1, i + 2)
    columns = (iota((half, width), 0) == (iota((half, width), 1) >> 1)).astype(bf16)
    for i in range(3):
        fine = dot_exact(relax(c3, i + 1, i + 3), columns)
        put_halves(grown, i, pl.ds(0, half, stride=2), fine)
        put_halves(grown, i, pl.ds(1, half, stride=2), fine)

    for k in range(2):
        side = slice(k * half, (k + 1) * half)
        for i in range(4):
            s3[i + 1, inner, side] = s2[i, :, side] + grown[(i + 1) >> 1, k]
        s3[5 * core, inner, side] = near_f[0, :, side] + grown[2 * core, k]
        s3[5 * (1 - core), inner, side] = sib[2 * (k + 1) * half : 2 * (k + 2) * half, :] + grown[2 * (1 - core), k]

    for j in range(4):

        def smooth(row, j=j):
            part = pl.ds(row, CHUNK)
            v = s3[j + 1, pl.ds(row + 8, CHUNK), :]
            f = stencil(s3, j + 1, row, CHUNK)
            if j in (1, 2):
                source, density, top = rhs[0, j - 1, part, :], dens[j - 1, part, :], WEIGHT
            else:
                edge = j // 3
                source, density = halo[edge, part, :], halo[2 + edge, part, :]
                top = WEIGHT * (brick < bricks - 1 if edge else brick > 0).astype(f32)
            factor = top / (density + 14.0 * scale)
            wd[j, part, :] = factor
            new = (1.0 - WEIGHT) * v + factor * (source + 2.0 * scale * (f - v))
            s4[j, pl.ds(row + 8, CHUNK), :] = new

        chunks(height, smooth)
    for j in range(2):

        def smooth_last(row, j=j):
            part = pl.ds(row, CHUNK)
            v = s4[j + 1, pl.ds(row + 8, CHUNK), :]
            f = stencil(s4, j + 1, row, CHUNK)
            new = (1.0 - WEIGHT) * v + wd[j + 1, part, :] * (rhs[0, j, part, :] + 2.0 * scale * (f - v))
            sol_out[0, j, part, :] = new

        chunks(height, smooth_last)
    to_a[...] = sol_out[0, pl.ds(1 - core, 1), :, :]
    to_b[...] = sol_out[0, pl.ds(core, 1), :, :]


def inside_kernel(kappa_in, rhs, dens, sol_in, out, s, kappa, sems):
    height, width = dens.shape[1:]
    inner = pl.ds(8, height)
    loads = [
        pltpu.make_async_copy(sol_in.at[0], s.at[:, inner, :], sems.at[0]),
        pltpu.make_async_copy(kappa_in, kappa, sems.at[1]),
    ]
    start_all(loads)
    clear_edges(s)
    wait_all(loads)
    scale = kappa[0]
    for j in range(2):

        def finish(row, j=j):
            part = pl.ds(row, CHUNK)
            more = pl.ds(row, CHUNK + 16)
            f = filter_yz(s[j, more, :] + 0.5 * s[1 - j, more, :])
            center = dens[j, part, :] + 16.0 * scale
            out[j, part, :] = rhs[0, j, part, :] - center * s[j, pl.ds(row + 8, CHUNK), :] + 2.0 * scale * f

        chunks(height, finish)


def residual_kernel(kappa_in, inside, halo_a, halo_b, out, s, kappa, sems):
    core = position()[0]
    height = inside.shape[1]
    inner = pl.ds(8, height)
    loads = [
        pltpu.make_async_copy(halo_b.at[0], s.at[core, inner, :], sems.at[0]),
        pltpu.make_async_copy(halo_a.at[0], s.at[1 - core, inner, :], sems.at[1]),
        pltpu.make_async_copy(kappa_in, kappa, sems.at[2]),
    ]
    start_all(loads)
    clear_edges(s)
    wait_all(loads)
    scale = kappa[0]
    for j in range(2):

        def finish(row, j=j):
            part = pl.ds(row, CHUNK)
            out[0, j, part, :] = inside[j, part, :] + scale * filter_yz(s[j, pl.ds(row, CHUNK + 16), :])

        chunks(height, finish)


def shape(*dims):
    return jax.ShapeDtypeStruct(dims, f32)


def local(rhs, density, kappa, block_group):
    bricks = lax.axis_size("brick")
    species = lax.axis_size("spec")
    height, width = rhs.shape[2:]
    half = height // 2
    in_chip = [(i, i ^ 1) for i in range(bricks)]
    next_chip = [(i, ((i + 1) ^ 1) - 1) for i in range(1, bricks - 1)]
    second_chip = [(i, i - 3) for i in range(4, bricks, 2)] + [(i, i + 3) for i in range(1, bricks - 3, 2)]

    def swap_a(x):
        return lax.ppermute(x, "brick", in_chip)

    def swap_b(x):
        return lax.ppermute(x, "brick", next_chip)

    def swap_far(x):
        return lax.ppermute(x, "brick", second_chip)

    def around(x, k):
        return lax.ppermute(x, "spec", [(i, (i + k) % species) for i in range(species)])

    pieces = [around(density, k) for k in (1, 2, 3)]
    rhs_b = swap_b(rhs)
    rhs_a = swap_a(rhs)
    dens = pl.pallas_call(
        gather_kernel,
        out_shape=shape(2, height, width),
        in_specs=[ANY] * 4,
        out_specs=VM,
        scratch_shapes=[pltpu.SemaphoreType.DMA((4,))],
        compiler_params=PARAMS,
        name="collect_density",
    )(density, *pieces)

    dens_b = swap_b(dens)
    dens_a = swap_a(dens)
    s2, halo, send_a, send_b, payload = pl.pallas_call(
        first_kernel,
        out_shape=(
            shape(4, height, width),
            shape(4, height, width),
            shape(6 * half, half),
            shape(1, height, width),
            shape(bricks, 128),
        ),
        in_specs=[ANY] + [VM] * 6,
        out_specs=[VM] * 5,
        scratch_shapes=[
            pltpu.VMEM((6, height + 16, width), f32),
            pltpu.VMEM((4, height + 16, width), f32),
            pltpu.VMEM((6, height, width), f32),
            pltpu.VMEM((6, height, width), f32),
            pltpu.VMEM((4, 2, height, half), f32),
            pltpu.SMEM((1,), f32),
            pltpu.SemaphoreType.DMA((1,)),
        ],
        compiler_params=PARAMS,
        name="smooth_and_restrict",
    )(kappa, rhs, dens, rhs_a, dens_a, rhs_b, dens_b)

    gathered = lax.all_to_all(payload.reshape(bricks, 1, 128), "brick", 0, 0, tiled=True)
    sib = swap_a(send_a)
    near_f = swap_b(send_b)
    both = pl.pallas_call(
        join_kernel,
        out_shape=shape(4 * half, half),
        in_specs=[ANY] * 2,
        out_specs=VM,
        scratch_shapes=[pltpu.SemaphoreType.DMA((2,))],
        compiler_params=PARAMS,
        name="join_chip",
    )(send_a, sib)
    near = swap_b(both)
    far = swap_far(both)
    near, far, gathered = lax.optimization_barrier((near, far, gathered))
    sib_near = swap_a(near)
    sib_far = swap_a(far)

    solution, to_a, to_b = pl.pallas_call(
        second_kernel,
        out_shape=(shape(1, 2, height, width), shape(1, height, width), shape(1, height, width)),
        in_specs=[ANY] + [VM] * 13,
        out_specs=[VM] * 3,
        scratch_shapes=[
            pltpu.VMEM((bricks + 32, 128), f32),
            pltpu.VMEM((9, half, half), f32),
            pltpu.VMEM((9, half, half), f32),
            pltpu.VMEM((9, half + 16, half), f32),
            pltpu.VMEM((7, half + 16, half), f32),
            pltpu.VMEM((5, half + 16, half), f32),
            pltpu.VMEM((3, 2, height, half), f32),
            pltpu.VMEM((6, height + 16, width), f32),
            pltpu.VMEM((4, height + 16, width), f32),
            pltpu.VMEM((4, height, width), f32),
            pltpu.SMEM((1,), f32),
            pltpu.SemaphoreType.DMA((1,)),
        ],
        compiler_params=PARAMS,
        name="correct_and_smooth",
    )(
        kappa, rhs, dens, halo, s2, near_f, send_a, sib, near, far, sib_near, sib_far, gathered, block_group
    )

    halo_b = swap_b(to_b)
    halo_a = swap_a(to_a)
    inside = pl.pallas_call(
        inside_kernel,
        out_shape=shape(2, height, width),
        in_specs=[ANY] + [VM] * 2 + [ANY],
        out_specs=VM,
        scratch_shapes=[pltpu.VMEM((2, height + 16, width), f32), pltpu.SMEM((1,), f32), pltpu.SemaphoreType.DMA((2,))],
        compiler_params=PARAMS,
        name="residual_inside",
    )(kappa, rhs, dens, solution)
    residual = pl.pallas_call(
        residual_kernel,
        out_shape=shape(1, 2, height, width),
        in_specs=[ANY, VM] + [ANY] * 2,
        out_specs=VM,
        scratch_shapes=[pltpu.VMEM((2, height + 16, width), f32), pltpu.SMEM((1,), f32), pltpu.SemaphoreType.DMA((3,))],
        compiler_params=PARAMS,
        name="residual",
    )(kappa, inside, halo_a, halo_b)
    return (solution, residual)


def solution(mesh):
    return jax.shard_map(
        local,
        mesh=mesh,
        in_specs=(P("spec", "brick", None, None), P("brick", "spec", None), P("spec"), P()),
        out_specs=(P("spec", "brick", None, None), P("spec", "brick", None, None)),
        check_vma=False,
    )
```

```python
import functools

import jax
import jax.numpy as jnp
from jax import lax
from jax.experimental import pallas as pl
from jax.experimental.pallas import tpu as pltpu
from jax.sharding import PartitionSpec as P

WEIGHT = 0.85
COARSE_WEIGHT = 0.6
COARSE_SWEEPS = 3
TILES = 4
CHUNK = 64
f32 = jnp.float32
bf16 = jnp.bfloat16
VM = pl.BlockSpec(memory_space=pltpu.VMEM)
ANY = pl.BlockSpec(memory_space=pl.ANY)
HBM = pl.BlockSpec(memory_space=pltpu.HBM)
PARAMS = pltpu.CompilerParams(vmem_limit_bytes=16 * 1024 * 1024)


def iota(shape, dim):
    return lax.broadcasted_iota(jnp.int32, shape, dim)


def split(x):
    high = x.astype(bf16)
    rest = x - high.astype(f32)
    middle = rest.astype(bf16)
    low = (rest - middle.astype(f32)).astype(bf16)
    return high, middle, low


def dot_exact(x, w):
    high, middle, low = split(x)
    dot = functools.partial(jnp.dot, preferred_element_type=f32)
    return dot(high, w) + (dot(middle, w) + dot(low, w))


def filter_z(y):
    width = y.shape[1]
    lane = iota((1, width), 1)
    before = jnp.where(lane == 0, 0.0, 0.5)
    after = jnp.where(lane == width - 1, 0.0, 0.5)
    return y + before * pltpu.roll(y, 1, 1) + after * pltpu.roll(y, width - 1, 1)


def filter_yz(m):
    rows = m.shape[0]
    y = m + 0.5 * (pltpu.roll(m, 1, 0) + pltpu.roll(m, rows - 1, 0))
    return filter_z(y[8 : rows - 8])


def stencil(ref, i, row, rows):
    part = pl.ds(row, rows + 16)
    return filter_yz(ref[i, part, :] + 0.5 * (ref[i - 1, part, :] + ref[i + 1, part, :]))


def clear_edges(ref):
    layers, rows, width = ref.shape
    zero = jnp.zeros((layers, 8, width), f32)
    ref[:, 0:8, :] = zero
    ref[:, rows - 8 : rows, :] = zero


def chunks(rows, body):
    for row in range(0, rows, CHUNK):
        body(row)


def coarsen_z(rows, width):
    return ((iota((width, width // 2), 0) >> 1) == iota((width, width // 2), 1)).astype(bf16)


def put_halves(ref, i, part, x):
    half = x.shape[1] // 2
    ref[i, 0, part, :] = x[:, :half]
    ref[i, 1, part, :] = x[:, half:]


def pair_rows(ref, i, half):
    even, odd = pl.ds(0, half, stride=2), pl.ds(1, half, stride=2)
    return jnp.concatenate([ref[i, k, even, :] + ref[i, k, odd, :] for k in range(2)], 1)


def position():
    brick = lax.axis_index("brick")
    return brick & 1, brick, lax.axis_size("brick")


def start_all(copies):
    for copy in copies:
        copy.start()


def wait_all(copies):
    for copy in copies:
        copy.wait()


def join_kernel(mine, other, out, sems):
    rows = out.shape[0] // 2
    copies = [
        pltpu.make_async_copy(mine.at[pl.ds(0, rows)], out.at[pl.ds(0, rows)], sems.at[0]),
        pltpu.make_async_copy(other.at[pl.ds(0, rows)], out.at[pl.ds(rows, rows)], sems.at[1]),
    ]
    start_all(copies)
    wait_all(copies)


def gather_kernel(shard, p1, p2, p3, dens, sems):
    count = 4
    rows = shard.shape[1]
    copies = []
    for k, piece in enumerate((shard, p1, p2, p3)):
        owner = lax.rem(lax.axis_index("spec") - k + count, count)
        place = pl.ds(pl.multiple_of(owner * rows, rows), rows)
        copies.append(pltpu.make_async_copy(piece, dens.at[:, place, :], sems.at[k]))
    start_all(copies)
    wait_all(copies)


def first_kernel(
    kappa_in, rhs, dens, rhs_a, dens_a, rhs_b, dens_b,
    s2_out, halo_out, send_a, send_b, payload,
    s1, s2, wd, rhs_w, work, kappa, sems,
):
    core, brick, bricks = position()
    load = pltpu.make_async_copy(kappa_in, kappa, sems.at[0])
    load.start()
    height, width = dens.shape[1:]
    half = height // 2
    clear_edges(s1)
    clear_edges(s2)
    load.wait()
    scale = kappa[0]
    scale1 = 0.25 * scale

    base_b = 4 * core
    base_a = 4 * (1 - core)
    valid_lo = (brick > 0).astype(f32)
    valid_hi = (brick < bricks - 1).astype(f32)
    valid_b = jnp.where(core == 0, valid_lo, valid_hi)
    valid_a = jnp.where(core == 0, valid_hi, valid_lo)
    for ref, density_ref, base, valid in ((rhs_b, dens_b, base_b, valid_b), (rhs_a, dens_a, base_a, valid_a), (rhs, dens, 2, None)):
        top = WEIGHT if valid is None else WEIGHT * valid

        def begin(row, ref=ref, density_ref=density_ref, base=base, top=top):
            part = pl.ds(row, CHUNK)
            pair = jnp.zeros((CHUNK, width), f32)
            for layer in range(2):
                density = density_ref[layer, part, :]
                factor = top / (density + 14.0 * scale)
                wd[base + layer, part, :] = factor
                source = ref[0, layer, part, :]
                rhs_w[base + layer, part, :] = source
                s1[base + layer, pl.ds(row + 8, CHUNK), :] = factor * source
                pair = pair + density
            put_halves(work, base >> 1, part, pair)

        chunks(height, begin)

    stores = [
        pltpu.make_async_copy(rhs_w.at[1], halo_out.at[0], sems.at[1]),
        pltpu.make_async_copy(rhs_w.at[4], halo_out.at[1], sems.at[2]),
        pltpu.make_async_copy(dens_b.at[1 - core], halo_out.at[2 + core], sems.at[3]),
        pltpu.make_async_copy(dens_a.at[core], halo_out.at[3 - core], sems.at[4]),
    ]
    start_all(stores)

    for j in range(1, 5):

        def smooth(row, j=j):
            part = pl.ds(row, CHUNK)
            v = s1[j, pl.ds(row + 8, CHUNK), :]
            f = stencil(s1, j, row, CHUNK)
            new = (1.0 - WEIGHT) * v + wd[j, part, :] * (rhs_w[j, part, :] + 2.0 * scale * (f - v))
            s2[j - 1, pl.ds(row + 8, CHUNK), :] = new
            s2_out[j - 1, part, :] = new

        chunks(height, smooth)
    mine = 1 + core
    send_a[2 * half : 4 * half, :] = s2_out[mine, :, :half]
    send_a[4 * half : 6 * half, :] = s2_out[mine, :, half:]
    send_b[0] = s2_out[2 - core]

    def restrict(row):
        part = pl.ds(row, CHUNK)
        total = jnp.zeros((CHUNK, width), f32)
        for layer in range(2):
            v = s2[1 + layer, pl.ds(row + 8, CHUNK), :]
            f = stencil(s2, 1 + layer, row, CHUNK)
            center = dens[layer, part, :] + 16.0 * scale
            total = total + (rhs_w[2 + layer, part, :] - center * v + 2.0 * scale * f)
        put_halves(work, 3, part, total)

    chunks(height, restrict)
    columns = coarsen_z(height, width)
    density1 = [0.125 * dot_exact(pair_rows(work, i, half), columns) for i in range(3)]
    coarse_res = 0.125 * dot_exact(pair_rows(work, 3, half), columns)

    send_a[0:half, :] = coarse_res
    send_a[half : 2 * half, :] = density1[1]

    first = 0.85 * coarse_res / (density1[1] + 14.0 * scale1)
    pad = jnp.zeros((8, half), f32)
    spread = filter_yz(jnp.concatenate([pad, first, pad], 0))
    own_factor = WEIGHT / (density1[1] + 14.0 * scale1)
    shares = [
        (WEIGHT * valid_lo) * scale1 / (density1[0] + 14.0 * scale1) * spread,
        (1.0 - WEIGHT) * first + own_factor * (coarse_res + 2.0 * scale1 * (spread - first)),
        (WEIGHT * valid_hi) * scale1 / (density1[2] + 14.0 * scale1) * spread,
    ]
    block = half // TILES
    filtered = []
    plain = []
    for e, share in enumerate(shares):
        rest = -(density1[e] + 16.0 * scale1) * share
        if e == 1:
            rest = rest + coarse_res
        for t in range(TILES):
            at = t * block
            row = 2.0 * jnp.sum(share[at : at + block], axis=0, keepdims=True)
            row = row - 0.5 * (share[at : at + 1] + share[at + block - 1 : at + block])
            if t > 0:
                row = row + 0.5 * share[at - 1 : at]
            if t < TILES - 1:
                row = row + 0.5 * share[at + block : at + block + 1]
            filtered.append(row)
            plain.append(jnp.sum(rest[at : at + block], axis=0, keepdims=True))
    for t in range(TILES):
        plain.append(jnp.sum(density1[1][t * block : (t + 1) * block], axis=0, keepdims=True))
    filtered.append(jnp.zeros((4, half), f32))
    filtered = jnp.concatenate(filtered, 0)
    plain = jnp.concatenate(plain, 0)
    cell = iota((half, 128), 0)
    tile = iota((half, 128), 1) & 3
    start = tile * block
    inside = ((cell >= start) & (cell < start + block)).astype(f32)
    ends = ((cell == start) | (cell == start + block - 1)).astype(f32)
    beside = ((cell == start - 1) | (cell == start + block)).astype(f32)
    plain_w = inside.astype(bf16)
    filter_w = (2.0 * inside - 0.5 * ends + 0.5 * beside).astype(bf16)
    row = iota((16, 128), 0)
    lane = iota((16, 128), 1)
    fits = ((lane >> 2) & 3) == (row & 3)
    out = jnp.where(fits & ((lane >> 4) == (row >> 2)), dot_exact(filtered, filter_w), 0.0)
    out = jnp.where(row >= 12, 0.0, out)
    out = out + jnp.where(fits & ((lane >> 4) == (row >> 2) + 3), dot_exact(plain, plain_w), 0.0)
    payload[...] = jnp.broadcast_to(jnp.sum(out, axis=0, keepdims=True)[None], payload.shape)
    wait_all(stores)


def lanes_sum(x):
    for step in (16, 32, 64):
        x = x + pltpu.roll(x, step, 1)
    return x


def row_before(x):
    return jnp.where(iota(x.shape, 0) == 0, 0.0, pltpu.roll(x, 1, 0))


def row_after(x):
    return jnp.where(iota(x.shape, 0) == x.shape[0] - 1, 0.0, pltpu.roll(x, x.shape[0] - 1, 0))


def solve_groups(gathered, groups, scale1, block):
    bricks = gathered.shape[0]
    lane = iota(gathered.shape, 1)
    slot = lane >> 4
    up = pltpu.roll(gathered, bricks - 1, 0)
    down = pltpu.roll(gathered, 1, 0)

    def pick(first):
        return lanes_sum(
            jnp.where(
                slot == first,
                up,
                jnp.where(slot == first + 1, gathered, jnp.where(slot == first + 2, down, 0.0)),
            )
        )

    filtered = pick(0)
    plain = pick(3)
    density_sum = lanes_sum(jnp.where(slot == 6, gathered, 0.0))
    remainder = plain + 2.0 * scale1 * filtered + scale1 * (row_before(filtered) + row_after(filtered))

    blocks = groups.shape[1]
    repeat = (iota((blocks, 128), 0) == (iota((blocks, 128), 1) & (blocks - 1))).astype(bf16)
    ids = jnp.dot(groups.astype(f32).astype(bf16), repeat, preferred_element_type=f32)
    diagonal_lane = (iota(gathered.shape, 0) & 7) == slot
    packed = jnp.where(diagonal_lane, ids, 0.0)
    member = [
        (ids == jnp.sum(packed[8 * j : 8 * j + 8], axis=0, keepdims=True)).astype(f32) for j in range(bricks // 8)
    ]

    def project(x):
        chosen = jnp.where(diagonal_lane, x, 0.0)
        total = jnp.zeros_like(x)
        for j in range(bricks // 8):
            total = total + member[j] * jnp.sum(chosen[8 * j : 8 * j + 8], axis=0, keepdims=True)
        return lanes_sum(total)

    place = iota(ids.shape, 0)
    as_before = jnp.where((place > 0) & (pltpu.roll(ids, 1, 0) == ids), 0.5, 0.0)
    as_after = jnp.where((place < bricks - 1) & (pltpu.roll(ids, bricks - 1, 0) == ids), 0.5, 0.0)
    inner = 2.0 * block - 1.0
    same = inner * inner * (1.0 + as_before + as_after)
    cells = float(block * block)
    diagonal = project(density_sum + scale1 * (16.0 * cells - 2.0 * same))
    group_rhs = project(remainder)
    column = lane & 3
    line = (lane >> 2) & 3
    center = density_sum + 16.0 * cells * scale1

    def image(g):
        z = inner * g + 0.5 * (
            jnp.where(column > 0, pltpu.roll(g, 1, 1), 0.0) + jnp.where(column < 3, pltpu.roll(g, 127, 1), 0.0)
        )
        y = inner * z + 0.5 * (
            jnp.where(line > 0, pltpu.roll(z, 4, 1), 0.0) + jnp.where(line < 3, pltpu.roll(z, 124, 1), 0.0)
        )
        return center * g - 2.0 * scale1 * (y + 0.5 * (row_before(y) + row_after(y)))

    factor = COARSE_WEIGHT / diagonal
    fix = factor * group_rhs
    for _ in range(COARSE_SWEEPS - 1):
        fix = fix + factor * (group_rhs - project(image(fix)))
    return fix


def second_kernel(
    kappa_in, halo_in, rhs, dens, s2, near_f, send_a, sib, near, far, sib_near, sib_far, gathered, groups,
    to_a, to_b,
    fixes, cres, cden, c1, c2, c3, grown, s3, s4, wd, halo, last, kappa, sems,
):
    core, brick, bricks = position()
    load = pltpu.make_async_copy(kappa_in, kappa, sems.at[0])
    load.start()
    load_halo = pltpu.make_async_copy(halo_in, halo, sems.at[1])
    load_halo.start()
    half = cres.shape[1]
    height, width = rhs.shape[2:]
    block = half // TILES
    inner = pl.ds(8, height)
    for ref in (c1, c2, c3, s3, s4):
        clear_edges(ref)
    load.wait()
    scale = kappa[0]
    scale1 = 0.25 * scale

    fixes[0:8, :] = jnp.zeros((8, 128), f32)
    count = gathered.shape[0]
    fixes[8 + count : 32 + count, :] = jnp.zeros((24, 128), f32)
    fixes[8 : 8 + count, :] = solve_groups(gathered[:, 0, :], groups[...], scale1, block)
    window = fixes[pl.ds(brick + 4, 16), :]
    lane = iota((128, TILES * half), 1)
    per = (lane >> (half.bit_length() - 1)) * 4 + ((lane & (half - 1)) >> (block.bit_length() - 1))
    spread = dot_exact(window, (iota((128, TILES * half), 0) == per).astype(bf16))

    sign = 2 * core - 1
    for ref, first, at in (
        (send_a, 0, 0), (sib, 0, -1),
        (near, 0, 1), (near, 2, 2), (far, 0, 3), (far, 2, 4),
        (sib_near, 0, -2), (sib_near, 2, -3), (sib_far, 0, -4),
    ):
        index = 4 + sign * at
        cres[index] = ref[first * half : (first + 1) * half, :]
        cden[index] = ref[(first + 1) * half : (first + 2) * half, :]

    body = pl.ds(8, half)
    factors = []
    for i in range(9):
        place = brick + (i - 4)
        valid = ((place >= 0) & (place < bricks)).astype(f32)
        factor = (WEIGHT * valid) / (cden[i] + 14.0 * scale1)
        cden[i] = factor
        c1[i, body, :] = factor * cres[i]

    def relax(ref, i, k):
        v = ref[i, body, :]
        f = stencil(ref, i, 0, half)
        return (1.0 - WEIGHT) * v + cden[k] * (cres[k] + 2.0 * scale1 * (f - v))

    for i in range(7):
        value = relax(c1, i + 1, i + 1)
        pieces = [
            jnp.broadcast_to(spread[i + 1 : i + 2, t * half : (t + 1) * half], (block, half)) for t in range(TILES)
        ]
        c2[i, body, :] = value + jnp.concatenate(pieces, 0)
    for i in range(5):
        c3[i, body, :] = relax(c2, i + 1, i + 2)
    columns = (iota((half, width), 0) == (iota((half, width), 1) >> 1)).astype(bf16)
    for i in range(3):
        fine = dot_exact(relax(c3, i + 1, i + 3), columns)
        put_halves(grown, i, pl.ds(0, half, stride=2), fine)
        put_halves(grown, i, pl.ds(1, half, stride=2), fine)

    load_halo.wait()
    for k in range(2):
        side = slice(k * half, (k + 1) * half)
        for i in range(4):
            s3[i + 1, inner, side] = s2[i, :, side] + grown[(i + 1) >> 1, k]
        s3[5 * core, inner, side] = near_f[0, :, side] + grown[2 * core, k]
        s3[5 * (1 - core), inner, side] = sib[2 * (k + 1) * half : 2 * (k + 2) * half, :] + grown[2 * (1 - core), k]

    for j in range(4):

        def smooth(row, j=j):
            part = pl.ds(row, CHUNK)
            v = s3[j + 1, pl.ds(row + 8, CHUNK), :]
            f = stencil(s3, j + 1, row, CHUNK)
            if j in (1, 2):
                source, density, top = rhs[0, j - 1, part, :], dens[j - 1, part, :], WEIGHT
            else:
                edge = j // 3
                source, density = halo[edge, part, :], halo[2 + edge, part, :]
                top = WEIGHT * (brick < bricks - 1 if edge else brick > 0).astype(f32)
            factor = top / (density + 14.0 * scale)
            wd[j, part, :] = factor
            new = (1.0 - WEIGHT) * v + factor * (source + 2.0 * scale * (f - v))
            s4[j, pl.ds(row + 8, CHUNK), :] = new

        chunks(height, smooth)
    for j in range(2):

        def smooth_last(row, j=j):
            part = pl.ds(row, CHUNK)
            v = s4[j + 1, pl.ds(row + 8, CHUNK), :]
            f = stencil(s4, j + 1, row, CHUNK)
            new = (1.0 - WEIGHT) * v + wd[j + 1, part, :] * (rhs[0, j, part, :] + 2.0 * scale * (f - v))
            last[j, part, :] = new

        chunks(height, smooth_last)
    to_a[0] = last[1 - core]
    to_b[0] = last[core]


def inside_kernel(kappa_in, rhs, dens, to_a, to_b, sol_out, out, s, kappa, sems):
    core = position()[0]
    load = pltpu.make_async_copy(kappa_in, kappa, sems.at[0])
    stores = [
        pltpu.make_async_copy(to_b.at[0], sol_out.at[0, core], sems.at[1]),
        pltpu.make_async_copy(to_a.at[0], sol_out.at[0, 1 - core], sems.at[2]),
    ]
    load.start()
    start_all(stores)
    height = dens.shape[1]
    inner = pl.ds(8, height)
    clear_edges(s)
    s[core, inner, :] = to_b[0]
    s[1 - core, inner, :] = to_a[0]
    load.wait()
    scale = kappa[0]
    for j in range(2):

        def finish(row, j=j):
            part = pl.ds(row, CHUNK)
            more = pl.ds(row, CHUNK + 16)
            f = filter_yz(s[j, more, :] + 0.5 * s[1 - j, more, :])
            center = dens[j, part, :] + 16.0 * scale
            out[j, part, :] = rhs[0, j, part, :] - center * s[j, pl.ds(row + 8, CHUNK), :] + 2.0 * scale * f

        chunks(height, finish)
    wait_all(stores)


def residual_kernel(kappa_in, inside, halo_a, halo_b, out, s, done, kappa, sems):
    core = position()[0]
    load = pltpu.make_async_copy(kappa_in, kappa, sems.at[0])
    load.start()
    height = inside.shape[1]
    inner = pl.ds(8, height)
    clear_edges(s)
    s[core, inner, :] = halo_b[0]
    s[1 - core, inner, :] = halo_a[0]
    load.wait()
    scale = kappa[0]
    stores = []
    for j in range(2):

        def finish(row, j=j):
            part = pl.ds(row, CHUNK)
            done[j, part, :] = inside[j, part, :] + scale * filter_yz(s[j, pl.ds(row, CHUNK + 16), :])

        chunks(height, finish)
        stores.append(pltpu.make_async_copy(done.at[j], out.at[0, j], sems.at[1 + j]))
        stores[-1].start()
    wait_all(stores)


def shape(*dims):
    return jax.ShapeDtypeStruct(dims, f32)


def local(rhs, density, kappa, block_group):
    bricks = lax.axis_size("brick")
    species = lax.axis_size("spec")
    height, width = rhs.shape[2:]
    half = height // 2
    in_chip = [(i, i ^ 1) for i in range(bricks)]
    next_chip = [(i, ((i + 1) ^ 1) - 1) for i in range(1, bricks - 1)]
    second_chip = [(i, i - 3) for i in range(4, bricks, 2)] + [(i, i + 3) for i in range(1, bricks - 3, 2)]

    def swap_a(x):
        return lax.ppermute(x, "brick", in_chip)

    def swap_b(x):
        return lax.ppermute(x, "brick", next_chip)

    def swap_far(x):
        return lax.ppermute(x, "brick", second_chip)

    def around(x, k):
        return lax.ppermute(x, "spec", [(i, (i + k) % species) for i in range(species)])

    pieces = [around(density, k) for k in (1, 2, 3)]
    rhs_b = swap_b(rhs)
    rhs_a = swap_a(rhs)
    dens = pl.pallas_call(
        gather_kernel,
        out_shape=shape(2, height, width),
        in_specs=[HBM] + [ANY] * 3,
        out_specs=VM,
        scratch_shapes=[pltpu.SemaphoreType.DMA((4,))],
        compiler_params=PARAMS,
        name="collect_density",
    )(pltpu.with_memory_space_constraint(density, pltpu.HBM), *pieces)

    dens_b = swap_b(dens)
    dens_a = swap_a(dens)
    s2, halo, send_a, send_b, payload = pl.pallas_call(
        first_kernel,
        out_shape=(
            shape(4, height, width),
            pltpu.HBM((4, height, width), f32),
            shape(6 * half, half),
            shape(1, height, width),
            shape(bricks, 8, 128),
        ),
        in_specs=[ANY] + [VM] * 6,
        out_specs=[VM, HBM, VM, VM, VM],
        scratch_shapes=[
            pltpu.VMEM((6, height + 16, width), f32),
            pltpu.VMEM((4, height + 16, width), f32),
            pltpu.VMEM((6, height, width), f32),
            pltpu.VMEM((6, height, width), f32),
            pltpu.VMEM((4, 2, height, half), f32),
            pltpu.SMEM((1,), f32),
            pltpu.SemaphoreType.DMA((5,)),
        ],
        compiler_params=PARAMS,
        name="smooth_and_restrict",
    )(kappa, rhs, dens, rhs_a, dens_a, rhs_b, dens_b)

    gathered = lax.all_to_all(payload, "brick", 0, 0, tiled=True)
    sib = swap_a(send_a)
    near_f = swap_b(send_b)
    both = pl.pallas_call(
        join_kernel,
        out_shape=shape(4 * half, half),
        in_specs=[ANY] * 2,
        out_specs=VM,
        scratch_shapes=[pltpu.SemaphoreType.DMA((2,))],
        compiler_params=PARAMS,
        name="join_chip",
    )(send_a, sib)
    near = swap_b(both)
    far = swap_far(both)
    near, far, gathered = lax.optimization_barrier((near, far, gathered))
    sib_near = swap_a(near)
    sib_far = swap_a(far)

    to_a, to_b = pl.pallas_call(
        second_kernel,
        out_shape=(shape(1, height, width), shape(1, height, width)),
        in_specs=[ANY, HBM] + [VM] * 12,
        out_specs=[VM] * 2,
        scratch_shapes=[
            pltpu.VMEM((bricks + 32, 128), f32),
            pltpu.VMEM((9, half, half), f32),
            pltpu.VMEM((9, half, half), f32),
            pltpu.VMEM((9, half + 16, half), f32),
            pltpu.VMEM((7, half + 16, half), f32),
            pltpu.VMEM((5, half + 16, half), f32),
            pltpu.VMEM((3, 2, height, half), f32),
            pltpu.VMEM((6, height + 16, width), f32),
            pltpu.VMEM((4, height + 16, width), f32),
            pltpu.VMEM((4, height, width), f32),
            pltpu.VMEM((4, height, width), f32),
            pltpu.VMEM((2, height, width), f32),
            pltpu.SMEM((1,), f32),
            pltpu.SemaphoreType.DMA((2,)),
        ],
        compiler_params=PARAMS,
        name="correct_and_smooth",
    )(
        kappa, pltpu.with_memory_space_constraint(halo, pltpu.HBM), rhs, dens, s2, near_f, send_a, sib, near, far, sib_near, sib_far, gathered, block_group
    )

    halo_b = swap_b(to_b)
    halo_a = swap_a(to_a)
    solution, inside = pl.pallas_call(
        inside_kernel,
        out_shape=(shape(1, 2, height, width), shape(2, height, width)),
        in_specs=[ANY] + [VM] * 4,
        out_specs=[ANY, VM],
        scratch_shapes=[
            pltpu.VMEM((2, height + 16, width), f32),
            pltpu.SMEM((1,), f32),
            pltpu.SemaphoreType.DMA((3,)),
        ],
        compiler_params=PARAMS,
        name="residual_inside",
    )(kappa, rhs, dens, to_a, to_b)
    residual = pl.pallas_call(
        residual_kernel,
        out_shape=shape(1, 2, height, width),
        in_specs=[ANY] + [VM] * 3,
        out_specs=ANY,
        scratch_shapes=[
            pltpu.VMEM((2, height + 16, width), f32),
            pltpu.VMEM((2, height, width), f32),
            pltpu.SMEM((1,), f32),
            pltpu.SemaphoreType.DMA((3,)),
        ],
        compiler_params=PARAMS,
        name="residual",
    )(kappa, inside, halo_a, halo_b)
    return (solution, residual)


def solution(mesh):
    return jax.shard_map(
        local,
        mesh=mesh,
        in_specs=(P("spec", "brick", None, None), P("brick", "spec", None), P("spec"), P()),
        out_specs=(P("spec", "brick", None, None), P("spec", "brick", None, None)),
        check_vma=False,
    )
```

```python
import functools

import jax
import jax.numpy as jnp
from jax import lax
from jax.experimental import pallas as pl
from jax.experimental.pallas import tpu as pltpu
from jax.sharding import PartitionSpec as P

WEIGHT = 0.85
COARSE_WEIGHT = 0.6
COARSE_SWEEPS = 3
TILES = 4
CHUNK = 64
f32 = jnp.float32
bf16 = jnp.bfloat16
VM = pl.BlockSpec(memory_space=pltpu.VMEM)
ANY = pl.BlockSpec(memory_space=pl.ANY)
HBM = pl.BlockSpec(memory_space=pltpu.HBM)
PARAMS = pltpu.CompilerParams(vmem_limit_bytes=16 * 1024 * 1024)


def iota(shape, dim):
    return lax.broadcasted_iota(jnp.int32, shape, dim)


def split(x):
    high = x.astype(bf16)
    rest = x - high.astype(f32)
    middle = rest.astype(bf16)
    low = (rest - middle.astype(f32)).astype(bf16)
    return high, middle, low


def dot_exact(x, w):
    high, middle, low = split(x)
    dot = functools.partial(jnp.dot, preferred_element_type=f32)
    return dot(high, w) + (dot(middle, w) + dot(low, w))


def filter_z(y):
    width = y.shape[1]
    lane = iota((1, width), 1)
    before = jnp.where(lane == 0, 0.0, 0.5)
    after = jnp.where(lane == width - 1, 0.0, 0.5)
    return y + before * pltpu.roll(y, 1, 1) + after * pltpu.roll(y, width - 1, 1)


def filter_yz(m):
    rows = m.shape[0]
    y = m + 0.5 * (pltpu.roll(m, 1, 0) + pltpu.roll(m, rows - 1, 0))
    return filter_z(y[8 : rows - 8])


def stencil(ref, i, row, rows):
    part = pl.ds(row, rows + 16)
    return filter_yz(ref[i, part, :] + 0.5 * (ref[i - 1, part, :] + ref[i + 1, part, :]))


def clear_edges(ref):
    layers, rows, width = ref.shape
    zero = jnp.zeros((layers, 8, width), f32)
    ref[:, 0:8, :] = zero
    ref[:, rows - 8 : rows, :] = zero


def chunks(rows, body):
    for row in range(0, rows, CHUNK):
        body(row)


def coarsen_z(rows, width):
    return ((iota((width, width // 2), 0) >> 1) == iota((width, width // 2), 1)).astype(bf16)


def put_halves(ref, i, part, x):
    half = x.shape[1] // 2
    ref[i, 0, part, :] = x[:, :half]
    ref[i, 1, part, :] = x[:, half:]


def pair_rows(ref, i, half):
    even, odd = pl.ds(0, half, stride=2), pl.ds(1, half, stride=2)
    return jnp.concatenate([ref[i, k, even, :] + ref[i, k, odd, :] for k in range(2)], 1)


def position():
    brick = lax.axis_index("brick")
    return brick & 1, brick, lax.axis_size("brick")


def start_all(copies):
    for copy in copies:
        copy.start()


def wait_all(copies):
    for copy in copies:
        copy.wait()


def join_kernel(mine, other, density1_sib, density1_own, near_f, near, far, sems):
    del near_f
    half = far.shape[0] // 3
    parts = [pl.ds(i * half, half) for i in range(4)]
    copies = [
        pltpu.make_async_copy(mine.at[parts[0]], near.at[parts[0]], sems.at[0]),
        pltpu.make_async_copy(density1_own, near.at[parts[1]], sems.at[1]),
        pltpu.make_async_copy(other.at[parts[0]], near.at[parts[2]], sems.at[2]),
        pltpu.make_async_copy(density1_sib, near.at[parts[3]], sems.at[3]),
        pltpu.make_async_copy(mine.at[parts[0]], far.at[parts[0]], sems.at[4]),
        pltpu.make_async_copy(density1_own, far.at[parts[1]], sems.at[5]),
        pltpu.make_async_copy(other.at[parts[1]], far.at[parts[2]], sems.at[6]),
    ]
    start_all(copies)
    wait_all(copies)


def gather_kernel(shard, p1, p2, p3, dens, sems):
    count = 4
    rows = shard.shape[1]
    copies = []
    for k, piece in enumerate((shard, p1, p2, p3)):
        owner = lax.rem(lax.axis_index("spec") - k + count, count)
        place = pl.ds(pl.multiple_of(owner * rows, rows), rows)
        copies.append(pltpu.make_async_copy(piece, dens.at[:, place, :], sems.at[k]))
    start_all(copies)
    wait_all(copies)


def begin_layers(source, density, layers, work, index, wd, s1, scale, top, keep):
    height = density.shape[1]

    def begin(row):
        part = pl.ds(row, CHUNK)
        pair = density[0, part, :] + density[1, part, :]
        put_halves(work, index, part, pair)
        for layer, slot in layers:
            factor = top / (density[layer, part, :] + 14.0 * scale)
            if slot in keep:
                wd[keep[slot], part, :] = factor
            s1[slot, pl.ds(row + 8, CHUNK), :] = factor * source[0, layer, part, :]

    chunks(height, begin)


def near_kernel(
    kappa_in, rhs, dens, rhs_a, dens_a, rhs_b,
    s1_own, s2_hi, wd_own, halo_out, density1_own, density1_sib, send_b,
    s1, wd, work, kappa, sems,
):
    del rhs_b
    core, brick, bricks = position()
    load = pltpu.make_async_copy(kappa_in, kappa, sems.at[0])
    stores = [
        pltpu.make_async_copy(rhs_a.at[0, core], halo_out.at[0], sems.at[1]),
        pltpu.make_async_copy(dens_a.at[core], halo_out.at[1], sems.at[2]),
    ]
    load.start()
    start_all(stores)
    height, width = dens.shape[1:]
    half = height // 2
    clear_edges(s1)
    clear_edges(s2_hi)
    load.wait()
    scale = kappa[0]
    valid = jnp.where(core == 0, brick < bricks - 1, brick > 0).astype(f32)
    begin_layers(rhs, dens, ((core, 0), (1 - core, 1)), work, 0, wd, s1, scale, WEIGHT, {0: 0, 1: 1})
    begin_layers(rhs_a, dens_a, ((core, 2), (1 - core, 3)), work, 1, wd, s1, scale, WEIGHT * valid, {2: 2})
    for j in (1, 2):

        def smooth(row, j=j):
            part = pl.ds(row, CHUNK)
            v = s1[j, pl.ds(row + 8, CHUNK), :]
            f = stencil(s1, j, row, CHUNK)
            source = rhs[0, 1 - core, part, :] if j == 1 else rhs_a[0, core, part, :]
            new = (1.0 - WEIGHT) * v + wd[j, part, :] * (source + 2.0 * scale * (f - v))
            s2_hi[j - 1, pl.ds(row + 8, CHUNK), :] = new
            if j == 1:
                send_b[0, part, :] = new

        chunks(height, smooth)
    s1_own[...] = s1[0:2]
    wd_own[...] = wd[0]
    columns = coarsen_z(height, width)
    density1_own[...] = 0.125 * dot_exact(pair_rows(work, 0, half), columns)
    density1_sib[...] = 0.125 * dot_exact(pair_rows(work, 1, half), columns)
    wait_all(stores)


def first_kernel(
    kappa_in, rhs, dens, rhs_b, dens_b, s1_own, s2_hi, wd_own, density1_own, density1_sib,
    s2_lo, halo_out, send_a, send_f, payload,
    s1, s2, wd, work, kappa, sems,
):
    core, brick, bricks = position()
    load = pltpu.make_async_copy(kappa_in, kappa, sems.at[0])
    stores = [
        pltpu.make_async_copy(rhs_b.at[0, 1 - core], halo_out.at[0], sems.at[1]),
        pltpu.make_async_copy(dens_b.at[1 - core], halo_out.at[1], sems.at[2]),
    ]
    load.start()
    start_all(stores)
    height, width = dens.shape[1:]
    half = height // 2
    clear_edges(s1)
    clear_edges(s2)
    s1[2:4] = s1_own[...]
    s2[2:4] = s2_hi[...]
    load.wait()
    scale = kappa[0]
    scale1 = 0.25 * scale
    valid_lo = jnp.where(core == 0, brick > 0, brick < bricks - 1).astype(f32)
    valid_hi = jnp.where(core == 0, brick < bricks - 1, brick > 0).astype(f32)
    begin_layers(rhs_b, dens_b, ((core, 0), (1 - core, 1)), work, 0, wd, s1, scale, WEIGHT * valid_lo, {1: 0})

    for j in (1, 2):

        def smooth(row, j=j):
            part = pl.ds(row, CHUNK)
            v = s1[j, pl.ds(row + 8, CHUNK), :]
            f = stencil(s1, j, row, CHUNK)
            source, factor = (rhs_b[0, 1 - core, part, :], wd[0, part, :]) if j == 1 else (rhs[0, core, part, :], wd_own[part, :])
            new = (1.0 - WEIGHT) * v + factor * (source + 2.0 * scale * (f - v))
            s2[j - 1, pl.ds(row + 8, CHUNK), :] = new
            s2_lo[j - 1, part, :] = new

        chunks(height, smooth)

    def restrict(row):
        part = pl.ds(row, CHUNK)
        total = jnp.zeros((CHUNK, width), f32)
        for slot, layer in ((1, core), (2, 1 - core)):
            v = s2[slot, pl.ds(row + 8, CHUNK), :]
            f = stencil(s2, slot, row, CHUNK)
            center = dens[layer, part, :] + 16.0 * scale
            total = total + (rhs[0, layer, part, :] - center * v + 2.0 * scale * f)
        put_halves(work, 1, part, total)

    chunks(height, restrict)
    columns = coarsen_z(height, width)
    density1 = [0.125 * dot_exact(pair_rows(work, 0, half), columns), density1_own[...], density1_sib[...]]
    coarse_res = 0.125 * dot_exact(pair_rows(work, 1, half), columns)

    send_a[0:half, :] = coarse_res
    send_f[0] = s2_lo[1]

    first = WEIGHT * coarse_res / (density1[1] + 14.0 * scale1)
    send_a[half : 2 * half, :] = first
    pad = jnp.zeros((8, half), f32)
    spread = filter_yz(jnp.concatenate([pad, first, pad], 0))
    own_factor = WEIGHT / (density1[1] + 14.0 * scale1)
    shares = [
        (WEIGHT * valid_lo) * scale1 / (density1[0] + 14.0 * scale1) * spread,
        (1.0 - WEIGHT) * first + own_factor * (coarse_res + 2.0 * scale1 * (spread - first)),
        (WEIGHT * valid_hi) * scale1 / (density1[2] + 14.0 * scale1) * spread,
    ]
    block = half // TILES
    filtered = []
    plain = []
    for e, share in enumerate(shares):
        rest = -(density1[e] + 16.0 * scale1) * share
        if e == 1:
            rest = rest + coarse_res
        for t in range(TILES):
            at = t * block
            row = 2.0 * jnp.sum(share[at : at + block], axis=0, keepdims=True)
            row = row - 0.5 * (share[at : at + 1] + share[at + block - 1 : at + block])
            if t > 0:
                row = row + 0.5 * share[at - 1 : at]
            if t < TILES - 1:
                row = row + 0.5 * share[at + block : at + block + 1]
            filtered.append(row)
            plain.append(jnp.sum(rest[at : at + block], axis=0, keepdims=True))
    for t in range(TILES):
        plain.append(jnp.sum(density1[1][t * block : (t + 1) * block], axis=0, keepdims=True))
    for rows in (filtered, plain):
        for t in range(TILES):
            low, high = rows[t], rows[2 * TILES + t]
            rows[t] = jnp.where(core == 0, low, high)
            rows[2 * TILES + t] = jnp.where(core == 0, high, low)
    filtered.append(jnp.zeros((4, half), f32))
    filtered = jnp.concatenate(filtered, 0)
    plain = jnp.concatenate(plain, 0)
    cell = iota((half, 128), 0)
    tile = iota((half, 128), 1) & 3
    start = tile * block
    inside = ((cell >= start) & (cell < start + block)).astype(f32)
    ends = ((cell == start) | (cell == start + block - 1)).astype(f32)
    beside = ((cell == start - 1) | (cell == start + block)).astype(f32)
    plain_w = inside.astype(bf16)
    filter_w = (2.0 * inside - 0.5 * ends + 0.5 * beside).astype(bf16)
    row = iota((16, 128), 0)
    lane = iota((16, 128), 1)
    fits = ((lane >> 2) & 3) == (row & 3)
    out = jnp.where(fits & ((lane >> 4) == (row >> 2)), dot_exact(filtered, filter_w), 0.0)
    out = jnp.where(row >= 12, 0.0, out)
    out = out + jnp.where(fits & ((lane >> 4) == (row >> 2) + 3), dot_exact(plain, plain_w), 0.0)
    payload[...] = jnp.broadcast_to(jnp.sum(out, axis=0, keepdims=True)[None], payload.shape)
    wait_all(stores)


def lanes_sum(x):
    for step in (16, 32, 64):
        x = x + pltpu.roll(x, step, 1)
    return x


def row_before(x):
    return jnp.where(iota(x.shape, 0) == 0, 0.0, pltpu.roll(x, 1, 0))


def row_after(x):
    return jnp.where(iota(x.shape, 0) == x.shape[0] - 1, 0.0, pltpu.roll(x, x.shape[0] - 1, 0))


def solve_groups(gathered, groups, scale1, block):
    bricks = gathered.shape[0]
    lane = iota(gathered.shape, 1)
    slot = lane >> 4
    up = pltpu.roll(gathered, bricks - 1, 0)
    down = pltpu.roll(gathered, 1, 0)

    def pick(first):
        return lanes_sum(
            jnp.where(
                slot == first,
                up,
                jnp.where(slot == first + 1, gathered, jnp.where(slot == first + 2, down, 0.0)),
            )
        )

    filtered = pick(0)
    plain = pick(3)
    density_sum = lanes_sum(jnp.where(slot == 6, gathered, 0.0))
    remainder = plain + 2.0 * scale1 * filtered + scale1 * (row_before(filtered) + row_after(filtered))

    blocks = groups.shape[1]
    repeat = (iota((blocks, 128), 0) == (iota((blocks, 128), 1) & (blocks - 1))).astype(bf16)
    ids = jnp.dot(groups.astype(f32).astype(bf16), repeat, preferred_element_type=f32)
    diagonal_lane = (iota(gathered.shape, 0) & 7) == slot
    packed = jnp.where(diagonal_lane, ids, 0.0)
    member = [
        (ids == jnp.sum(packed[8 * j : 8 * j + 8], axis=0, keepdims=True)).astype(f32) for j in range(bricks // 8)
    ]

    def project(x):
        chosen = jnp.where(diagonal_lane, x, 0.0)
        total = jnp.zeros_like(x)
        for j in range(bricks // 8):
            total = total + member[j] * jnp.sum(chosen[8 * j : 8 * j + 8], axis=0, keepdims=True)
        return lanes_sum(total)

    place = iota(ids.shape, 0)
    as_before = jnp.where((place > 0) & (pltpu.roll(ids, 1, 0) == ids), 0.5, 0.0)
    as_after = jnp.where((place < bricks - 1) & (pltpu.roll(ids, bricks - 1, 0) == ids), 0.5, 0.0)
    inner = 2.0 * block - 1.0
    same = inner * inner * (1.0 + as_before + as_after)
    cells = float(block * block)
    diagonal = project(density_sum + scale1 * (16.0 * cells - 2.0 * same))
    group_rhs = project(remainder)
    column = lane & 3
    line = (lane >> 2) & 3
    center = density_sum + 16.0 * cells * scale1

    def image(g):
        z = inner * g + 0.5 * (
            jnp.where(column > 0, pltpu.roll(g, 1, 1), 0.0) + jnp.where(column < 3, pltpu.roll(g, 127, 1), 0.0)
        )
        y = inner * z + 0.5 * (
            jnp.where(line > 0, pltpu.roll(z, 4, 1), 0.0) + jnp.where(line < 3, pltpu.roll(z, 124, 1), 0.0)
        )
        return center * g - 2.0 * scale1 * (y + 0.5 * (row_before(y) + row_after(y)))

    factor = COARSE_WEIGHT / diagonal
    fix = factor * group_rhs
    for _ in range(COARSE_SWEEPS - 1):
        fix = fix + factor * (group_rhs - project(image(fix)))
    return fix


def second_kernel(
    kappa_in, halo_lo_in, halo_hi_in, rhs, dens, s2_lo, s2_hi, near_f, sib_f, density1_sib, density1_own, send_a, sib, near, far, sib_near, sib_far, gathered, groups,
    to_a, to_b,
    fixes, cres, cden, c1, c2, c3, grown, s3, s4, wd, halo, kappa, sems,
):
    core, brick, bricks = position()
    load = pltpu.make_async_copy(kappa_in, kappa, sems.at[0])
    load.start()
    loads = [
        pltpu.make_async_copy(halo_lo_in, halo.at[pl.ds(0, 2)], sems.at[1]),
        pltpu.make_async_copy(halo_hi_in, halo.at[pl.ds(2, 2)], sems.at[2]),
    ]
    start_all(loads)
    half = cres.shape[1]
    height, width = rhs.shape[2:]
    block = half // TILES
    for ref in (c1, c2, c3, s3, s4):
        clear_edges(ref)
    load.wait()
    scale = kappa[0]
    scale1 = 0.25 * scale

    fixes[0:8, :] = jnp.zeros((8, 128), f32)
    count = gathered.shape[0]
    fixes[8 + count : 32 + count, :] = jnp.zeros((24, 128), f32)
    fixes[8 : 8 + count, :] = solve_groups(gathered[:, 0, :], groups[...], scale1, block)
    window = fixes[pl.ds(brick + 4, 16), :]
    lane = iota((128, TILES * half), 1)
    per = (lane >> (half.bit_length() - 1)) * 4 + ((lane & (half - 1)) >> (block.bit_length() - 1))
    spread = dot_exact(window, (iota((128, TILES * half), 0) == per).astype(bf16))

    for index, (ref, i), (ref_density, k) in (
        (1, (far, 0), (far, 1)),
        (2, (near, 2), (near, 3)),
        (3, (near, 0), (near, 1)),
        (4, (send_a, 0), (density1_own, 0)),
        (5, (sib, 0), (density1_sib, 0)),
        (6, (sib_near, 0), (sib_near, 1)),
        (7, (sib_near, 2), (sib_near, 3)),
        (8, (sib_far, 0), (sib_far, 1)),
    ):
        cres[index] = ref[i * half : (i + 1) * half, :]
        cden[index] = ref_density[k * half : (k + 1) * half, :]

    body = pl.ds(8, half)
    c1[0, body, :] = far[2 * half : 3 * half, :]
    for i in range(1, 9):
        place = brick + jnp.where(core == 0, i - 4, 4 - i)
        valid = ((place >= 0) & (place < bricks)).astype(f32)
        factor = (WEIGHT * valid) / (cden[i] + 14.0 * scale1)
        cden[i] = factor
        c1[i, body, :] = factor * cres[i]

    def relax(ref, i, k):
        v = ref[i, body, :]
        f = stencil(ref, i, 0, half)
        return (1.0 - WEIGHT) * v + cden[k] * (cres[k] + 2.0 * scale1 * (f - v))

    for i in range(7):
        value = relax(c1, i + 1, i + 1)
        row = jnp.where(core == 0, spread[i + 1 : i + 2], spread[7 - i : 8 - i])
        pieces = [jnp.broadcast_to(row[:, t * half : (t + 1) * half], (block, half)) for t in range(TILES)]
        c2[i, body, :] = value + jnp.concatenate(pieces, 0)
    for i in range(5):
        c3[i, body, :] = relax(c2, i + 1, i + 2)
    columns = (iota((half, width), 0) == (iota((half, width), 1) >> 1)).astype(bf16)
    for i in range(3):
        fine = dot_exact(relax(c3, i + 1, i + 3), columns)
        put_halves(grown, i, pl.ds(0, half, stride=2), fine)
        put_halves(grown, i, pl.ds(1, half, stride=2), fine)

    wait_all(loads)
    inner = pl.ds(8, height)
    for k in range(2):
        side = slice(k * half, (k + 1) * half)
        s3[0, inner, side] = near_f[0, :, side] + grown[0, k]
        s3[1, inner, side] = s2_lo[0, :, side] + grown[0, k]
        s3[2, inner, side] = s2_lo[1, :, side] + grown[1, k]
        s3[3, inner, side] = s2_hi[0, inner, side] + grown[1, k]
        s3[4, inner, side] = s2_hi[1, inner, side] + grown[2, k]
        s3[5, inner, side] = sib_f[0, :, side] + grown[2, k]

    at_start = jnp.where(core == 0, brick > 0, brick < bricks - 1).astype(f32)
    at_end = jnp.where(core == 0, brick < bricks - 1, brick > 0).astype(f32)
    for j in range(4):

        def smooth(row, j=j):
            part = pl.ds(row, CHUNK)
            v = s3[j + 1, pl.ds(row + 8, CHUNK), :]
            f = stencil(s3, j + 1, row, CHUNK)
            if j in (1, 2):
                layer = core if j == 1 else 1 - core
                source, density, top = rhs[0, layer, part, :], dens[layer, part, :], WEIGHT
            else:
                edge = 2 * (j // 3)
                source, density = halo[edge, part, :], halo[edge + 1, part, :]
                top = WEIGHT * (at_end if edge else at_start)
            factor = top / (density + 14.0 * scale)
            wd[j, part, :] = factor
            new = (1.0 - WEIGHT) * v + factor * (source + 2.0 * scale * (f - v))
            s4[j, pl.ds(row + 8, CHUNK), :] = new

        chunks(height, smooth)
    for j, out in ((0, to_b), (1, to_a)):

        def smooth_last(row, j=j, out=out):
            part = pl.ds(row, CHUNK)
            v = s4[j + 1, pl.ds(row + 8, CHUNK), :]
            f = stencil(s4, j + 1, row, CHUNK)
            source = rhs[0, core if j == 0 else 1 - core, part, :]
            out[0, part, :] = (1.0 - WEIGHT) * v + wd[j + 1, part, :] * (source + 2.0 * scale * (f - v))

        chunks(height, smooth_last)


def inside_kernel(kappa_in, rhs, dens, to_a, to_b, sol_out, out, s, kappa, sems):
    core = position()[0]
    load = pltpu.make_async_copy(kappa_in, kappa, sems.at[0])
    stores = [
        pltpu.make_async_copy(to_b.at[0], sol_out.at[0, core], sems.at[1]),
        pltpu.make_async_copy(to_a.at[0], sol_out.at[0, 1 - core], sems.at[2]),
    ]
    load.start()
    start_all(stores)
    height = dens.shape[1]
    inner = pl.ds(8, height)
    clear_edges(s)
    s[core, inner, :] = to_b[0]
    s[1 - core, inner, :] = to_a[0]
    load.wait()
    scale = kappa[0]
    for j in range(2):

        def finish(row, j=j):
            part = pl.ds(row, CHUNK)
            more = pl.ds(row, CHUNK + 16)
            f = filter_yz(s[j, more, :] + 0.5 * s[1 - j, more, :])
            center = dens[j, part, :] + 16.0 * scale
            out[j, part, :] = rhs[0, j, part, :] - center * s[j, pl.ds(row + 8, CHUNK), :] + 2.0 * scale * f

        chunks(height, finish)
    wait_all(stores)


def residual_kernel(kappa_in, inside, halo_a, halo_b, out, s, done, kappa, sems):
    core = position()[0]
    load = pltpu.make_async_copy(kappa_in, kappa, sems.at[0])
    load.start()
    height = inside.shape[1]
    inner = pl.ds(8, height)
    clear_edges(s)
    s[core, inner, :] = halo_b[0]
    s[1 - core, inner, :] = halo_a[0]
    load.wait()
    scale = kappa[0]
    stores = []
    for j in range(2):

        def finish(row, j=j):
            part = pl.ds(row, CHUNK)
            done[j, part, :] = inside[j, part, :] + scale * filter_yz(s[j, pl.ds(row, CHUNK + 16), :])

        chunks(height, finish)
        stores.append(pltpu.make_async_copy(done.at[j], out.at[0, j], sems.at[1 + j]))
        stores[-1].start()
    wait_all(stores)


def shape(*dims):
    return jax.ShapeDtypeStruct(dims, f32)


def local(rhs, density, kappa, block_group):
    bricks = lax.axis_size("brick")
    species = lax.axis_size("spec")
    height, width = rhs.shape[2:]
    half = height // 2
    in_chip = [(i, i ^ 1) for i in range(bricks)]
    next_chip = [(i, ((i + 1) ^ 1) - 1) for i in range(1, bricks - 1)]
    second_chip = [(i, i - 3) for i in range(4, bricks, 2)] + [(i, i + 3) for i in range(1, bricks - 3, 2)]

    def swap_a(x):
        return lax.ppermute(x, "brick", in_chip)

    def swap_b(x):
        return lax.ppermute(x, "brick", next_chip)

    def swap_far(x):
        return lax.ppermute(x, "brick", second_chip)

    def around(x, k):
        return lax.ppermute(x, "spec", [(i, (i + k) % species) for i in range(species)])

    pieces = [around(density, k) for k in (1, 2, 3)]
    rhs_b = swap_b(rhs)
    rhs_a = swap_a(rhs)
    dens = pl.pallas_call(
        gather_kernel,
        out_shape=shape(2, height, width),
        in_specs=[HBM] + [ANY] * 3,
        out_specs=VM,
        scratch_shapes=[pltpu.SemaphoreType.DMA((4,))],
        compiler_params=PARAMS,
        name="collect_density",
    )(pltpu.with_memory_space_constraint(density, pltpu.HBM), *pieces)

    dens_b = swap_b(dens)
    dens_a = swap_a(dens)
    s1_own, s2_hi, wd_own, halo_hi, density1_own, density1_sib, send_b = pl.pallas_call(
        near_kernel,
        out_shape=(
            shape(2, height + 16, width),
            shape(2, height + 16, width),
            shape(height, width),
            pltpu.HBM((2, height, width), f32),
            shape(half, half),
            shape(half, half),
            shape(1, height, width),
        ),
        in_specs=[ANY] + [VM] * 4 + [ANY],
        out_specs=[VM, VM, VM, HBM, VM, VM, VM],
        scratch_shapes=[
            pltpu.VMEM((4, height + 16, width), f32),
            pltpu.VMEM((3, height, width), f32),
            pltpu.VMEM((2, 2, height, half), f32),
            pltpu.SMEM((1,), f32),
            pltpu.SemaphoreType.DMA((3,)),
        ],
        compiler_params=PARAMS,
        name="smooth_in_chip",
    )(kappa, rhs, dens, rhs_a, dens_a, rhs_b)
    near_f = swap_b(send_b)
    s2_lo, halo_lo, send_a, send_f, payload = pl.pallas_call(
        first_kernel,
        out_shape=(
            shape(2, height, width),
            pltpu.HBM((2, height, width), f32),
            shape(2 * half, half),
            shape(1, height, width),
            shape(bricks, 8, 128),
        ),
        in_specs=[ANY] + [VM] * 9,
        out_specs=[VM, HBM, VM, VM, VM],
        scratch_shapes=[
            pltpu.VMEM((4, height + 16, width), f32),
            pltpu.VMEM((4, height + 16, width), f32),
            pltpu.VMEM((1, height, width), f32),
            pltpu.VMEM((2, 2, height, half), f32),
            pltpu.SMEM((1,), f32),
            pltpu.SemaphoreType.DMA((3,)),
        ],
        compiler_params=PARAMS,
        name="smooth_and_restrict",
    )(kappa, rhs, dens, rhs_b, dens_b, s1_own, s2_hi, wd_own, density1_own, density1_sib)

    gathered = lax.all_to_all(payload, "brick", 0, 0, tiled=True)
    sib = swap_a(send_a)
    sib_f = swap_a(send_f)
    near_out, far_out = pl.pallas_call(
        join_kernel,
        out_shape=(shape(4 * half, half), shape(3 * half, half)),
        in_specs=[ANY] * 5,
        out_specs=[VM] * 2,
        scratch_shapes=[pltpu.SemaphoreType.DMA((7,))],
        compiler_params=PARAMS,
        name="join_chip",
    )(send_a, sib, density1_sib, density1_own, near_f)
    near = swap_b(near_out)
    far = swap_far(far_out)
    near, far, gathered = lax.optimization_barrier((near, far, gathered))
    sib_near = swap_a(near)
    sib_far = swap_a(far)

    in_hbm = functools.partial(pltpu.with_memory_space_constraint, memory_space=pltpu.HBM)
    to_a, to_b = pl.pallas_call(
        second_kernel,
        out_shape=(shape(1, height, width), shape(1, height, width)),
        in_specs=[ANY, HBM, HBM] + [VM] * 16,
        out_specs=[VM] * 2,
        scratch_shapes=[
            pltpu.VMEM((bricks + 32, 128), f32),
            pltpu.VMEM((9, half, half), f32),
            pltpu.VMEM((9, half, half), f32),
            pltpu.VMEM((9, half + 16, half), f32),
            pltpu.VMEM((7, half + 16, half), f32),
            pltpu.VMEM((5, half + 16, half), f32),
            pltpu.VMEM((3, 2, height, half), f32),
            pltpu.VMEM((6, height + 16, width), f32),
            pltpu.VMEM((4, height + 16, width), f32),
            pltpu.VMEM((4, height, width), f32),
            pltpu.VMEM((4, height, width), f32),
            pltpu.SMEM((1,), f32),
            pltpu.SemaphoreType.DMA((3,)),
        ],
        compiler_params=PARAMS,
        name="correct_and_smooth",
    )(
        kappa, in_hbm(halo_lo), in_hbm(halo_hi), rhs, dens, s2_lo, s2_hi, near_f, sib_f, density1_sib, density1_own, send_a,
        sib, near, far, sib_near, sib_far,
        gathered, block_group
    )

    halo_b = swap_b(to_b)
    halo_a = swap_a(to_a)
    solution, inside = pl.pallas_call(
        inside_kernel,
        out_shape=(shape(1, 2, height, width), shape(2, height, width)),
        in_specs=[ANY] + [VM] * 4,
        out_specs=[ANY, VM],
        scratch_shapes=[
            pltpu.VMEM((2, height + 16, width), f32),
            pltpu.SMEM((1,), f32),
            pltpu.SemaphoreType.DMA((3,)),
        ],
        compiler_params=PARAMS,
        name="residual_inside",
    )(kappa, rhs, dens, to_a, to_b)
    residual = pl.pallas_call(
        residual_kernel,
        out_shape=shape(1, 2, height, width),
        in_specs=[ANY] + [VM] * 3,
        out_specs=ANY,
        scratch_shapes=[
            pltpu.VMEM((2, height + 16, width), f32),
            pltpu.VMEM((2, height, width), f32),
            pltpu.SMEM((1,), f32),
            pltpu.SemaphoreType.DMA((3,)),
        ],
        compiler_params=PARAMS,
        name="residual",
    )(kappa, inside, halo_a, halo_b)
    return (solution, residual)


def solution(mesh):
    return jax.shard_map(
        local,
        mesh=mesh,
        in_specs=(P("spec", "brick", None, None), P("brick", "spec", None), P("spec"), P()),
        out_specs=(P("spec", "brick", None, None), P("spec", "brick", None, None)),
        check_vma=False,
    )
```

```python
import functools

import jax
import jax.numpy as jnp
from jax import lax
from jax.experimental import pallas as pl
from jax.experimental.pallas import tpu as pltpu
from jax.sharding import PartitionSpec as P

WEIGHT = 0.85
COARSE_WEIGHT = 0.6
COARSE_SWEEPS = 3
TILES = 4
CHUNK = 64
f32 = jnp.float32
bf16 = jnp.bfloat16
VM = pl.BlockSpec(memory_space=pltpu.VMEM)
ANY = pl.BlockSpec(memory_space=pl.ANY)
SM = pl.BlockSpec(memory_space=pltpu.SMEM)
HBM = pl.BlockSpec(memory_space=pltpu.HBM)
PARAMS = pltpu.CompilerParams(vmem_limit_bytes=16 * 1024 * 1024)


def iota(shape, dim):
    return lax.broadcasted_iota(jnp.int32, shape, dim)


def split(x):
    high = x.astype(bf16)
    rest = x - high.astype(f32)
    middle = rest.astype(bf16)
    low = (rest - middle.astype(f32)).astype(bf16)
    return high, middle, low


def dot_exact(x, w):
    high, middle, low = split(x)
    dot = functools.partial(jnp.dot, preferred_element_type=f32)
    return dot(high, w) + (dot(middle, w) + dot(low, w))


def filter_z(y):
    width = y.shape[1]
    lane = iota((1, width), 1)
    before = jnp.where(lane == 0, 0.0, 0.5)
    after = jnp.where(lane == width - 1, 0.0, 0.5)
    return y + before * pltpu.roll(y, 1, 1) + after * pltpu.roll(y, width - 1, 1)


def filter_yz(m):
    rows = m.shape[0]
    y = m + 0.5 * (pltpu.roll(m, 1, 0) + pltpu.roll(m, rows - 1, 0))
    return filter_z(y[8 : rows - 8])


def stencil(ref, i, row, rows):
    part = pl.ds(row, rows + 16)
    return filter_yz(ref[i, part, :] + 0.5 * (ref[i - 1, part, :] + ref[i + 1, part, :]))


def clear_edges(ref):
    layers, rows, width = ref.shape
    zero = jnp.zeros((layers, 8, width), f32)
    ref[:, 0:8, :] = zero
    ref[:, rows - 8 : rows, :] = zero


def chunks(rows, body):
    for row in range(0, rows, CHUNK):
        body(row)


def coarsen_z(rows, width):
    return ((iota((width, width // 2), 0) >> 1) == iota((width, width // 2), 1)).astype(bf16)


def put_halves(ref, i, part, x):
    half = x.shape[1] // 2
    ref[i, 0, part, :] = x[:, :half]
    ref[i, 1, part, :] = x[:, half:]


def pair_rows(ref, i, half):
    even, odd = pl.ds(0, half, stride=2), pl.ds(1, half, stride=2)
    return jnp.concatenate([ref[i, k, even, :] + ref[i, k, odd, :] for k in range(2)], 1)


def position():
    brick = lax.axis_index("brick")
    return brick & 1, brick, lax.axis_size("brick")


def start_all(copies):
    for copy in copies:
        copy.start()


def wait_all(copies):
    for copy in copies:
        copy.wait()


def join_kernel(mine, other, density1_sib, density1_own, near_f, near, far):
    del near_f
    half = far.shape[0] // 3
    parts = [pl.ds(i * half, half) for i in range(4)]
    near[parts[0], :] = mine[parts[0], :]
    near[parts[1], :] = density1_own[...]
    near[parts[2], :] = other[parts[0], :]
    near[parts[3], :] = density1_sib[...]
    far[parts[0], :] = mine[parts[0], :]
    far[parts[1], :] = density1_own[...]
    far[parts[2], :] = other[parts[1], :]


def gather_kernel(shard, p1, p2, p3, dens, sems):
    count = 4
    rows = shard.shape[1]

    def place(k):
        owner = lax.rem(lax.axis_index("spec") - k + count, count)
        return pl.ds(pl.multiple_of(owner * rows, rows), rows)

    own = pltpu.make_async_copy(shard, dens.at[:, place(0), :], sems.at[0])
    own.start()
    for k, piece in ((1, p1), (2, p2), (3, p3)):
        dens[:, place(k), :] = piece[...]
    own.wait()


def begin_layers(source, density, layers, work, index, wd, s1, scale, top, keep):
    height = density.shape[1]

    def begin(row):
        part = pl.ds(row, CHUNK)
        pair = density[0, part, :] + density[1, part, :]
        put_halves(work, index, part, pair)
        for layer, slot in layers:
            factor = top / (density[layer, part, :] + 14.0 * scale)
            if slot in keep:
                wd[keep[slot], part, :] = factor
            s1[slot, pl.ds(row + 8, CHUNK), :] = factor * source[0, layer, part, :]

    chunks(height, begin)


def near_kernel(
    kappa, rhs, dens, rhs_a, dens_a, rhs_b,
    s1_own, s2_hi, wd_own, halo_out, density1_own, density1_sib, send_b,
    s1, wd, work, sems,
):
    del rhs_b
    core, brick, bricks = position()
    stores = [
        pltpu.make_async_copy(rhs_a.at[0, core], halo_out.at[0], sems.at[1]),
        pltpu.make_async_copy(dens_a.at[core], halo_out.at[1], sems.at[2]),
    ]
    start_all(stores)
    height, width = dens.shape[1:]
    half = height // 2
    clear_edges(s1)
    clear_edges(s2_hi)
    scale = kappa[0]
    valid = jnp.where(core == 0, brick < bricks - 1, brick > 0).astype(f32)
    begin_layers(rhs, dens, ((core, 0), (1 - core, 1)), work, 0, wd, s1, scale, WEIGHT, {0: 0, 1: 1})
    begin_layers(rhs_a, dens_a, ((core, 2), (1 - core, 3)), work, 1, wd, s1, scale, WEIGHT * valid, {2: 2})
    for j in (1, 2):

        def smooth(row, j=j):
            part = pl.ds(row, CHUNK)
            v = s1[j, pl.ds(row + 8, CHUNK), :]
            f = stencil(s1, j, row, CHUNK)
            source = rhs[0, 1 - core, part, :] if j == 1 else rhs_a[0, core, part, :]
            new = (1.0 - WEIGHT) * v + wd[j, part, :] * (source + 2.0 * scale * (f - v))
            s2_hi[j - 1, pl.ds(row + 8, CHUNK), :] = new
            if j == 1:
                send_b[0, part, :] = new

        chunks(height, smooth)
    s1_own[...] = s1[0:2]
    wd_own[...] = wd[0]
    columns = coarsen_z(height, width)
    density1_own[...] = 0.125 * dot_exact(pair_rows(work, 0, half), columns)
    density1_sib[...] = 0.125 * dot_exact(pair_rows(work, 1, half), columns)
    wait_all(stores)


def first_kernel(
    kappa, rhs, dens, rhs_b, dens_b, s1_own, s2_hi, wd_own, density1_own, density1_sib,
    s2_lo, halo_out, send_a, send_f, payload,
    s1, s2, wd, work, sems,
):
    core, brick, bricks = position()
    stores = [
        pltpu.make_async_copy(rhs_b.at[0, 1 - core], halo_out.at[0], sems.at[1]),
        pltpu.make_async_copy(dens_b.at[1 - core], halo_out.at[1], sems.at[2]),
    ]
    start_all(stores)
    height, width = dens.shape[1:]
    half = height // 2
    clear_edges(s1)
    clear_edges(s2)
    s1[2:4] = s1_own[...]
    s2[2:4] = s2_hi[...]
    scale = kappa[0]
    scale1 = 0.25 * scale
    valid_lo = jnp.where(core == 0, brick > 0, brick < bricks - 1).astype(f32)
    valid_hi = jnp.where(core == 0, brick < bricks - 1, brick > 0).astype(f32)
    begin_layers(rhs_b, dens_b, ((core, 0), (1 - core, 1)), work, 0, wd, s1, scale, WEIGHT * valid_lo, {1: 0})

    for j in (1, 2):

        def smooth(row, j=j):
            part = pl.ds(row, CHUNK)
            v = s1[j, pl.ds(row + 8, CHUNK), :]
            f = stencil(s1, j, row, CHUNK)
            source, factor = (rhs_b[0, 1 - core, part, :], wd[0, part, :]) if j == 1 else (rhs[0, core, part, :], wd_own[part, :])
            new = (1.0 - WEIGHT) * v + factor * (source + 2.0 * scale * (f - v))
            s2[j - 1, pl.ds(row + 8, CHUNK), :] = new
            s2_lo[j - 1, part, :] = new

        chunks(height, smooth)

    def restrict(row):
        part = pl.ds(row, CHUNK)
        total = jnp.zeros((CHUNK, width), f32)
        for slot, layer in ((1, core), (2, 1 - core)):
            v = s2[slot, pl.ds(row + 8, CHUNK), :]
            f = stencil(s2, slot, row, CHUNK)
            center = dens[layer, part, :] + 16.0 * scale
            total = total + (rhs[0, layer, part, :] - center * v + 2.0 * scale * f)
        put_halves(work, 1, part, total)

    chunks(height, restrict)
    columns = coarsen_z(height, width)
    density1 = [0.125 * dot_exact(pair_rows(work, 0, half), columns), density1_own[...], density1_sib[...]]
    coarse_res = 0.125 * dot_exact(pair_rows(work, 1, half), columns)

    send_a[0:half, :] = coarse_res
    stores.append(pltpu.make_async_copy(s2.at[1, pl.ds(8, height), :], send_f.at[0], sems.at[0]))
    stores[-1].start()

    first = WEIGHT * coarse_res / (density1[1] + 14.0 * scale1)
    send_a[half : 2 * half, :] = first
    pad = jnp.zeros((8, half), f32)
    spread = filter_yz(jnp.concatenate([pad, first, pad], 0))
    own_factor = WEIGHT / (density1[1] + 14.0 * scale1)
    shares = [
        (WEIGHT * valid_lo) * scale1 / (density1[0] + 14.0 * scale1) * spread,
        (1.0 - WEIGHT) * first + own_factor * (coarse_res + 2.0 * scale1 * (spread - first)),
        (WEIGHT * valid_hi) * scale1 / (density1[2] + 14.0 * scale1) * spread,
    ]
    block = half // TILES
    filtered = []
    plain = []
    for e, share in enumerate(shares):
        rest = -(density1[e] + 16.0 * scale1) * share
        if e == 1:
            rest = rest + coarse_res
        for t in range(TILES):
            at = t * block
            row = 2.0 * jnp.sum(share[at : at + block], axis=0, keepdims=True)
            row = row - 0.5 * (share[at : at + 1] + share[at + block - 1 : at + block])
            if t > 0:
                row = row + 0.5 * share[at - 1 : at]
            if t < TILES - 1:
                row = row + 0.5 * share[at + block : at + block + 1]
            filtered.append(row)
            plain.append(jnp.sum(rest[at : at + block], axis=0, keepdims=True))
    for t in range(TILES):
        plain.append(jnp.sum(density1[1][t * block : (t + 1) * block], axis=0, keepdims=True))
    for rows in (filtered, plain):
        for t in range(TILES):
            low, high = rows[t], rows[2 * TILES + t]
            rows[t] = jnp.where(core == 0, low, high)
            rows[2 * TILES + t] = jnp.where(core == 0, high, low)
    filtered.append(jnp.zeros((4, half), f32))
    filtered = jnp.concatenate(filtered, 0)
    plain = jnp.concatenate(plain, 0)
    cell = iota((half, 128), 0)
    tile = iota((half, 128), 1) & 3
    start = tile * block
    inside = ((cell >= start) & (cell < start + block)).astype(f32)
    ends = ((cell == start) | (cell == start + block - 1)).astype(f32)
    beside = ((cell == start - 1) | (cell == start + block)).astype(f32)
    plain_w = inside.astype(bf16)
    filter_w = (2.0 * inside - 0.5 * ends + 0.5 * beside).astype(bf16)
    row = iota((16, 128), 0)
    lane = iota((16, 128), 1)
    fits = ((lane >> 2) & 3) == (row & 3)
    out = jnp.where(fits & ((lane >> 4) == (row >> 2)), dot_exact(filtered, filter_w), 0.0)
    out = jnp.where(row >= 12, 0.0, out)
    out = out + jnp.where(fits & ((lane >> 4) == (row >> 2) + 3), dot_exact(plain, plain_w), 0.0)
    payload[...] = jnp.broadcast_to(jnp.sum(out, axis=0, keepdims=True)[None], payload.shape)
    wait_all(stores)


def lanes_sum(x):
    for step in (16, 32, 64):
        x = x + pltpu.roll(x, step, 1)
    return x


def row_before(x):
    return jnp.where(iota(x.shape, 0) == 0, 0.0, pltpu.roll(x, 1, 0))


def row_after(x):
    return jnp.where(iota(x.shape, 0) == x.shape[0] - 1, 0.0, pltpu.roll(x, x.shape[0] - 1, 0))


def solve_groups(gathered, groups, scale1, block):
    bricks = gathered.shape[0]
    lane = iota(gathered.shape, 1)
    slot = lane >> 4
    up = pltpu.roll(gathered, bricks - 1, 0)
    down = pltpu.roll(gathered, 1, 0)

    def pick(first):
        return lanes_sum(
            jnp.where(
                slot == first,
                up,
                jnp.where(slot == first + 1, gathered, jnp.where(slot == first + 2, down, 0.0)),
            )
        )

    filtered = pick(0)
    plain = pick(3)
    density_sum = lanes_sum(jnp.where(slot == 6, gathered, 0.0))
    remainder = plain + 2.0 * scale1 * filtered + scale1 * (row_before(filtered) + row_after(filtered))

    blocks = groups.shape[1]
    repeat = (iota((blocks, 128), 0) == (iota((blocks, 128), 1) & (blocks - 1))).astype(bf16)
    ids = jnp.dot(groups.astype(f32).astype(bf16), repeat, preferred_element_type=f32)
    diagonal_lane = (iota(gathered.shape, 0) & 7) == slot
    packed = jnp.where(diagonal_lane, ids, 0.0)
    member = [
        (ids == jnp.sum(packed[8 * j : 8 * j + 8], axis=0, keepdims=True)).astype(f32) for j in range(bricks // 8)
    ]

    def project(x):
        chosen = jnp.where(diagonal_lane, x, 0.0)
        total = jnp.zeros_like(x)
        for j in range(bricks // 8):
            total = total + member[j] * jnp.sum(chosen[8 * j : 8 * j + 8], axis=0, keepdims=True)
        return lanes_sum(total)

    place = iota(ids.shape, 0)
    as_before = jnp.where((place > 0) & (pltpu.roll(ids, 1, 0) == ids), 0.5, 0.0)
    as_after = jnp.where((place < bricks - 1) & (pltpu.roll(ids, bricks - 1, 0) == ids), 0.5, 0.0)
    inner = 2.0 * block - 1.0
    same = inner * inner * (1.0 + as_before + as_after)
    cells = float(block * block)
    diagonal = project(density_sum + scale1 * (16.0 * cells - 2.0 * same))
    group_rhs = project(remainder)
    column = lane & 3
    line = (lane >> 2) & 3
    center = density_sum + 16.0 * cells * scale1

    def image(g):
        z = inner * g + 0.5 * (
            jnp.where(column > 0, pltpu.roll(g, 1, 1), 0.0) + jnp.where(column < 3, pltpu.roll(g, 127, 1), 0.0)
        )
        y = inner * z + 0.5 * (
            jnp.where(line > 0, pltpu.roll(z, 4, 1), 0.0) + jnp.where(line < 3, pltpu.roll(z, 124, 1), 0.0)
        )
        return center * g - 2.0 * scale1 * (y + 0.5 * (row_before(y) + row_after(y)))

    factor = COARSE_WEIGHT / diagonal
    fix = factor * group_rhs
    for _ in range(COARSE_SWEEPS - 1):
        fix = fix + factor * (group_rhs - project(image(fix)))
    return fix


def solve_kernel(kappa, gathered, groups, spread, fixes):
    core, brick, _ = position()
    scale1 = 0.25 * kappa[0]
    half = spread.shape[1] // TILES
    block = half // TILES
    fixes[0:8, :] = jnp.zeros((8, 128), f32)
    count = gathered.shape[0]
    fixes[8 + count : 32 + count, :] = jnp.zeros((24, 128), f32)
    fixes[8 : 8 + count, :] = solve_groups(gathered[:, 0, :], groups[...], scale1, block)
    window = fixes[pl.ds(brick + 4, 16), :]
    turn = jnp.zeros_like(window)
    row = iota(window.shape, 0)
    for i in range(9):
        turn = jnp.where(row == i, window[8 - i : 9 - i], turn)
    window = jnp.where(core == 0, window, turn)
    lane = iota((128, TILES * half), 1)
    per = (lane >> (half.bit_length() - 1)) * 4 + ((lane & (half - 1)) >> (block.bit_length() - 1))
    spread[...] = dot_exact(window, (iota((128, TILES * half), 0) == per).astype(bf16))


def second_kernel(
    kappa, halo_lo_in, halo_hi_in, rhs, dens, s2_lo, s2_hi, near_f, sib_f, density1_sib, density1_own, send_a, sib, near, far, sib_near, sib_far, spread,
    to_a, to_b,
    cres, cden, c1, c2, c3, grown, s3, s4, wd, halo, sems,
):
    core, brick, bricks = position()
    loads = [
        pltpu.make_async_copy(halo_lo_in, halo.at[pl.ds(0, 2)], sems.at[1]),
        pltpu.make_async_copy(halo_hi_in, halo.at[pl.ds(2, 2)], sems.at[2]),
    ]
    start_all(loads)
    half = cres.shape[1]
    height, width = rhs.shape[2:]
    block = half // TILES
    for ref in (c1, c2, c3, s3, s4):
        clear_edges(ref)
    scale = kappa[0]
    scale1 = 0.25 * scale

    for index, (ref, i), (ref_density, k) in (
        (1, (far, 0), (far, 1)),
        (2, (near, 2), (near, 3)),
        (3, (near, 0), (near, 1)),
        (4, (send_a, 0), (density1_own, 0)),
        (5, (sib, 0), (density1_sib, 0)),
        (6, (sib_near, 0), (sib_near, 1)),
        (7, (sib_near, 2), (sib_near, 3)),
        (8, (sib_far, 0), (sib_far, 1)),
    ):
        cres[index] = ref[i * half : (i + 1) * half, :]
        cden[index] = ref_density[k * half : (k + 1) * half, :]

    body = pl.ds(8, half)
    c1[0, body, :] = far[2 * half : 3 * half, :]
    for i in range(1, 9):
        place = brick + jnp.where(core == 0, i - 4, 4 - i)
        valid = ((place >= 0) & (place < bricks)).astype(f32)
        factor = (WEIGHT * valid) / (cden[i] + 14.0 * scale1)
        cden[i] = factor
        c1[i, body, :] = factor * cres[i]

    def relax(ref, i, k):
        v = ref[i, body, :]
        f = stencil(ref, i, 0, half)
        return (1.0 - WEIGHT) * v + cden[k] * (cres[k] + 2.0 * scale1 * (f - v))

    for i in range(7):
        value = relax(c1, i + 1, i + 1)
        row = spread[i + 1 : i + 2, :]
        pieces = [jnp.broadcast_to(row[:, t * half : (t + 1) * half], (block, half)) for t in range(TILES)]
        c2[i, body, :] = value + jnp.concatenate(pieces, 0)
    for i in range(5):
        c3[i, body, :] = relax(c2, i + 1, i + 2)
    columns = (iota((half, width), 0) == (iota((half, width), 1) >> 1)).astype(bf16)
    for i in range(3):
        fine = dot_exact(relax(c3, i + 1, i + 3), columns)
        put_halves(grown, i, pl.ds(0, half, stride=2), fine)
        put_halves(grown, i, pl.ds(1, half, stride=2), fine)

    wait_all(loads)
    inner = pl.ds(8, height)
    for k in range(2):
        side = slice(k * half, (k + 1) * half)
        s3[0, inner, side] = near_f[0, :, side] + grown[0, k]
        s3[1, inner, side] = s2_lo[0, :, side] + grown[0, k]
        s3[2, inner, side] = s2_lo[1, :, side] + grown[1, k]
        s3[3, inner, side] = s2_hi[0, inner, side] + grown[1, k]
        s3[4, inner, side] = s2_hi[1, inner, side] + grown[2, k]
        s3[5, inner, side] = sib_f[0, :, side] + grown[2, k]

    at_start = jnp.where(core == 0, brick > 0, brick < bricks - 1).astype(f32)
    at_end = jnp.where(core == 0, brick < bricks - 1, brick > 0).astype(f32)
    for j in range(4):

        def smooth(row, j=j):
            part = pl.ds(row, CHUNK)
            v = s3[j + 1, pl.ds(row + 8, CHUNK), :]
            f = stencil(s3, j + 1, row, CHUNK)
            if j in (1, 2):
                layer = core if j == 1 else 1 - core
                source, density, top = rhs[0, layer, part, :], dens[layer, part, :], WEIGHT
            else:
                edge = 2 * (j // 3)
                source, density = halo[edge, part, :], halo[edge + 1, part, :]
                top = WEIGHT * (at_end if edge else at_start)
            factor = top / (density + 14.0 * scale)
            wd[j, part, :] = factor
            new = (1.0 - WEIGHT) * v + factor * (source + 2.0 * scale * (f - v))
            s4[j, pl.ds(row + 8, CHUNK), :] = new

        chunks(height, smooth)
    for j, out in ((0, to_b), (1, to_a)):

        def smooth_last(row, j=j, out=out):
            part = pl.ds(row, CHUNK)
            v = s4[j + 1, pl.ds(row + 8, CHUNK), :]
            f = stencil(s4, j + 1, row, CHUNK)
            source = rhs[0, core if j == 0 else 1 - core, part, :]
            out[0, part, :] = (1.0 - WEIGHT) * v + wd[j + 1, part, :] * (source + 2.0 * scale * (f - v))

        chunks(height, smooth_last)


def inside_kernel(kappa, rhs, dens, to_a, to_b, sol_out, out, s, sems):
    core = position()[0]
    stores = [
        pltpu.make_async_copy(to_b.at[0], sol_out.at[0, core], sems.at[1]),
        pltpu.make_async_copy(to_a.at[0], sol_out.at[0, 1 - core], sems.at[2]),
    ]
    start_all(stores)
    height = dens.shape[1]
    inner = pl.ds(8, height)
    clear_edges(s)
    s[core, inner, :] = to_b[0]
    s[1 - core, inner, :] = to_a[0]
    scale = kappa[0]
    for j in range(2):

        def finish(row, j=j):
            part = pl.ds(row, CHUNK)
            more = pl.ds(row, CHUNK + 16)
            f = filter_yz(s[j, more, :] + 0.5 * s[1 - j, more, :])
            center = dens[j, part, :] + 16.0 * scale
            out[j, part, :] = rhs[0, j, part, :] - center * s[j, pl.ds(row + 8, CHUNK), :] + 2.0 * scale * f

        chunks(height, finish)
    wait_all(stores)


def residual_kernel(kappa, inside, halo_a, halo_b, out, s, done, sems):
    core = position()[0]
    height = inside.shape[1]
    inner = pl.ds(8, height)
    clear_edges(s)
    s[core, inner, :] = halo_b[0]
    s[1 - core, inner, :] = halo_a[0]
    scale = kappa[0]
    stores = []
    for j in range(2):

        def finish(row, j=j):
            part = pl.ds(row, CHUNK)
            done[j, part, :] = inside[j, part, :] + scale * filter_yz(s[j, pl.ds(row, CHUNK + 16), :])

        chunks(height, finish)
        stores.append(pltpu.make_async_copy(done.at[j], out.at[0, j], sems.at[1 + j]))
        stores[-1].start()
    wait_all(stores)


def shape(*dims):
    return jax.ShapeDtypeStruct(dims, f32)


def local(rhs, density, kappa, block_group):
    bricks = lax.axis_size("brick")
    species = lax.axis_size("spec")
    height, width = rhs.shape[2:]
    half = height // 2
    in_chip = [(i, i ^ 1) for i in range(bricks)]
    next_chip = [(i, ((i + 1) ^ 1) - 1) for i in range(1, bricks - 1)]
    second_chip = [(i, i - 3) for i in range(4, bricks, 2)] + [(i, i + 3) for i in range(1, bricks - 3, 2)]

    def swap_a(x):
        return lax.ppermute(x, "brick", in_chip)

    def swap_b(x):
        return lax.ppermute(x, "brick", next_chip)

    def swap_far(x):
        return lax.ppermute(x, "brick", second_chip)

    def around(x, k):
        return lax.ppermute(x, "spec", [(i, (i + k) % species) for i in range(species)])

    pieces = [around(density, k) for k in (1, 2, 3)]
    rhs_b = swap_b(rhs)
    rhs_a = swap_a(rhs)
    dens = pl.pallas_call(
        gather_kernel,
        out_shape=shape(2, height, width),
        in_specs=[HBM] + [VM] * 3,
        out_specs=VM,
        scratch_shapes=[pltpu.SemaphoreType.DMA((1,))],
        compiler_params=PARAMS,
        name="collect_density",
    )(pltpu.with_memory_space_constraint(density, pltpu.HBM), *pieces)

    dens_b = swap_b(dens)
    dens_a = swap_a(dens)
    s1_own, s2_hi, wd_own, halo_hi, density1_own, density1_sib, send_b = pl.pallas_call(
        near_kernel,
        out_shape=(
            shape(2, height + 16, width),
            shape(2, height + 16, width),
            shape(height, width),
            pltpu.HBM((2, height, width), f32),
            shape(half, half),
            shape(half, half),
            shape(1, height, width),
        ),
        in_specs=[SM] + [VM] * 4 + [ANY],
        out_specs=[VM, VM, VM, HBM, VM, VM, VM],
        scratch_shapes=[
            pltpu.VMEM((4, height + 16, width), f32),
            pltpu.VMEM((3, height, width), f32),
            pltpu.VMEM((2, 2, height, half), f32),
            pltpu.SemaphoreType.DMA((3,)),
        ],
        compiler_params=PARAMS,
        name="smooth_in_chip",
    )(kappa, rhs, dens, rhs_a, dens_a, rhs_b)
    near_f = swap_b(send_b)
    s2_lo, halo_lo, send_a, send_f, payload = pl.pallas_call(
        first_kernel,
        out_shape=(
            shape(2, height, width),
            pltpu.HBM((2, height, width), f32),
            shape(2 * half, half),
            pltpu.HBM((1, height, width), f32),
            shape(bricks, 5, 128),
        ),
        in_specs=[SM] + [VM] * 9,
        out_specs=[VM, HBM, VM, HBM, VM],
        scratch_shapes=[
            pltpu.VMEM((4, height + 16, width), f32),
            pltpu.VMEM((4, height + 16, width), f32),
            pltpu.VMEM((1, height, width), f32),
            pltpu.VMEM((2, 2, height, half), f32),
            pltpu.SemaphoreType.DMA((3,)),
        ],
        compiler_params=PARAMS,
        name="smooth_and_restrict",
    )(kappa, rhs, dens, rhs_b, dens_b, s1_own, s2_hi, wd_own, density1_own, density1_sib)

    gathered = lax.all_to_all(payload, "brick", 0, 0, tiled=True)
    sib = swap_a(send_a)
    sib_f = swap_a(send_f)
    near_out, far_out = pl.pallas_call(
        join_kernel,
        out_shape=(shape(4 * half, half), shape(3 * half, half)),
        in_specs=[VM] * 4 + [ANY],
        out_specs=[VM] * 2,
        compiler_params=PARAMS,
        name="join_chip",
    )(send_a, sib, density1_sib, density1_own, near_f)
    near = swap_b(near_out)
    far = swap_far(far_out)
    half_lanes = TILES * half
    spread = pl.pallas_call(
        solve_kernel,
        out_shape=shape(16, half_lanes),
        in_specs=[SM] + [VM] * 2,
        out_specs=VM,
        scratch_shapes=[pltpu.VMEM((bricks + 32, 128), f32)],
        compiler_params=PARAMS,
        name="solve_aggregates",
    )(kappa, gathered, block_group)
    near, far, spread = lax.optimization_barrier((near, far, spread))
    sib_near = swap_a(near)
    sib_far = swap_a(far)

    in_hbm = functools.partial(pltpu.with_memory_space_constraint, memory_space=pltpu.HBM)
    to_a, to_b = pl.pallas_call(
        second_kernel,
        out_shape=(shape(1, height, width), shape(1, height, width)),
        in_specs=[SM, HBM, HBM] + [VM] * 15,
        out_specs=[VM] * 2,
        scratch_shapes=[
            pltpu.VMEM((9, half, half), f32),
            pltpu.VMEM((9, half, half), f32),
            pltpu.VMEM((9, half + 16, half), f32),
            pltpu.VMEM((7, half + 16, half), f32),
            pltpu.VMEM((5, half + 16, half), f32),
            pltpu.VMEM((3, 2, height, half), f32),
            pltpu.VMEM((6, height + 16, width), f32),
            pltpu.VMEM((4, height + 16, width), f32),
            pltpu.VMEM((4, height, width), f32),
            pltpu.VMEM((4, height, width), f32),
            pltpu.SemaphoreType.DMA((3,)),
        ],
        compiler_params=PARAMS,
        name="correct_and_smooth",
    )(
        kappa, in_hbm(halo_lo), in_hbm(halo_hi), rhs, dens, s2_lo, s2_hi, near_f, sib_f, density1_sib, density1_own, send_a,
        sib, near, far, sib_near, sib_far, spread
    )

    halo_b = swap_b(to_b)
    halo_a = swap_a(to_a)
    solution, inside = pl.pallas_call(
        inside_kernel,
        out_shape=(shape(1, 2, height, width), shape(2, height, width)),
        in_specs=[SM] + [VM] * 4,
        out_specs=[ANY, VM],
        scratch_shapes=[
            pltpu.VMEM((2, height + 16, width), f32),
            pltpu.SemaphoreType.DMA((3,)),
        ],
        compiler_params=PARAMS,
        name="residual_inside",
    )(kappa, rhs, dens, to_a, to_b)
    residual = pl.pallas_call(
        residual_kernel,
        out_shape=shape(1, 2, height, width),
        in_specs=[SM] + [VM] * 3,
        out_specs=ANY,
        scratch_shapes=[
            pltpu.VMEM((2, height + 16, width), f32),
            pltpu.VMEM((2, height, width), f32),
            pltpu.SemaphoreType.DMA((3,)),
        ],
        compiler_params=PARAMS,
        name="residual",
    )(kappa, inside, halo_a, halo_b)
    return (solution, residual)


def solution(mesh):
    return jax.shard_map(
        local,
        mesh=mesh,
        in_specs=(P("spec", "brick", None, None), P("brick", "spec", None), P("spec"), P()),
        out_specs=(P("spec", "brick", None, None), P("spec", "brick", None, None)),
        check_vma=False,
    )
```

```python
import functools

import jax
import jax.numpy as jnp
from jax import lax
from jax.experimental import pallas as pl
from jax.experimental.pallas import tpu as pltpu
from jax.sharding import PartitionSpec as P

WEIGHT = 0.85
COARSE_WEIGHT = 0.6
COARSE_SWEEPS = 3
TILES = 4
CHUNK = 64
f32 = jnp.float32
bf16 = jnp.bfloat16
VM = pl.BlockSpec(memory_space=pltpu.VMEM)
ANY = pl.BlockSpec(memory_space=pl.ANY)
SM = pl.BlockSpec(memory_space=pltpu.SMEM)
HBM = pl.BlockSpec(memory_space=pltpu.HBM)
PARAMS = pltpu.CompilerParams(vmem_limit_bytes=16 * 1024 * 1024)


def iota(shape, dim):
    return lax.broadcasted_iota(jnp.int32, shape, dim)


def split(x):
    high = x.astype(bf16)
    rest = x - high.astype(f32)
    middle = rest.astype(bf16)
    low = (rest - middle.astype(f32)).astype(bf16)
    return high, middle, low


def dot_exact(x, w):
    high, middle, low = split(x)
    dot = functools.partial(jnp.dot, preferred_element_type=f32)
    return dot(high, w) + (dot(middle, w) + dot(low, w))


def filter_z(y):
    width = y.shape[1]
    lane = iota((1, width), 1)
    before = jnp.where(lane == 0, 0.0, 0.5)
    after = jnp.where(lane == width - 1, 0.0, 0.5)
    return y + before * pltpu.roll(y, 1, 1) + after * pltpu.roll(y, width - 1, 1)


def filter_yz(m):
    rows = m.shape[0]
    y = m + 0.5 * (pltpu.roll(m, 1, 0) + pltpu.roll(m, rows - 1, 0))
    return filter_z(y[8 : rows - 8])


def stencil(ref, i, row, rows):
    part = pl.ds(row, rows + 16)
    return filter_yz(ref[i, part, :] + 0.5 * (ref[i - 1, part, :] + ref[i + 1, part, :]))


def clear_edges(ref):
    layers, rows, width = ref.shape
    zero = jnp.zeros((layers, 8, width), f32)
    ref[:, 0:8, :] = zero
    ref[:, rows - 8 : rows, :] = zero


def chunks(rows, body):
    for row in range(0, rows, CHUNK):
        body(row)


def coarsen_z(rows, width):
    return ((iota((width, width // 2), 0) >> 1) == iota((width, width // 2), 1)).astype(bf16)


def put_halves(ref, i, part, x):
    half = x.shape[1] // 2
    ref[i, 0, part, :] = x[:, :half]
    ref[i, 1, part, :] = x[:, half:]


def pair_rows(ref, i, half):
    even, odd = pl.ds(0, half, stride=2), pl.ds(1, half, stride=2)
    return jnp.concatenate([ref[i, k, even, :] + ref[i, k, odd, :] for k in range(2)], 1)


def position():
    brick = lax.axis_index("brick")
    return brick & 1, brick, lax.axis_size("brick")


def start_all(copies):
    for copy in copies:
        copy.start()


def wait_all(copies):
    for copy in copies:
        copy.wait()


def join_kernel(mine, other, density1_sib, density1_own, near_f, near, far):
    del near_f
    half = far.shape[0] // 3
    parts = [pl.ds(i * half, half) for i in range(4)]
    near[parts[0], :] = mine[parts[0], :]
    near[parts[1], :] = density1_own[...]
    near[parts[2], :] = other[parts[0], :]
    near[parts[3], :] = density1_sib[...]
    far[parts[0], :] = mine[parts[0], :]
    far[parts[1], :] = density1_own[...]
    far[parts[2], :] = other[parts[1], :]


def gather_kernel(shard, p1, p2, p3, dens, sems):
    count = 4
    rows = shard.shape[1]

    def place(k):
        owner = lax.rem(lax.axis_index("spec") - k + count, count)
        return pl.ds(pl.multiple_of(owner * rows, rows), rows)

    own = pltpu.make_async_copy(shard, dens.at[:, place(0), :], sems.at[0])
    own.start()
    for k, piece in ((1, p1), (2, p2), (3, p3)):
        dens[:, place(k), :] = piece[...]
    own.wait()


def begin_layers(source, density, layers, work, index, wd, s1, scale, top, keep):
    height = density.shape[1]

    def begin(row):
        part = pl.ds(row, CHUNK)
        pair = density[0, part, :] + density[1, part, :]
        put_halves(work, index, part, pair)
        for layer, slot in layers:
            factor = top / (density[layer, part, :] + 14.0 * scale)
            if slot in keep:
                wd[keep[slot], part, :] = factor
            s1[slot, pl.ds(row + 8, CHUNK), :] = factor * source[0, layer, part, :]

    chunks(height, begin)


def near_kernel(
    kappa, rhs, dens, rhs_a, dens_a, rhs_b,
    s1_own, s2_hi, wd_own, halo_out, density1_own, density1_sib, send_b,
    s1, wd, work, sems,
):
    del rhs_b
    core, brick, bricks = position()
    stores = [
        pltpu.make_async_copy(rhs_a.at[0, core], halo_out.at[0], sems.at[1]),
        pltpu.make_async_copy(dens_a.at[core], halo_out.at[1], sems.at[2]),
    ]
    start_all(stores)
    height, width = dens.shape[1:]
    half = height // 2
    clear_edges(s1)
    clear_edges(s2_hi)
    scale = kappa[0]
    valid = jnp.where(core == 0, brick < bricks - 1, brick > 0).astype(f32)
    begin_layers(rhs, dens, ((core, 0), (1 - core, 1)), work, 0, wd, s1, scale, WEIGHT, {0: 0, 1: 1})
    begin_layers(rhs_a, dens_a, ((core, 2), (1 - core, 3)), work, 1, wd, s1, scale, WEIGHT * valid, {2: 2})
    for j in (1, 2):

        def smooth(row, j=j):
            part = pl.ds(row, CHUNK)
            v = s1[j, pl.ds(row + 8, CHUNK), :]
            f = stencil(s1, j, row, CHUNK)
            source = rhs[0, 1 - core, part, :] if j == 1 else rhs_a[0, core, part, :]
            new = (1.0 - WEIGHT) * v + wd[j, part, :] * (source + 2.0 * scale * (f - v))
            s2_hi[j - 1, pl.ds(row + 8, CHUNK), :] = new
            if j == 1:
                send_b[0, part, :] = new

        chunks(height, smooth)
    s1_own[...] = s1[0:2]
    wd_own[...] = wd[0]
    columns = coarsen_z(height, width)
    density1_own[...] = 0.125 * dot_exact(pair_rows(work, 0, half), columns)
    density1_sib[...] = 0.125 * dot_exact(pair_rows(work, 1, half), columns)
    wait_all(stores)


def first_kernel(
    kappa, rhs, dens, rhs_b, dens_b, s1_own, s2_hi, wd_own, density1_own, density1_sib,
    s2_lo, halo_out, send_a, send_f, payload,
    s1, s2, wd, work, sems,
):
    core, brick, bricks = position()
    stores = [
        pltpu.make_async_copy(rhs_b.at[0, 1 - core], halo_out.at[0], sems.at[1]),
        pltpu.make_async_copy(dens_b.at[1 - core], halo_out.at[1], sems.at[2]),
    ]
    start_all(stores)
    height, width = dens.shape[1:]
    half = height // 2
    clear_edges(s1)
    clear_edges(s2)
    s1[2:4] = s1_own[...]
    s2[2:4] = s2_hi[...]
    scale = kappa[0]
    scale1 = 0.25 * scale
    valid_lo = jnp.where(core == 0, brick > 0, brick < bricks - 1).astype(f32)
    valid_hi = jnp.where(core == 0, brick < bricks - 1, brick > 0).astype(f32)
    begin_layers(rhs_b, dens_b, ((core, 0), (1 - core, 1)), work, 0, wd, s1, scale, WEIGHT * valid_lo, {1: 0})

    for j in (1, 2):

        def smooth(row, j=j):
            part = pl.ds(row, CHUNK)
            v = s1[j, pl.ds(row + 8, CHUNK), :]
            f = stencil(s1, j, row, CHUNK)
            source, factor = (rhs_b[0, 1 - core, part, :], wd[0, part, :]) if j == 1 else (rhs[0, core, part, :], wd_own[part, :])
            new = (1.0 - WEIGHT) * v + factor * (source + 2.0 * scale * (f - v))
            s2[j - 1, pl.ds(row + 8, CHUNK), :] = new
            s2_lo[j - 1, part, :] = new

        chunks(height, smooth)

    def restrict(row):
        part = pl.ds(row, CHUNK)
        total = jnp.zeros((CHUNK, width), f32)
        for slot, layer in ((1, core), (2, 1 - core)):
            v = s2[slot, pl.ds(row + 8, CHUNK), :]
            f = stencil(s2, slot, row, CHUNK)
            center = dens[layer, part, :] + 16.0 * scale
            total = total + (rhs[0, layer, part, :] - center * v + 2.0 * scale * f)
        put_halves(work, 1, part, total)

    chunks(height, restrict)
    columns = coarsen_z(height, width)
    density1 = [0.125 * dot_exact(pair_rows(work, 0, half), columns), density1_own[...], density1_sib[...]]
    coarse_res = 0.125 * dot_exact(pair_rows(work, 1, half), columns)

    send_a[0:half, :] = coarse_res
    stores.append(pltpu.make_async_copy(s2.at[1, pl.ds(8, height), :], send_f.at[0], sems.at[0]))
    stores[-1].start()

    first = WEIGHT * coarse_res / (density1[1] + 14.0 * scale1)
    send_a[half : 2 * half, :] = first
    pad = jnp.zeros((8, half), f32)
    spread = filter_yz(jnp.concatenate([pad, first, pad], 0))
    own_factor = WEIGHT / (density1[1] + 14.0 * scale1)
    shares = [
        (WEIGHT * valid_lo) * scale1 / (density1[0] + 14.0 * scale1) * spread,
        (1.0 - WEIGHT) * first + own_factor * (coarse_res + 2.0 * scale1 * (spread - first)),
        (WEIGHT * valid_hi) * scale1 / (density1[2] + 14.0 * scale1) * spread,
    ]
    block = half // TILES
    filtered = []
    plain = []
    for e, share in enumerate(shares):
        rest = -(density1[e] + 16.0 * scale1) * share
        if e == 1:
            rest = rest + coarse_res
        for t in range(TILES):
            at = t * block
            row = 2.0 * jnp.sum(share[at : at + block], axis=0, keepdims=True)
            row = row - 0.5 * (share[at : at + 1] + share[at + block - 1 : at + block])
            if t > 0:
                row = row + 0.5 * share[at - 1 : at]
            if t < TILES - 1:
                row = row + 0.5 * share[at + block : at + block + 1]
            filtered.append(row)
            plain.append(jnp.sum(rest[at : at + block], axis=0, keepdims=True))
    for t in range(TILES):
        plain.append(jnp.sum(density1[1][t * block : (t + 1) * block], axis=0, keepdims=True))
    for rows in (filtered, plain):
        for t in range(TILES):
            low, high = rows[t], rows[2 * TILES + t]
            rows[t] = jnp.where(core == 0, low, high)
            rows[2 * TILES + t] = jnp.where(core == 0, high, low)
    filtered.append(jnp.zeros((4, half), f32))
    filtered = jnp.concatenate(filtered, 0)
    plain = jnp.concatenate(plain, 0)
    cell = iota((half, 128), 0)
    tile = iota((half, 128), 1) & 3
    start = tile * block
    inside = ((cell >= start) & (cell < start + block)).astype(f32)
    ends = ((cell == start) | (cell == start + block - 1)).astype(f32)
    beside = ((cell == start - 1) | (cell == start + block)).astype(f32)
    plain_w = inside.astype(bf16)
    filter_w = (2.0 * inside - 0.5 * ends + 0.5 * beside).astype(bf16)
    row = iota((16, 128), 0)
    lane = iota((16, 128), 1)
    fits = ((lane >> 2) & 3) == (row & 3)
    out = jnp.where(fits & ((lane >> 4) == (row >> 2)), dot_exact(filtered, filter_w), 0.0)
    out = jnp.where(row >= 12, 0.0, out)
    out = out + jnp.where(fits & ((lane >> 4) == (row >> 2) + 3), dot_exact(plain, plain_w), 0.0)
    payload[...] = jnp.broadcast_to(jnp.sum(out, axis=0, keepdims=True)[None], payload.shape)
    wait_all(stores)


def lanes_sum(x):
    for step in (16, 32, 64):
        x = x + pltpu.roll(x, step, 1)
    return x


def row_before(x):
    return jnp.where(iota(x.shape, 0) == 0, 0.0, pltpu.roll(x, 1, 0))


def row_after(x):
    return jnp.where(iota(x.shape, 0) == x.shape[0] - 1, 0.0, pltpu.roll(x, x.shape[0] - 1, 0))


def solve_groups(gathered, groups, scale1, block):
    bricks = gathered.shape[0]
    lane = iota(gathered.shape, 1)
    slot = lane >> 4
    up = pltpu.roll(gathered, bricks - 1, 0)
    down = pltpu.roll(gathered, 1, 0)

    def pick(first):
        return lanes_sum(
            jnp.where(
                slot == first,
                up,
                jnp.where(slot == first + 1, gathered, jnp.where(slot == first + 2, down, 0.0)),
            )
        )

    filtered = pick(0)
    plain = pick(3)
    density_sum = lanes_sum(jnp.where(slot == 6, gathered, 0.0))
    remainder = plain + 2.0 * scale1 * filtered + scale1 * (row_before(filtered) + row_after(filtered))

    blocks = groups.shape[1]
    repeat = (iota((blocks, 128), 0) == (iota((blocks, 128), 1) & (blocks - 1))).astype(bf16)
    ids = jnp.dot(groups.astype(f32).astype(bf16), repeat, preferred_element_type=f32)
    diagonal_lane = (iota(gathered.shape, 0) & 7) == slot
    packed = jnp.where(diagonal_lane, ids, 0.0)
    member = [
        (ids == jnp.sum(packed[8 * j : 8 * j + 8], axis=0, keepdims=True)).astype(f32) for j in range(bricks // 8)
    ]

    def project(x):
        chosen = jnp.where(diagonal_lane, x, 0.0)
        total = jnp.zeros_like(x)
        for j in range(bricks // 8):
            total = total + member[j] * jnp.sum(chosen[8 * j : 8 * j + 8], axis=0, keepdims=True)
        return lanes_sum(total)

    place = iota(ids.shape, 0)
    as_before = jnp.where((place > 0) & (pltpu.roll(ids, 1, 0) == ids), 0.5, 0.0)
    as_after = jnp.where((place < bricks - 1) & (pltpu.roll(ids, bricks - 1, 0) == ids), 0.5, 0.0)
    inner = 2.0 * block - 1.0
    same = inner * inner * (1.0 + as_before + as_after)
    cells = float(block * block)
    diagonal = project(density_sum + scale1 * (16.0 * cells - 2.0 * same))
    group_rhs = project(remainder)
    column = lane & 3
    line = (lane >> 2) & 3
    center = density_sum + 16.0 * cells * scale1

    def image(g):
        z = inner * g + 0.5 * (
            jnp.where(column > 0, pltpu.roll(g, 1, 1), 0.0) + jnp.where(column < 3, pltpu.roll(g, 127, 1), 0.0)
        )
        y = inner * z + 0.5 * (
            jnp.where(line > 0, pltpu.roll(z, 4, 1), 0.0) + jnp.where(line < 3, pltpu.roll(z, 124, 1), 0.0)
        )
        return center * g - 2.0 * scale1 * (y + 0.5 * (row_before(y) + row_after(y)))

    factor = COARSE_WEIGHT / diagonal
    fix = factor * group_rhs
    for _ in range(COARSE_SWEEPS - 1):
        fix = fix + factor * (group_rhs - project(image(fix)))
    return fix


def solve_kernel(kappa, gathered, groups, spread, fixes):
    core, brick, _ = position()
    scale1 = 0.25 * kappa[0]
    half = spread.shape[1] // TILES
    block = half // TILES
    fixes[0:8, :] = jnp.zeros((8, 128), f32)
    count = gathered.shape[0]
    fixes[8 + count : 32 + count, :] = jnp.zeros((24, 128), f32)
    fixes[8 : 8 + count, :] = solve_groups(gathered[:, 0, :], groups[...], scale1, block)
    window = fixes[pl.ds(brick + 4, 16), :]
    turn = jnp.zeros_like(window)
    row = iota(window.shape, 0)
    for i in range(9):
        turn = jnp.where(row == i, window[8 - i : 9 - i], turn)
    window = jnp.where(core == 0, window, turn)
    lane = iota((128, TILES * half), 1)
    per = (lane >> (half.bit_length() - 1)) * 4 + ((lane & (half - 1)) >> (block.bit_length() - 1))
    spread[...] = dot_exact(window, (iota((128, TILES * half), 0) == per).astype(bf16))


def second_kernel(
    kappa, halo_lo_in, halo_hi_in, rhs, dens, s2_lo, s2_hi, near_f, sib_f, density1_sib, density1_own, send_a, sib, near, far, sib_near, sib_far, spread,
    to_b, s4, wd_last,
    cres, cden, c1, c2, c3, grown, s3, wd, halo, sems,
):
    core, brick, bricks = position()
    loads = [
        pltpu.make_async_copy(halo_lo_in, halo.at[pl.ds(0, 2)], sems.at[1]),
        pltpu.make_async_copy(halo_hi_in, halo.at[pl.ds(2, 2)], sems.at[2]),
    ]
    start_all(loads)
    half = cres.shape[1]
    height, width = rhs.shape[2:]
    block = half // TILES
    for ref in (c1, c2, c3, s3, s4):
        clear_edges(ref)
    scale = kappa[0]
    scale1 = 0.25 * scale

    for index, (ref, i), (ref_density, k) in (
        (1, (far, 0), (far, 1)),
        (2, (near, 2), (near, 3)),
        (3, (near, 0), (near, 1)),
        (4, (send_a, 0), (density1_own, 0)),
        (5, (sib, 0), (density1_sib, 0)),
        (6, (sib_near, 0), (sib_near, 1)),
        (7, (sib_near, 2), (sib_near, 3)),
        (8, (sib_far, 0), (sib_far, 1)),
    ):
        cres[index] = ref[i * half : (i + 1) * half, :]
        cden[index] = ref_density[k * half : (k + 1) * half, :]

    body = pl.ds(8, half)
    c1[0, body, :] = far[2 * half : 3 * half, :]
    for i in range(1, 9):
        place = brick + jnp.where(core == 0, i - 4, 4 - i)
        valid = ((place >= 0) & (place < bricks)).astype(f32)
        factor = (WEIGHT * valid) / (cden[i] + 14.0 * scale1)
        cden[i] = factor
        c1[i, body, :] = factor * cres[i]

    def relax(ref, i, k):
        v = ref[i, body, :]
        f = stencil(ref, i, 0, half)
        return (1.0 - WEIGHT) * v + cden[k] * (cres[k] + 2.0 * scale1 * (f - v))

    for i in range(7):
        value = relax(c1, i + 1, i + 1)
        row = spread[i + 1 : i + 2, :]
        pieces = [jnp.broadcast_to(row[:, t * half : (t + 1) * half], (block, half)) for t in range(TILES)]
        c2[i, body, :] = value + jnp.concatenate(pieces, 0)
    for i in range(5):
        c3[i, body, :] = relax(c2, i + 1, i + 2)
    columns = (iota((half, width), 0) == (iota((half, width), 1) >> 1)).astype(bf16)
    for i in range(3):
        fine = dot_exact(relax(c3, i + 1, i + 3), columns)
        put_halves(grown, i, pl.ds(0, half, stride=2), fine)
        put_halves(grown, i, pl.ds(1, half, stride=2), fine)

    wait_all(loads)
    inner = pl.ds(8, height)
    for k in range(2):
        side = slice(k * half, (k + 1) * half)
        s3[0, inner, side] = near_f[0, :, side] + grown[0, k]
        s3[1, inner, side] = s2_lo[0, :, side] + grown[0, k]
        s3[2, inner, side] = s2_lo[1, :, side] + grown[1, k]
        s3[3, inner, side] = s2_hi[0, inner, side] + grown[1, k]
        s3[4, inner, side] = s2_hi[1, inner, side] + grown[2, k]
        s3[5, inner, side] = sib_f[0, :, side] + grown[2, k]

    at_start = jnp.where(core == 0, brick > 0, brick < bricks - 1).astype(f32)
    at_end = jnp.where(core == 0, brick < bricks - 1, brick > 0).astype(f32)
    for j in range(4):

        def smooth(row, j=j):
            part = pl.ds(row, CHUNK)
            v = s3[j + 1, pl.ds(row + 8, CHUNK), :]
            f = stencil(s3, j + 1, row, CHUNK)
            if j in (1, 2):
                layer = core if j == 1 else 1 - core
                source, density, top = rhs[0, layer, part, :], dens[layer, part, :], WEIGHT
            else:
                edge = 2 * (j // 3)
                source, density = halo[edge, part, :], halo[edge + 1, part, :]
                top = WEIGHT * (at_end if edge else at_start)
            factor = top / (density + 14.0 * scale)
            wd[j, part, :] = factor
            new = (1.0 - WEIGHT) * v + factor * (source + 2.0 * scale * (f - v))
            s4[j, pl.ds(row + 8, CHUNK), :] = new

        chunks(height, smooth)
    to_b[0, height : height + 8, :] = jnp.zeros((8, width), f32)

    def smooth_last(row):
        part = pl.ds(row, CHUNK)
        v = s4[1, pl.ds(row + 8, CHUNK), :]
        f = stencil(s4, 1, row, CHUNK)
        to_b[0, part, :] = (1.0 - WEIGHT) * v + wd[1, part, :] * (rhs[0, core, part, :] + 2.0 * scale * (f - v))
        wd_last[part, :] = wd[2, part, :]

    chunks(height, smooth_last)


def inside_kernel(kappa, rhs, dens, to_b, s4, wd, to_a, sol_out, out, s, sems):
    core = position()[0]
    scale = kappa[0]
    height = dens.shape[1]
    inner = pl.ds(8, height)
    store_b = pltpu.make_async_copy(to_b.at[0, pl.ds(0, height)], sol_out.at[0, core], sems.at[1])
    store_b.start()
    clear_edges(s)
    s[0, inner, :] = to_b[0, :height, :]

    def smooth_last(row):
        part = pl.ds(row, CHUNK)
        v = s4[2, pl.ds(row + 8, CHUNK), :]
        f = stencil(s4, 2, row, CHUNK)
        new = (1.0 - WEIGHT) * v + wd[part, :] * (rhs[0, 1 - core, part, :] + 2.0 * scale * (f - v))
        to_a[0, part, :] = new
        s[1, pl.ds(row + 8, CHUNK), :] = new

    chunks(height, smooth_last)
    store_a = pltpu.make_async_copy(to_a.at[0], sol_out.at[0, 1 - core], sems.at[2])
    store_a.start()
    for j, layer in ((0, core), (1, 1 - core)):

        def finish(row, j=j, layer=layer):
            part = pl.ds(row, CHUNK)
            more = pl.ds(row, CHUNK + 16)
            f = filter_yz(s[j, more, :] + 0.5 * s[1 - j, more, :])
            center = dens[layer, part, :] + 16.0 * scale
            out[layer, part, :] = rhs[0, layer, part, :] - center * s[j, pl.ds(row + 8, CHUNK), :] + 2.0 * scale * f

        chunks(height, finish)
    store_b.wait()
    store_a.wait()


def residual_kernel(kappa, inside, halo_a, halo_b, out, s, done, sems):
    core = position()[0]
    height = inside.shape[1]
    inner = pl.ds(8, height)
    clear_edges(s)
    s[core, inner, :] = halo_b[0, :height, :]
    s[1 - core, inner, :] = halo_a[0]
    scale = kappa[0]
    stores = []
    for j in range(2):

        def finish(row, j=j):
            part = pl.ds(row, CHUNK)
            done[j, part, :] = inside[j, part, :] + scale * filter_yz(s[j, pl.ds(row, CHUNK + 16), :])

        chunks(height, finish)
        stores.append(pltpu.make_async_copy(done.at[j], out.at[0, j], sems.at[1 + j]))
        stores[-1].start()
    wait_all(stores)


def shape(*dims):
    return jax.ShapeDtypeStruct(dims, f32)


def local(rhs, density, kappa, block_group):
    bricks = lax.axis_size("brick")
    species = lax.axis_size("spec")
    height, width = rhs.shape[2:]
    half = height // 2
    in_chip = [(i, i ^ 1) for i in range(bricks)]
    next_chip = [(i, ((i + 1) ^ 1) - 1) for i in range(1, bricks - 1)]
    second_chip = [(i, i - 3) for i in range(4, bricks, 2)] + [(i, i + 3) for i in range(1, bricks - 3, 2)]

    def swap_a(x):
        return lax.ppermute(x, "brick", in_chip)

    def swap_b(x):
        return lax.ppermute(x, "brick", next_chip)

    def swap_far(x):
        return lax.ppermute(x, "brick", second_chip)

    def around(x, k):
        return lax.ppermute(x, "spec", [(i, (i + k) % species) for i in range(species)])

    pieces = [around(density, k) for k in (1, 2, 3)]
    rhs_b = swap_b(rhs)
    rhs_a = swap_a(rhs)
    dens = pl.pallas_call(
        gather_kernel,
        out_shape=shape(2, height, width),
        in_specs=[HBM] + [VM] * 3,
        out_specs=VM,
        scratch_shapes=[pltpu.SemaphoreType.DMA((1,))],
        compiler_params=PARAMS,
        name="collect_density",
    )(pltpu.with_memory_space_constraint(density, pltpu.HBM), *pieces)

    dens_b = swap_b(dens)
    dens_a = swap_a(dens)
    s1_own, s2_hi, wd_own, halo_hi, density1_own, density1_sib, send_b = pl.pallas_call(
        near_kernel,
        out_shape=(
            shape(2, height + 16, width),
            shape(2, height + 16, width),
            shape(height, width),
            pltpu.HBM((2, height, width), f32),
            shape(half, half),
            shape(half, half),
            shape(1, height, width),
        ),
        in_specs=[SM] + [VM] * 4 + [ANY],
        out_specs=[VM, VM, VM, HBM, VM, VM, VM],
        scratch_shapes=[
            pltpu.VMEM((4, height + 16, width), f32),
            pltpu.VMEM((3, height, width), f32),
            pltpu.VMEM((2, 2, height, half), f32),
            pltpu.SemaphoreType.DMA((3,)),
        ],
        compiler_params=PARAMS,
        name="smooth_in_chip",
    )(kappa, rhs, dens, rhs_a, dens_a, rhs_b)
    near_f = swap_b(send_b)
    s2_lo, halo_lo, send_a, send_f, payload = pl.pallas_call(
        first_kernel,
        out_shape=(
            shape(2, height, width),
            pltpu.HBM((2, height, width), f32),
            shape(2 * half, half),
            pltpu.HBM((1, height, width), f32),
            shape(bricks, 5, 128),
        ),
        in_specs=[SM] + [VM] * 9,
        out_specs=[VM, HBM, VM, HBM, VM],
        scratch_shapes=[
            pltpu.VMEM((4, height + 16, width), f32),
            pltpu.VMEM((4, height + 16, width), f32),
            pltpu.VMEM((1, height, width), f32),
            pltpu.VMEM((2, 2, height, half), f32),
            pltpu.SemaphoreType.DMA((3,)),
        ],
        compiler_params=PARAMS,
        name="smooth_and_restrict",
    )(kappa, rhs, dens, rhs_b, dens_b, s1_own, s2_hi, wd_own, density1_own, density1_sib)

    gathered = lax.all_to_all(payload, "brick", 0, 0, tiled=True)
    sib = swap_a(send_a)
    sib_f = swap_a(send_f)
    near_out, far_out = pl.pallas_call(
        join_kernel,
        out_shape=(shape(4 * half, half), shape(3 * half, half)),
        in_specs=[VM] * 4 + [ANY],
        out_specs=[VM] * 2,
        compiler_params=PARAMS,
        name="join_chip",
    )(send_a, sib, density1_sib, density1_own, near_f)
    near = swap_b(near_out)
    far = swap_far(far_out)
    half_lanes = TILES * half
    spread = pl.pallas_call(
        solve_kernel,
        out_shape=shape(16, half_lanes),
        in_specs=[SM] + [VM] * 2,
        out_specs=VM,
        scratch_shapes=[pltpu.VMEM((bricks + 32, 128), f32)],
        compiler_params=PARAMS,
        name="solve_aggregates",
    )(kappa, gathered, block_group)
    near, far, spread = lax.optimization_barrier((near, far, spread))
    sib_near = swap_a(near)
    sib_far = swap_a(far)

    in_hbm = functools.partial(pltpu.with_memory_space_constraint, memory_space=pltpu.HBM)
    to_b, s4, wd_last = pl.pallas_call(
        second_kernel,
        out_shape=(shape(1, height + 8, width), shape(4, height + 16, width), shape(height, width)),
        in_specs=[SM, HBM, HBM] + [VM] * 15,
        out_specs=[VM] * 3,
        scratch_shapes=[
            pltpu.VMEM((9, half, half), f32),
            pltpu.VMEM((9, half, half), f32),
            pltpu.VMEM((9, half + 16, half), f32),
            pltpu.VMEM((7, half + 16, half), f32),
            pltpu.VMEM((5, half + 16, half), f32),
            pltpu.VMEM((3, 2, height, half), f32),
            pltpu.VMEM((6, height + 16, width), f32),
            pltpu.VMEM((4, height, width), f32),
            pltpu.VMEM((4, height, width), f32),
            pltpu.SemaphoreType.DMA((3,)),
        ],
        compiler_params=PARAMS,
        name="correct_and_smooth",
    )(
        kappa, in_hbm(halo_lo), in_hbm(halo_hi), rhs, dens, s2_lo, s2_hi, near_f, sib_f, density1_sib, density1_own, send_a,
        sib, near, far, sib_near, sib_far, spread
    )

    halo_b = swap_b(to_b)
    to_a, solution, inside = pl.pallas_call(
        inside_kernel,
        out_shape=(shape(1, height, width), shape(1, 2, height, width), shape(2, height, width)),
        in_specs=[SM] + [VM] * 5,
        out_specs=[VM, ANY, VM],
        scratch_shapes=[
            pltpu.VMEM((2, height + 16, width), f32),
            pltpu.SemaphoreType.DMA((3,)),
        ],
        compiler_params=PARAMS,
        name="residual_inside",
    )(kappa, rhs, dens, to_b, s4, wd_last)
    halo_a = swap_a(to_a)
    residual = pl.pallas_call(
        residual_kernel,
        out_shape=shape(1, 2, height, width),
        in_specs=[SM] + [VM] * 3,
        out_specs=ANY,
        scratch_shapes=[
            pltpu.VMEM((2, height + 16, width), f32),
            pltpu.VMEM((2, height, width), f32),
            pltpu.SemaphoreType.DMA((3,)),
        ],
        compiler_params=PARAMS,
        name="residual",
    )(kappa, inside, halo_a, halo_b)
    return (solution, residual)


def solution(mesh):
    return jax.shard_map(
        local,
        mesh=mesh,
        in_specs=(P("spec", "brick", None, None), P("brick", "spec", None), P("spec"), P()),
        out_specs=(P("spec", "brick", None, None), P("spec", "brick", None, None)),
        check_vma=False,
    )
```

```python
import functools

import jax
import jax.numpy as jnp
from jax import lax
from jax.experimental import pallas as pl
from jax.experimental.pallas import tpu as pltpu
from jax.sharding import PartitionSpec as P

WEIGHT = 0.85
COARSE_WEIGHT = 0.6
COARSE_SWEEPS = 3
TILES = 4
CHUNK = 64
f32 = jnp.float32
bf16 = jnp.bfloat16
VM = pl.BlockSpec(memory_space=pltpu.VMEM)
ANY = pl.BlockSpec(memory_space=pl.ANY)
SM = pl.BlockSpec(memory_space=pltpu.SMEM)
HBM = pl.BlockSpec(memory_space=pltpu.HBM)
PARAMS = pltpu.CompilerParams(vmem_limit_bytes=16 * 1024 * 1024)


def iota(shape, dim):
    return lax.broadcasted_iota(jnp.int32, shape, dim)


def split(x):
    high = x.astype(bf16)
    rest = x - high.astype(f32)
    middle = rest.astype(bf16)
    low = (rest - middle.astype(f32)).astype(bf16)
    return high, middle, low


def dot_exact(x, w):
    high, middle, low = split(x)
    dot = functools.partial(jnp.dot, preferred_element_type=f32)
    return dot(high, w) + (dot(middle, w) + dot(low, w))


def filter_z(y):
    width = y.shape[1]
    lane = iota((1, width), 1)
    before = jnp.where(lane == 0, 0.0, 0.5)
    after = jnp.where(lane == width - 1, 0.0, 0.5)
    return y + before * pltpu.roll(y, 1, 1) + after * pltpu.roll(y, width - 1, 1)


def filter_yz(m):
    rows = m.shape[0]
    y = m + 0.5 * (pltpu.roll(m, 1, 0) + pltpu.roll(m, rows - 1, 0))
    return filter_z(y[8 : rows - 8])


def stencil(ref, i, row, rows):
    part = pl.ds(row, rows + 16)
    return filter_yz(ref[i, part, :] + 0.5 * (ref[i - 1, part, :] + ref[i + 1, part, :]))


def clear_edges(ref):
    layers, rows, width = ref.shape
    zero = jnp.zeros((layers, 8, width), f32)
    ref[:, 0:8, :] = zero
    ref[:, rows - 8 : rows, :] = zero


def chunks(rows, body):
    for row in range(0, rows, CHUNK):
        body(row)


def coarsen_z(rows, width):
    return ((iota((width, width // 2), 0) >> 1) == iota((width, width // 2), 1)).astype(bf16)


def put_halves(ref, i, part, x):
    half = x.shape[1] // 2
    ref[i, 0, part, :] = x[:, :half]
    ref[i, 1, part, :] = x[:, half:]


def pair_rows(ref, i, half):
    even, odd = pl.ds(0, half, stride=2), pl.ds(1, half, stride=2)
    return jnp.concatenate([ref[i, k, even, :] + ref[i, k, odd, :] for k in range(2)], 1)


def position():
    brick = lax.axis_index("brick")
    return brick & 1, brick, lax.axis_size("brick")


def start_all(copies):
    for copy in copies:
        copy.start()


def wait_all(copies):
    for copy in copies:
        copy.wait()


def join_kernel(mine, other, density1_sib, density1_own, near_f, near, far):
    del near_f
    half = near.shape[0] // 3
    parts = [pl.ds(i * half, half) for i in range(4)]
    near[parts[0], :] = mine[parts[0], :]
    near[parts[1], :] = other[parts[0], :]
    near[parts[2], :] = density1_sib[...]
    far[parts[0], :] = mine[parts[0], :]
    far[parts[1], :] = density1_own[...]
    far[parts[2], :] = other[parts[1], :]


def gather_kernel(shard, p1, p2, p3, dens, sems):
    count = 4
    rows = shard.shape[1]

    def place(k):
        owner = lax.rem(lax.axis_index("spec") - k + count, count)
        return pl.ds(pl.multiple_of(owner * rows, rows), rows)

    own = pltpu.make_async_copy(shard, dens.at[:, place(0), :], sems.at[0])
    own.start()
    for k, piece in ((1, p1), (2, p2), (3, p3)):
        dens[:, place(k), :] = piece[...]
    own.wait()


def begin_layers(source, density, layers, work, index, wd, s1, scale, top, keep):
    height = density.shape[1]

    def begin(row):
        part = pl.ds(row, CHUNK)
        pair = density[0, part, :] + density[1, part, :]
        put_halves(work, index, part, pair)
        for layer, slot in layers:
            factor = top / (density[layer, part, :] + 14.0 * scale)
            if slot in keep:
                wd[keep[slot], part, :] = factor
            s1[slot, pl.ds(row + 8, CHUNK), :] = factor * source[0, layer, part, :]

    chunks(height, begin)


def near_kernel(
    kappa, rhs, dens, rhs_a, dens_a, rhs_b,
    s1_own, s2_hi, wd_own, halo_out, density1_own, density1_sib, send_b,
    s1, wd, work, sems,
):
    del rhs_b
    core, brick, bricks = position()
    stores = [
        pltpu.make_async_copy(rhs_a.at[0, core], halo_out.at[0], sems.at[1]),
        pltpu.make_async_copy(dens_a.at[core], halo_out.at[1], sems.at[2]),
    ]
    start_all(stores)
    height, width = dens.shape[1:]
    half = height // 2
    clear_edges(s1)
    clear_edges(s2_hi)
    scale = kappa[0]
    valid = jnp.where(core == 0, brick < bricks - 1, brick > 0).astype(f32)
    begin_layers(rhs, dens, ((core, 0), (1 - core, 1)), work, 0, wd, s1, scale, WEIGHT, {0: 0, 1: 1})
    begin_layers(rhs_a, dens_a, ((core, 2), (1 - core, 3)), work, 1, wd, s1, scale, WEIGHT * valid, {2: 2})
    for j in (1, 2):

        def smooth(row, j=j):
            part = pl.ds(row, CHUNK)
            v = s1[j, pl.ds(row + 8, CHUNK), :]
            f = stencil(s1, j, row, CHUNK)
            source = rhs[0, 1 - core, part, :] if j == 1 else rhs_a[0, core, part, :]
            new = (1.0 - WEIGHT) * v + wd[j, part, :] * (source + 2.0 * scale * (f - v))
            s2_hi[j - 1, pl.ds(row + 8, CHUNK), :] = new
            if j == 1:
                send_b[0, part, :] = new

        chunks(height, smooth)
    s1_own[...] = s1[0:2]
    wd_own[...] = wd[0]
    columns = coarsen_z(height, width)
    density1_own[...] = 0.125 * dot_exact(pair_rows(work, 0, half), columns)
    density1_sib[...] = 0.125 * dot_exact(pair_rows(work, 1, half), columns)
    wait_all(stores)


def first_kernel(
    kappa, rhs, dens, rhs_b, dens_b, s1_own, s2_hi, wd_own, density1_own, density1_sib,
    s2_lo, halo_out, send_a, send_f, payload,
    s1, s2, wd, work, sems,
):
    core, brick, bricks = position()
    stores = [
        pltpu.make_async_copy(rhs_b.at[0, 1 - core], halo_out.at[0], sems.at[1]),
        pltpu.make_async_copy(dens_b.at[1 - core], halo_out.at[1], sems.at[2]),
    ]
    start_all(stores)
    height, width = dens.shape[1:]
    half = height // 2
    clear_edges(s1)
    clear_edges(s2)
    s1[2:4] = s1_own[...]
    s2[2:4] = s2_hi[...]
    scale = kappa[0]
    scale1 = 0.25 * scale
    valid_lo = jnp.where(core == 0, brick > 0, brick < bricks - 1).astype(f32)
    valid_hi = jnp.where(core == 0, brick < bricks - 1, brick > 0).astype(f32)
    begin_layers(rhs_b, dens_b, ((core, 0), (1 - core, 1)), work, 0, wd, s1, scale, WEIGHT * valid_lo, {1: 0})

    for j in (1, 2):

        def smooth(row, j=j):
            part = pl.ds(row, CHUNK)
            v = s1[j, pl.ds(row + 8, CHUNK), :]
            f = stencil(s1, j, row, CHUNK)
            source, factor = (rhs_b[0, 1 - core, part, :], wd[0, part, :]) if j == 1 else (rhs[0, core, part, :], wd_own[part, :])
            new = (1.0 - WEIGHT) * v + factor * (source + 2.0 * scale * (f - v))
            s2[j - 1, pl.ds(row + 8, CHUNK), :] = new
            s2_lo[j - 1, part, :] = new

        chunks(height, smooth)

    def restrict(row):
        part = pl.ds(row, CHUNK)
        total = jnp.zeros((CHUNK, width), f32)
        for slot, layer in ((1, core), (2, 1 - core)):
            v = s2[slot, pl.ds(row + 8, CHUNK), :]
            f = stencil(s2, slot, row, CHUNK)
            center = dens[layer, part, :] + 16.0 * scale
            total = total + (rhs[0, layer, part, :] - center * v + 2.0 * scale * f)
        put_halves(work, 1, part, total)

    chunks(height, restrict)
    columns = coarsen_z(height, width)
    density1 = [0.125 * dot_exact(pair_rows(work, 0, half), columns), density1_own[...], density1_sib[...]]
    coarse_res = 0.125 * dot_exact(pair_rows(work, 1, half), columns)

    send_a[0:half, :] = coarse_res
    stores.append(pltpu.make_async_copy(s2.at[1, pl.ds(8, height), :], send_f.at[0], sems.at[0]))
    stores[-1].start()

    first = WEIGHT * coarse_res / (density1[1] + 14.0 * scale1)
    send_a[half : 2 * half, :] = first
    send_a[2 * half : 3 * half, :] = density1[0]
    pad = jnp.zeros((8, half), f32)
    spread = filter_yz(jnp.concatenate([pad, first, pad], 0))
    own_factor = WEIGHT / (density1[1] + 14.0 * scale1)
    shares = [
        (WEIGHT * valid_lo) * scale1 / (density1[0] + 14.0 * scale1) * spread,
        (1.0 - WEIGHT) * first + own_factor * (coarse_res + 2.0 * scale1 * (spread - first)),
        (WEIGHT * valid_hi) * scale1 / (density1[2] + 14.0 * scale1) * spread,
    ]
    block = half // TILES
    filtered = []
    plain = []
    for e, share in enumerate(shares):
        rest = -(density1[e] + 16.0 * scale1) * share
        if e == 1:
            rest = rest + coarse_res
        for t in range(TILES):
            at = t * block
            row = 2.0 * jnp.sum(share[at : at + block], axis=0, keepdims=True)
            row = row - 0.5 * (share[at : at + 1] + share[at + block - 1 : at + block])
            if t > 0:
                row = row + 0.5 * share[at - 1 : at]
            if t < TILES - 1:
                row = row + 0.5 * share[at + block : at + block + 1]
            filtered.append(row)
            plain.append(jnp.sum(rest[at : at + block], axis=0, keepdims=True))
    for t in range(TILES):
        plain.append(jnp.sum(density1[1][t * block : (t + 1) * block], axis=0, keepdims=True))
    for rows in (filtered, plain):
        for t in range(TILES):
            low, high = rows[t], rows[2 * TILES + t]
            rows[t] = jnp.where(core == 0, low, high)
            rows[2 * TILES + t] = jnp.where(core == 0, high, low)
    filtered.append(jnp.zeros((4, half), f32))
    filtered = jnp.concatenate(filtered, 0)
    plain = jnp.concatenate(plain, 0)
    cell = iota((half, 128), 0)
    tile = iota((half, 128), 1) & 3
    start = tile * block
    inside = ((cell >= start) & (cell < start + block)).astype(f32)
    ends = ((cell == start) | (cell == start + block - 1)).astype(f32)
    beside = ((cell == start - 1) | (cell == start + block)).astype(f32)
    plain_w = inside.astype(bf16)
    filter_w = (2.0 * inside - 0.5 * ends + 0.5 * beside).astype(bf16)
    row = iota((16, 128), 0)
    lane = iota((16, 128), 1)
    fits = ((lane >> 2) & 3) == (row & 3)
    out = jnp.where(fits & ((lane >> 4) == (row >> 2)), dot_exact(filtered, filter_w), 0.0)
    out = jnp.where(row >= 12, 0.0, out)
    out = out + jnp.where(fits & ((lane >> 4) == (row >> 2) + 3), dot_exact(plain, plain_w), 0.0)
    payload[...] = jnp.broadcast_to(jnp.sum(out, axis=0, keepdims=True)[None], payload.shape)
    wait_all(stores)


def lanes_sum(x):
    for step in (16, 32, 64):
        x = x + pltpu.roll(x, step, 1)
    return x


def row_before(x):
    return jnp.where(iota(x.shape, 0) == 0, 0.0, pltpu.roll(x, 1, 0))


def row_after(x):
    return jnp.where(iota(x.shape, 0) == x.shape[0] - 1, 0.0, pltpu.roll(x, x.shape[0] - 1, 0))


def solve_groups(gathered, groups, scale1, block):
    bricks = gathered.shape[0]
    lane = iota(gathered.shape, 1)
    slot = lane >> 4
    up = pltpu.roll(gathered, bricks - 1, 0)
    down = pltpu.roll(gathered, 1, 0)

    def pick(first):
        return lanes_sum(
            jnp.where(
                slot == first,
                up,
                jnp.where(slot == first + 1, gathered, jnp.where(slot == first + 2, down, 0.0)),
            )
        )

    filtered = pick(0)
    plain = pick(3)
    density_sum = lanes_sum(jnp.where(slot == 6, gathered, 0.0))
    remainder = plain + 2.0 * scale1 * filtered + scale1 * (row_before(filtered) + row_after(filtered))

    blocks = groups.shape[1]
    repeat = (iota((blocks, 128), 0) == (iota((blocks, 128), 1) & (blocks - 1))).astype(bf16)
    ids = jnp.dot(groups.astype(f32).astype(bf16), repeat, preferred_element_type=f32)
    diagonal_lane = (iota(gathered.shape, 0) & 7) == slot
    packed = jnp.where(diagonal_lane, ids, 0.0)
    member = [
        (ids == jnp.sum(packed[8 * j : 8 * j + 8], axis=0, keepdims=True)).astype(f32) for j in range(bricks // 8)
    ]

    def project(x):
        chosen = jnp.where(diagonal_lane, x, 0.0)
        total = jnp.zeros_like(x)
        for j in range(bricks // 8):
            total = total + member[j] * jnp.sum(chosen[8 * j : 8 * j + 8], axis=0, keepdims=True)
        return lanes_sum(total)

    place = iota(ids.shape, 0)
    as_before = jnp.where((place > 0) & (pltpu.roll(ids, 1, 0) == ids), 0.5, 0.0)
    as_after = jnp.where((place < bricks - 1) & (pltpu.roll(ids, bricks - 1, 0) == ids), 0.5, 0.0)
    inner = 2.0 * block - 1.0
    same = inner * inner * (1.0 + as_before + as_after)
    cells = float(block * block)
    diagonal = project(density_sum + scale1 * (16.0 * cells - 2.0 * same))
    group_rhs = project(remainder)
    column = lane & 3
    line = (lane >> 2) & 3
    center = density_sum + 16.0 * cells * scale1

    def image(g):
        z = inner * g + 0.5 * (
            jnp.where(column > 0, pltpu.roll(g, 1, 1), 0.0) + jnp.where(column < 3, pltpu.roll(g, 127, 1), 0.0)
        )
        y = inner * z + 0.5 * (
            jnp.where(line > 0, pltpu.roll(z, 4, 1), 0.0) + jnp.where(line < 3, pltpu.roll(z, 124, 1), 0.0)
        )
        return center * g - 2.0 * scale1 * (y + 0.5 * (row_before(y) + row_after(y)))

    factor = COARSE_WEIGHT / diagonal
    fix = factor * group_rhs
    for _ in range(COARSE_SWEEPS - 1):
        fix = fix + factor * (group_rhs - project(image(fix)))
    return fix


def solve_kernel(kappa, gathered, groups, spread, fixes):
    core, brick, _ = position()
    scale1 = 0.25 * kappa[0]
    half = spread.shape[1] // TILES
    block = half // TILES
    fixes[0:8, :] = jnp.zeros((8, 128), f32)
    count = gathered.shape[0]
    fixes[8 + count : 32 + count, :] = jnp.zeros((24, 128), f32)
    fixes[8 : 8 + count, :] = solve_groups(gathered[:, 0, :], groups[...], scale1, block)
    window = fixes[pl.ds(brick + 4, 16), :]
    turn = jnp.zeros_like(window)
    row = iota(window.shape, 0)
    for i in range(9):
        turn = jnp.where(row == i, window[8 - i : 9 - i], turn)
    window = jnp.where(core == 0, window, turn)
    lane = iota((128, TILES * half), 1)
    per = (lane >> (half.bit_length() - 1)) * 4 + ((lane & (half - 1)) >> (block.bit_length() - 1))
    spread[...] = dot_exact(window, (iota((128, TILES * half), 0) == per).astype(bf16))


def second_kernel(
    kappa, halo_lo_in, halo_hi_in, rhs, dens, s2_lo, s2_hi, near_f, sib_f, density1_sib, density1_own, send_a, sib, near, far, sib_near, sib_far, spread,
    to_b, s4, wd_last,
    cres, cden, c1, c2, c3, grown, s3, wd, halo, sems,
):
    core, brick, bricks = position()
    loads = [
        pltpu.make_async_copy(halo_lo_in, halo.at[pl.ds(0, 2)], sems.at[1]),
        pltpu.make_async_copy(halo_hi_in, halo.at[pl.ds(2, 2)], sems.at[2]),
    ]
    start_all(loads)
    half = cres.shape[1]
    height, width = rhs.shape[2:]
    block = half // TILES
    for ref in (c1, c2, c3, s3, s4):
        clear_edges(ref)
    scale = kappa[0]
    scale1 = 0.25 * scale

    for index, (ref, i), (ref_density, k) in (
        (1, (far, 0), (far, 1)),
        (2, (near, 1), (near, 2)),
        (3, (near, 0), (send_a, 2)),
        (4, (send_a, 0), (density1_own, 0)),
        (5, (sib, 0), (density1_sib, 0)),
        (6, (sib_near, 0), (sib, 2)),
        (7, (sib_near, 1), (sib_near, 2)),
        (8, (sib_far, 0), (sib_far, 1)),
    ):
        cres[index] = ref[i * half : (i + 1) * half, :]
        cden[index] = ref_density[k * half : (k + 1) * half, :]

    body = pl.ds(8, half)
    c1[0, body, :] = far[2 * half : 3 * half, :]
    for i in range(1, 9):
        place = brick + jnp.where(core == 0, i - 4, 4 - i)
        valid = ((place >= 0) & (place < bricks)).astype(f32)
        factor = (WEIGHT * valid) / (cden[i] + 14.0 * scale1)
        cden[i] = factor
        c1[i, body, :] = factor * cres[i]

    def relax(ref, i, k):
        v = ref[i, body, :]
        f = stencil(ref, i, 0, half)
        return (1.0 - WEIGHT) * v + cden[k] * (cres[k] + 2.0 * scale1 * (f - v))

    for i in range(7):
        value = relax(c1, i + 1, i + 1)
        row = spread[i + 1 : i + 2, :]
        pieces = [jnp.broadcast_to(row[:, t * half : (t + 1) * half], (block, half)) for t in range(TILES)]
        c2[i, body, :] = value + jnp.concatenate(pieces, 0)
    for i in range(5):
        c3[i, body, :] = relax(c2, i + 1, i + 2)
    columns = (iota((half, width), 0) == (iota((half, width), 1) >> 1)).astype(bf16)
    for i in range(3):
        fine = dot_exact(relax(c3, i + 1, i + 3), columns)
        put_halves(grown, i, pl.ds(0, half, stride=2), fine)
        put_halves(grown, i, pl.ds(1, half, stride=2), fine)

    wait_all(loads)
    inner = pl.ds(8, height)
    for k in range(2):
        side = slice(k * half, (k + 1) * half)
        s3[0, inner, side] = near_f[0, :, side] + grown[0, k]
        s3[1, inner, side] = s2_lo[0, :, side] + grown[0, k]
        s3[2, inner, side] = s2_lo[1, :, side] + grown[1, k]
        s3[3, inner, side] = s2_hi[0, inner, side] + grown[1, k]
        s3[4, inner, side] = s2_hi[1, inner, side] + grown[2, k]
        s3[5, inner, side] = sib_f[0, :, side] + grown[2, k]

    at_start = jnp.where(core == 0, brick > 0, brick < bricks - 1).astype(f32)
    at_end = jnp.where(core == 0, brick < bricks - 1, brick > 0).astype(f32)
    for j in range(4):

        def smooth(row, j=j):
            part = pl.ds(row, CHUNK)
            v = s3[j + 1, pl.ds(row + 8, CHUNK), :]
            f = stencil(s3, j + 1, row, CHUNK)
            if j in (1, 2):
                layer = core if j == 1 else 1 - core
                source, density, top = rhs[0, layer, part, :], dens[layer, part, :], WEIGHT
            else:
                edge = 2 * (j // 3)
                source, density = halo[edge, part, :], halo[edge + 1, part, :]
                top = WEIGHT * (at_end if edge else at_start)
            factor = top / (density + 14.0 * scale)
            wd[j, part, :] = factor
            new = (1.0 - WEIGHT) * v + factor * (source + 2.0 * scale * (f - v))
            s4[j, pl.ds(row + 8, CHUNK), :] = new

        chunks(height, smooth)
    to_b[0, height : height + 8, :] = jnp.zeros((8, width), f32)

    def smooth_last(row):
        part = pl.ds(row, CHUNK)
        v = s4[1, pl.ds(row + 8, CHUNK), :]
        f = stencil(s4, 1, row, CHUNK)
        to_b[0, part, :] = (1.0 - WEIGHT) * v + wd[1, part, :] * (rhs[0, core, part, :] + 2.0 * scale * (f - v))
        wd_last[part, :] = wd[2, part, :]

    chunks(height, smooth_last)


def inside_kernel(kappa, rhs, dens, to_b, s4, wd, to_a, sol_out, out, s, sems):
    core = position()[0]
    scale = kappa[0]
    height = dens.shape[1]
    inner = pl.ds(8, height)
    store_b = pltpu.make_async_copy(to_b.at[0, pl.ds(0, height)], sol_out.at[0, core], sems.at[1])
    store_b.start()
    clear_edges(s)
    s[0, inner, :] = to_b[0, :height, :]

    def smooth_last(row):
        part = pl.ds(row, CHUNK)
        v = s4[2, pl.ds(row + 8, CHUNK), :]
        f = stencil(s4, 2, row, CHUNK)
        new = (1.0 - WEIGHT) * v + wd[part, :] * (rhs[0, 1 - core, part, :] + 2.0 * scale * (f - v))
        to_a[0, part, :] = new
        s[1, pl.ds(row + 8, CHUNK), :] = new

    chunks(height, smooth_last)
    store_a = pltpu.make_async_copy(to_a.at[0], sol_out.at[0, 1 - core], sems.at[2])
    store_a.start()
    for j, layer in ((0, core), (1, 1 - core)):

        def finish(row, j=j, layer=layer):
            part = pl.ds(row, CHUNK)
            more = pl.ds(row, CHUNK + 16)
            f = filter_yz(s[j, more, :] + 0.5 * s[1 - j, more, :])
            center = dens[layer, part, :] + 16.0 * scale
            out[layer, part, :] = rhs[0, layer, part, :] - center * s[j, pl.ds(row + 8, CHUNK), :] + 2.0 * scale * f

        chunks(height, finish)
    store_b.wait()
    store_a.wait()


def residual_kernel(kappa, inside, halo_a, halo_b, out, s, done, sems):
    core = position()[0]
    height = inside.shape[1]
    inner = pl.ds(8, height)
    clear_edges(s)
    s[core, inner, :] = halo_b[0, :height, :]
    s[1 - core, inner, :] = halo_a[0]
    scale = kappa[0]
    stores = []
    for j in range(2):

        def finish(row, j=j):
            part = pl.ds(row, CHUNK)
            done[j, part, :] = inside[j, part, :] + scale * filter_yz(s[j, pl.ds(row, CHUNK + 16), :])

        chunks(height, finish)
        stores.append(pltpu.make_async_copy(done.at[j], out.at[0, j], sems.at[1 + j]))
        stores[-1].start()
    wait_all(stores)


def shape(*dims):
    return jax.ShapeDtypeStruct(dims, f32)


def local(rhs, density, kappa, block_group):
    bricks = lax.axis_size("brick")
    species = lax.axis_size("spec")
    height, width = rhs.shape[2:]
    half = height // 2
    in_chip = [(i, i ^ 1) for i in range(bricks)]
    next_chip = [(i, ((i + 1) ^ 1) - 1) for i in range(1, bricks - 1)]
    second_chip = [(i, i - 3) for i in range(4, bricks, 2)] + [(i, i + 3) for i in range(1, bricks - 3, 2)]

    def swap_a(x):
        return lax.ppermute(x, "brick", in_chip)

    def swap_b(x):
        return lax.ppermute(x, "brick", next_chip)

    def swap_far(x):
        return lax.ppermute(x, "brick", second_chip)

    def around(x, k):
        return lax.ppermute(x, "spec", [(i, (i + k) % species) for i in range(species)])

    pieces = [around(density, k) for k in (1, 2, 3)]
    rhs_b = swap_b(rhs)
    rhs_a = swap_a(rhs)
    dens = pl.pallas_call(
        gather_kernel,
        out_shape=shape(2, height, width),
        in_specs=[HBM] + [VM] * 3,
        out_specs=VM,
        scratch_shapes=[pltpu.SemaphoreType.DMA((1,))],
        compiler_params=PARAMS,
        name="collect_density",
    )(pltpu.with_memory_space_constraint(density, pltpu.HBM), *pieces)

    dens_b = swap_b(dens)
    dens_a = swap_a(dens)
    s1_own, s2_hi, wd_own, halo_hi, density1_own, density1_sib, send_b = pl.pallas_call(
        near_kernel,
        out_shape=(
            shape(2, height + 16, width),
            shape(2, height + 16, width),
            shape(height, width),
            pltpu.HBM((2, height, width), f32),
            shape(half, half),
            shape(half, half),
            shape(1, height, width),
        ),
        in_specs=[SM] + [VM] * 4 + [ANY],
        out_specs=[VM, VM, VM, HBM, VM, VM, VM],
        scratch_shapes=[
            pltpu.VMEM((4, height + 16, width), f32),
            pltpu.VMEM((3, height, width), f32),
            pltpu.VMEM((2, 2, height, half), f32),
            pltpu.SemaphoreType.DMA((3,)),
        ],
        compiler_params=PARAMS,
        name="smooth_in_chip",
    )(kappa, rhs, dens, rhs_a, dens_a, rhs_b)
    near_f = swap_b(send_b)
    s2_lo, halo_lo, send_a, send_f, payload = pl.pallas_call(
        first_kernel,
        out_shape=(
            shape(2, height, width),
            pltpu.HBM((2, height, width), f32),
            shape(3 * half, half),
            pltpu.HBM((1, height, width), f32),
            shape(bricks, 5, 128),
        ),
        in_specs=[SM] + [VM] * 9,
        out_specs=[VM, HBM, VM, HBM, VM],
        scratch_shapes=[
            pltpu.VMEM((4, height + 16, width), f32),
            pltpu.VMEM((4, height + 16, width), f32),
            pltpu.VMEM((1, height, width), f32),
            pltpu.VMEM((2, 2, height, half), f32),
            pltpu.SemaphoreType.DMA((3,)),
        ],
        compiler_params=PARAMS,
        name="smooth_and_restrict",
    )(kappa, rhs, dens, rhs_b, dens_b, s1_own, s2_hi, wd_own, density1_own, density1_sib)

    gathered = lax.all_to_all(payload, "brick", 0, 0, tiled=True)
    sib = swap_a(send_a)
    sib_f = swap_a(send_f)
    near_out, far_out = pl.pallas_call(
        join_kernel,
        out_shape=(shape(3 * half, half), shape(3 * half, half)),
        in_specs=[VM] * 4 + [ANY],
        out_specs=[VM] * 2,
        compiler_params=PARAMS,
        name="join_chip",
    )(send_a, sib, density1_sib, density1_own, near_f)
    near = swap_b(near_out)
    far = swap_far(far_out)
    half_lanes = TILES * half
    spread = pl.pallas_call(
        solve_kernel,
        out_shape=shape(16, half_lanes),
        in_specs=[SM] + [VM] * 2,
        out_specs=VM,
        scratch_shapes=[pltpu.VMEM((bricks + 32, 128), f32)],
        compiler_params=PARAMS,
        name="solve_aggregates",
    )(kappa, gathered, block_group)
    near, far, spread = lax.optimization_barrier((near, far, spread))
    sib_near = swap_a(near)
    sib_far = swap_a(far)

    in_hbm = functools.partial(pltpu.with_memory_space_constraint, memory_space=pltpu.HBM)
    to_b, s4, wd_last = pl.pallas_call(
        second_kernel,
        out_shape=(shape(1, height + 8, width), shape(4, height + 16, width), shape(height, width)),
        in_specs=[SM, HBM, HBM] + [VM] * 15,
        out_specs=[VM] * 3,
        scratch_shapes=[
            pltpu.VMEM((9, half, half), f32),
            pltpu.VMEM((9, half, half), f32),
            pltpu.VMEM((9, half + 16, half), f32),
            pltpu.VMEM((7, half + 16, half), f32),
            pltpu.VMEM((5, half + 16, half), f32),
            pltpu.VMEM((3, 2, height, half), f32),
            pltpu.VMEM((6, height + 16, width), f32),
            pltpu.VMEM((4, height, width), f32),
            pltpu.VMEM((4, height, width), f32),
            pltpu.SemaphoreType.DMA((3,)),
        ],
        compiler_params=PARAMS,
        name="correct_and_smooth",
    )(
        kappa, in_hbm(halo_lo), in_hbm(halo_hi), rhs, dens, s2_lo, s2_hi, near_f, sib_f, density1_sib, density1_own, send_a,
        sib, near, far, sib_near, sib_far, spread
    )

    halo_b = swap_b(to_b)
    to_a, solution, inside = pl.pallas_call(
        inside_kernel,
        out_shape=(shape(1, height, width), shape(1, 2, height, width), shape(2, height, width)),
        in_specs=[SM] + [VM] * 5,
        out_specs=[VM, ANY, VM],
        scratch_shapes=[
            pltpu.VMEM((2, height + 16, width), f32),
            pltpu.SemaphoreType.DMA((3,)),
        ],
        compiler_params=PARAMS,
        name="residual_inside",
    )(kappa, rhs, dens, to_b, s4, wd_last)
    halo_a = swap_a(to_a)
    residual = pl.pallas_call(
        residual_kernel,
        out_shape=shape(1, 2, height, width),
        in_specs=[SM] + [VM] * 3,
        out_specs=ANY,
        scratch_shapes=[
            pltpu.VMEM((2, height + 16, width), f32),
            pltpu.VMEM((2, height, width), f32),
            pltpu.SemaphoreType.DMA((3,)),
        ],
        compiler_params=PARAMS,
        name="residual",
    )(kappa, inside, halo_a, halo_b)
    return (solution, residual)


def solution(mesh):
    return jax.shard_map(
        local,
        mesh=mesh,
        in_specs=(P("spec", "brick", None, None), P("brick", "spec", None), P("spec"), P()),
        out_specs=(P("spec", "brick", None, None), P("spec", "brick", None, None)),
        check_vma=False,
    )
```
